32 devices in a mesh: sec: 8 (over y, x, core), row: 4 (over z).
Axes of the slice: x: 2, y: 2, z: 4, core: 2. Of those that a mesh axis runs over, the one named last changes fastest.
Arguments:
- first_pts: float32 [4, 16, 8, 32, 2, 128], P(None, 'sec', 'row'), may hold values from -1 to 1
- second_pts: float32 [4, 16, 8, 32, 2, 128], P(None, 'sec', 'row'), may hold values from -1 to 1
- counts: int32 [4, 16, 8, 32], P(None, 'sec', 'row'), may hold values from 32 to 128, as said below
Outputs:
- affines: float32 [6, 16, 8, 32], P(None, 'sec', 'row')
- residual: float32 [4, 16, 8, 32, 2, 128], P(None, 'sec', 'row')
The draws below stay inside these ranges and needn't reach their ends.
Inputs may be any that keep to these rules, and one draw needn't show every extreme that they name: `counts`: points 0 to the count minus one of a pair are live, the rest are padding.
All inputs are finite; a program needn't handle non-finite values.
Results may differ from the reference program's by a relative error of at most 0.035.
Values sent between devices are 32-bit elements; how exact they have to be, the bound alone decides.
A program may use at most 64 MiB of HBM per device.

```python
import jax
import jax.numpy as jnp
from jax import lax

COLS = 32
P_SIZE = 128
ITERS = 4
NSEC = 16
NROWS = 8


def draw_counts(key, part):
    base_counts = jax.random.randint(jax.random.fold_in(key, 11), (4, NSEC, NROWS, COLS), P_SIZE // 4, P_SIZE + 1)
    chosen = jax.random.randint(jax.random.fold_in(key, 12), (NSEC,), 0, COLS)
    chosen_cell = jnp.arange(COLS)[None, None, None, :] == chosen[None, :, None, None]
    kind_zero = jnp.arange(4)[:, None, None, None] == 0
    row_zero = jnp.arange(NROWS)[None, None, :, None] == 0
    return jnp.where(chosen_cell & kind_zero & row_zero, P_SIZE, base_counts).astype(jnp.int32)


def levels(key, extent, shards, low, high):
    factor_of = 1.0
    for dim, blocks in shards:
        draws = jax.random.uniform(jax.random.fold_in(jax.random.fold_in(key, 6), dim), (blocks,), jnp.float32, low / len(shards), high / len(shards))
        factor_of = factor_of * jnp.repeat(jnp.exp(draws), extent[dim] // blocks).reshape((-1,) + (1,) * (len(extent) - 1 - dim))
    return factor_of


def setup_inputs(seed: int = 0) -> dict:
    splits = jax.random.split(jax.random.key(seed), 4)
    first_pts = jnp.clip(jax.random.uniform(splits[0], (4, NSEC, NROWS, COLS, 2, P_SIZE), jnp.float32, -1.0, 1.0) * levels(splits[0], (4, NSEC, NROWS, COLS, 2, P_SIZE), ((1, 8), (2, 4)), -0.4, 0.0), -1.0, 1.0)
    second_pts = jnp.clip(jax.random.uniform(splits[1], (4, NSEC, NROWS, COLS, 2, P_SIZE), jnp.float32, -1.0, 1.0) * levels(splits[1], (4, NSEC, NROWS, COLS, 2, P_SIZE), ((1, 8), (2, 4)), -0.4, 0.0), -1.0, 1.0)
    counts = draw_counts(jax.random.fold_in(splits[3], 71), 0)
    return {"first_pts": first_pts, "second_pts": second_pts, "counts": counts}


reg_root = (0.7, 0.7, 0.3, 0.7, 0.7, 0.3)
kind_moves = ((2, 1), (1, 1), (0, 1), (0, 2))


def transform(affine, points):
    coord_x = points[..., 0, :]
    coord_y = points[..., 1, :]
    factor = [affine[number][..., None] for number in range(6)]
    return jnp.stack([factor[0] * coord_x + factor[1] * coord_y + factor[2],
                      factor[3] * coord_x + factor[4] * coord_y + factor[5]], axis=-2)


def moments(errors, points):
    err_x = errors[..., 0, :]
    err_y = errors[..., 1, :]
    pos_x = points[..., 0, :]
    pos_y = points[..., 1, :]
    return jnp.stack([jnp.sum(err_x * pos_x, -1), jnp.sum(err_x * pos_y, -1), jnp.sum(err_x, -1),
                      jnp.sum(err_y * pos_x, -1), jnp.sum(err_y * pos_y, -1), jnp.sum(err_y, -1)], 0)


def toward(values, axis_no, offset):
    length = values.shape[axis_no]
    kept = lax.slice_in_dim(values, offset, length, axis=axis_no)
    zeros = jnp.zeros_like(lax.slice_in_dim(values, 0, offset, axis=axis_no))
    return jnp.concatenate([kept, zeros], axis=axis_no)


def away(values, axis_no, offset):
    length = values.shape[axis_no]
    kept = lax.slice_in_dim(values, 0, length - offset, axis=axis_no)
    zeros = jnp.zeros_like(lax.slice_in_dim(values, 0, offset, axis=axis_no))
    return jnp.concatenate([zeros, kept], axis=axis_no)


def inner(list_a, reg_a, list_b, reg_b):
    summed = jnp.sum(reg_a * reg_b)
    for kind_no in range(4):
        summed = summed + jnp.sum(list_a[kind_no] * list_b[kind_no])
    return summed


def reference(first_pts, second_pts, counts):
    n_sec = counts.shape[1]
    n_row = counts.shape[2]
    n_col = counts.shape[3]
    width = first_pts.shape[-1]
    live = jnp.arange(width)[None, None, None, None, :] < counts[..., None]
    sec_ids = jnp.arange(n_sec)[:, None, None]
    row_ids = jnp.arange(n_row)[None, :, None]
    col_ids = jnp.arange(n_col)[None, None, :]
    valid = [col_ids < n_col - 1, row_ids < n_row - 1, sec_ids < n_sec - 1, sec_ids < n_sec - 2]
    masks = [jnp.where(live[kind_no] & valid[kind_no][..., None], 1.0, 0.0).astype(jnp.float32)[..., None, :]
             for kind_no in range(4)]
    root = jnp.array(reg_root, jnp.float32)[:, None, None, None]

    def forward(affine):
        result = []
        for kind_no in range(4):
            axis_no, offset = kind_moves[kind_no]
            image = toward(transform(affine, second_pts[kind_no]), axis_no, offset)
            result.append(masks[kind_no] * (transform(affine, first_pts[kind_no]) - image))
        return result

    def backward(errors, reg_part):
        summed = root * reg_part
        for kind_no in range(4):
            axis_no, offset = kind_moves[kind_no]
            moved = away(errors[kind_no], axis_no, offset)
            summed = summed + moments(errors[kind_no], first_pts[kind_no]) - moments(moved, second_pts[kind_no])
        return summed

    ones = jnp.ones((1, n_sec, n_row, n_col), jnp.float32)
    identity = jnp.array([1.0, 0.0, 0.0, 0.0, 1.0, 0.0], jnp.float32)[:, None, None, None] * ones
    resid = forward(-identity)
    resid_reg = jnp.zeros((6, n_sec, n_row, n_col), jnp.float32)
    search = backward(resid, resid_reg)
    image = forward(search)
    image_reg = root * search
    gamma = jnp.sum(search * search)
    curv = inner(image, image_reg, image, image_reg)
    direction = search
    along = image
    along_reg = image_reg
    solution = jnp.zeros((6, n_sec, n_row, n_col), jnp.float32)
    for sweep in range(ITERS):
        alpha = gamma / curv
        solution = solution + alpha * direction
        resid = [resid[kind_no] - alpha * along[kind_no] for kind_no in range(4)]
        resid_reg = resid_reg - alpha * along_reg
        if sweep < ITERS - 1:
            search = backward(resid, resid_reg)
            image = forward(search)
            image_reg = root * search
            gamma_new = jnp.sum(search * search)
            omega = inner(image, image_reg, image, image_reg)
            cross = inner(image, image_reg, along, along_reg)
            beta = gamma_new / gamma
            direction = search + beta * direction
            along = [image[kind_no] + beta * along[kind_no] for kind_no in range(4)]
            along_reg = image_reg + beta * along_reg
            curv = omega + 2.0 * beta * cross + beta * beta * curv
            gamma = gamma_new
    return solution, jnp.stack(resid, 0)
```

```python
import functools

import jax
import jax.numpy as jnp
from jax import lax
from jax.experimental import pallas as pl
from jax.experimental.pallas import tpu as pltpu
from jax.sharding import PartitionSpec as P

MESH = pl.DeviceIdType.MESH
f32 = jnp.float32

CROSS = ((5, 6, 1), (7, 8, 2), (3, 4, 0))
SECOND = ((9, 10, 3), (10, 11, 4), (3, 4, 0))
FIRST = ((12, 13, 1), (13, 14, 2), (1, 2, 0))
REG = (0.7, 0.7, 0.3)


def each(count, body):
    if count <= 8:
        for number in range(count):
            body(number)
    else:

        def step(number, carry):
            body(number)
            return carry

        lax.fori_loop(0, count, step, 0)


def kernel(
    n_sec, n_row, f_hbm, g_hbm, cnt, aff, res,
    first, second, pts, out, grams, moved, got_row, got_sec,
    held, next_sec, prev_sec, next_row, prev_row,
    part, from_row, from_sec,
    load_sem, store_sem, pts_send, pts_recv, gram_send, gram_recv,
    halo_send, halo_recv, row_send, row_recv, sec_send, sec_recv,
):
    sec = lax.axis_index("sec")
    row = lax.axis_index("row")
    has_next_sec = sec < n_sec - 1
    has_prev_sec = sec > 0
    has_next_row = row < n_row - 1
    has_prev_row = row > 0
    up_sec = {"sec": lax.rem(sec + 1, n_sec)}
    down_sec = {"sec": lax.rem(sec + n_sec - 1, n_sec)}
    up_row = {"row": lax.rem(row + 1, n_row)}
    down_row = {"row": lax.rem(row + n_row - 1, n_row)}

    def remote(src, dst, send, recv, where):
        return pltpu.make_async_remote_copy(
            src_ref=src, dst_ref=dst, send_sem=send, recv_sem=recv, device_id=where, device_id_type=MESH
        )

    barrier = pltpu.get_barrier_semaphore()
    each(
        n_sec - 1,
        lambda d: pl.semaphore_signal(
            barrier, inc=1, device_id={"sec": lax.rem(sec + d + 1, n_sec)}, device_id_type=MESH
        ),
    )
    each(
        n_row - 1,
        lambda d: pl.semaphore_signal(
            barrier, inc=1, device_id={"row": lax.rem(row + d + 1, n_row)}, device_id_type=MESH
        ),
    )
    loads = [
        pltpu.make_async_copy(f_hbm.at[kind], first.at[kind], load_sem.at[kind]) for kind in range(4)
    ]
    loads.append(pltpu.make_async_copy(g_hbm.at[0], second.at[0, pl.ds(0, 256)], load_sem.at[4]))
    loads.append(
        pltpu.make_async_copy(g_hbm.at[1, pl.ds(64, 64)], second.at[1, pl.ds(0, 64)], load_sem.at[5])
    )
    loads.append(
        pltpu.make_async_copy(g_hbm.at[1, pl.ds(192, 64)], second.at[1, pl.ds(128, 64)], load_sem.at[6])
    )
    loads.append(
        pltpu.make_async_copy(g_hbm.at[2, pl.ds(128, 128)], second.at[2, pl.ds(0, 128)], load_sem.at[7])
    )
    for copy in loads:
        copy.start()
    zero = jnp.zeros((8, 128), f32)
    pl.semaphore_wait(barrier, n_sec + n_row - 2)

    sends = [
        remote(g_hbm.at[3], second.at[3, pl.ds(0, 256)], pts_send.at[0], pts_recv.at[0], down_sec),
        remote(
            g_hbm.at[2, pl.ds(0, 128)], second.at[2, pl.ds(128, 128)], pts_send.at[1], pts_recv.at[1], down_sec
        ),
        remote(
            g_hbm.at[1, pl.ds(0, 64)], second.at[1, pl.ds(64, 64)], pts_send.at[2], pts_recv.at[2], down_row
        ),
        remote(
            g_hbm.at[1, pl.ds(128, 64)], second.at[1, pl.ds(192, 64)], pts_send.at[3], pts_recv.at[3], down_row
        ),
    ]

    @pl.when(has_prev_row)
    def _():
        sends[2].start()
        sends[3].start()

    @pl.when(has_prev_sec)
    def _():
        sends[1].start()
        sends[0].start()

    lane = lax.broadcasted_iota(jnp.int32, (1, 128), 1)
    col_of = lane % 32
    row_of = (lane // 32) % 2
    sec_of = lane // 64
    valid = (
        col_of < 31,
        row * 2 + row_of < n_row * 2 - 1,
        sec * 2 + sec_of < n_sec * 2 - 1,
        sec * 2 + sec_of < n_sec * 2 - 2,
    )
    live = []
    for kind in range(4):
        live.append(jnp.where(valid[kind], cnt[pl.ds(kind, 1), :], 0))
    point = lax.broadcasted_iota(jnp.int32, (128, 128), 0)

    def turned(ref, kind, start):
        values = ref[kind, pl.ds(start, 128, stride=2), :].T
        return jnp.where(point < live[kind], values, 0.0)

    for kind in range(4):
        loads[kind].wait()
        pts[kind, 0] = turned(first, kind, 0)
        pts[kind, 1] = turned(first, kind, 1)

    for kind in range(4):
        if kind == 0:
            loads[4].wait()
        elif kind == 1:
            loads[5].wait()
            loads[6].wait()

            @pl.when(has_next_row)
            def _():
                sends[2].wait_recv()
                sends[3].wait_recv()
        elif kind == 2:
            loads[7].wait()

            @pl.when(has_next_sec)
            def _():
                sends[1].wait_recv()
        else:

            @pl.when(has_next_sec)
            def _():
                sends[0].wait_recv()
        shift = 2 if kind == 0 else 0
        pts[kind, 2] = turned(second, kind, shift)
        pts[kind, 3] = turned(second, kind, shift + 1)
        sums = [None] * 15
        for block in range(16):
            u1, v1, u2, v2 = [pts[kind, number, pl.ds(block * 8, 8), :] for number in range(4)]
            terms = (
                u1, v1, u2, v2, u1 * u2, u1 * v2, v1 * u2, v1 * v2,
                u2 * u2, u2 * v2, v2 * v2, u1 * u1, u1 * v1, v1 * v1,
            )
            for number, term in enumerate(terms):
                sums[number + 1] = term if block == 0 else sums[number + 1] + term
        grams[kind, pl.ds(0, 1), :] = live[kind].astype(f32)
        for number in range(1, 15):
            grams[kind, pl.ds(number, 1), :] = jnp.sum(sums[number], axis=0, keepdims=True)
        grams[kind, pl.ds(15, 1), :] = jnp.zeros((1, 128), f32)
        if kind == 1:
            gram_row = remote(grams.at[1], got_row, gram_send.at[0], gram_recv.at[0], up_row)

            @pl.when(has_next_row)
            def _():
                gram_row.start()

            @pl.when(jnp.logical_not(has_prev_row))
            def _():
                got_row[...] = jnp.zeros((16, 128), f32)
        if kind == 3:
            gram_sec = remote(grams.at[pl.ds(2, 2)], got_sec, gram_send.at[1], gram_recv.at[1], up_sec)

            @pl.when(has_next_sec)
            def _():
                gram_sec.start()

            @pl.when(jnp.logical_not(has_prev_sec))
            def _():
                got_sec[...] = jnp.zeros((2, 16, 128), f32)

    sub = lax.broadcasted_iota(jnp.int32, (8, 128), 0)
    kind_of = sub // 2
    is_y = (sub % 2) == 1
    lanes = lax.broadcasted_iota(jnp.int32, (8, 128), 1)
    second_row = (lanes // 32) % 2 == 1
    second_sec = lanes // 64 == 1

    def by_kind(values):
        return jnp.where(
            kind_of == 0, values[0], jnp.where(kind_of == 1, values[1], jnp.where(kind_of == 2, values[2], values[3]))
        )

    def over_kinds(values):
        values = values + pltpu.roll(values, 4, 0)
        return values + pltpu.roll(values, 2, 0)

    def spread(ref, number):
        return by_kind([ref[kind, pl.ds(number, 1), :] for kind in range(4)])

    own = [spread(grams, number) for number in range(15)]

    @pl.when(has_prev_row)
    def _():
        gram_row.wait_recv()

    @pl.when(has_prev_sec)
    def _():
        gram_sec.wait_recv()

    wide = lax.broadcasted_iota(jnp.int32, (16, 128), 1)
    moved[0] = pltpu.roll(grams[0], 1, 1)
    moved[1] = jnp.where(
        (wide // 32) % 2 == 1, pltpu.roll(grams[1], 32, 1), pltpu.roll(got_row[...], 96, 1)
    )
    moved[2] = pltpu.roll(jnp.where(wide // 64 == 1, got_sec[0], grams[2]), 64, 1)
    moved[3] = got_sec[1]
    other = [spread(moved, number) for number in range(12)]

    diag = [[None] * 3 for _ in range(3)]
    for a in range(3):
        for c in range(a, 3):
            diag[a][c] = over_kinds(own[FIRST[a][c]] + other[SECOND[a][c]])
            diag[c][a] = diag[a][c]
    cross = [[own[CROSS[a][c]] for c in range(3)] for a in range(3)]
    back = [[other[CROSS[c][a]] for c in range(3)] for a in range(3)]

    along = (jnp.where(is_y, 0.0, -1.0), jnp.where(is_y, -1.0, 0.0))
    start = []
    for a in range(3):
        there = (cross[a][0] + back[a][0]) * along[0] + (cross[a][1] + back[a][1]) * along[1]
        start.append(diag[a][0] * along[0] + diag[a][1] * along[1] - over_kinds(there))
    for a in range(3):
        diag[a][a] = diag[a][a] + f32(REG[a]) * f32(REG[a])

    def halo_copies(number):
        send, recv = halo_send.at[number], halo_recv.at[number]
        source = held.at[number]
        return (
            remote(source, next_sec.at[number], send.at[0], recv.at[0], down_sec),
            remote(source, prev_sec.at[number], send.at[1], recv.at[1], up_sec),
            remote(source, next_row.at[number], send.at[2], recv.at[2], down_row),
            remote(source, prev_row.at[number], send.at[3], recv.at[3], up_row),
        )

    sent_to = (has_prev_sec, has_next_sec, has_prev_row, has_next_row)
    got_from = (has_next_sec, has_prev_sec, has_next_row, has_prev_row)
    landing = (next_sec, prev_sec, next_row, prev_row)

    def send_halo(number, values):
        for c in range(3):
            held[number, c] = values[c]
        for copy, wanted in zip(halo_copies(number), sent_to):
            pl.when(wanted)(copy.start)

    def wait_halo(number):
        for copy, wanted in zip(halo_copies(number), got_from):
            pl.when(wanted)(copy.wait_recv)

    def ahead(values, of_sec, of_row):
        return by_kind(
            [
                pltpu.roll(values, 127, 1),
                jnp.where(second_row, pltpu.roll(of_row, 32, 1), pltpu.roll(values, 96, 1)),
                pltpu.roll(jnp.where(second_sec, values, of_sec), 64, 1),
                of_sec,
            ]
        )

    def behind(values, of_sec, of_row):
        return by_kind(
            [
                pltpu.roll(values, 1, 1),
                jnp.where(second_row, pltpu.roll(values, 32, 1), pltpu.roll(of_row, 96, 1)),
                pltpu.roll(jnp.where(second_sec, of_sec, values), 64, 1),
                of_sec,
            ]
        )

    def normal(number, values):
        wait_halo(number)
        front = [ahead(values[c], next_sec[number, c], next_row[number, c]) for c in range(3)]
        rear = [behind(values[c], prev_sec[number, c], prev_row[number, c]) for c in range(3)]
        result = []
        for a in range(3):
            here = diag[a][0] * values[0] + diag[a][1] * values[1] + diag[a][2] * values[2]
            there = cross[a][0] * front[0] + back[a][0] * rear[0]
            for c in (1, 2):
                there = there + cross[a][c] * front[c] + back[a][c] * rear[c]
            result.append(here - over_kinds(there))
        return result

    def dot_row(left, right):
        return jnp.sum(
            left[0] * right[0] + left[1] * right[1] + left[2] * right[2], axis=0, keepdims=True
        )

    def row_copy(turn, d):
        return remote(
            part.at[turn, 0], from_row.at[turn, d], row_send.at[turn, d], row_recv.at[turn, d],
            {"row": lax.rem(row + d + 1, n_row)},
        )

    def sec_copy(turn, d):
        return remote(
            part.at[turn, 1], from_sec.at[turn, d], sec_send.at[turn, d], sec_recv.at[turn, d],
            {"sec": lax.rem(sec + d + 1, n_sec)},
        )

    def sum_open(turn, pairs):
        for number, (left, right) in enumerate(pairs):
            part[turn, 0, pl.ds(number, 1), :] = dot_row(left, right)
        if len(pairs) < 8:
            part[turn, 0, pl.ds(len(pairs), 8 - len(pairs)), :] = jnp.zeros((8 - len(pairs), 128), f32)
        each(n_row - 1, lambda d: row_copy(turn, d).start())

    def sum_middle(turn):
        each(n_row - 1, lambda d: row_copy(turn, d).wait_recv())
        total = part[turn, 0]
        for d in range(n_row - 1):
            total = total + from_row[turn, d]
        part[turn, 1] = total
        each(n_sec - 1, lambda d: sec_copy(turn, d).start())

    def sum_close(turn):
        each(n_sec - 1, lambda d: sec_copy(turn, d).wait_recv())
        total = part[turn, 1]
        for d in range(n_sec - 1):
            total = total + from_sec[turn, d]
        total = jnp.broadcast_to(jnp.sum(total, axis=1, keepdims=True), (8, 128))
        return [total[number : number + 1, :] for number in range(8)]

    def mix(factors, vectors):
        result = []
        for c in range(3):
            value = factors[0] * vectors[0][c]
            for factor, vector in zip(factors[1:], vectors[1:]):
                value = value + factor * vector[c]
            result.append(value)
        return result

    for number in range(4):
        for ref, wanted in zip(landing, got_from):

            @pl.when(jnp.logical_not(wanted))
            def _():
                for c in range(3):
                    ref[number, c] = zero

    w0 = start
    send_halo(0, w0)
    w1 = normal(0, w0)
    send_halo(1, w1)
    w2 = normal(1, w1)
    send_halo(2, w2)
    sum_open(0, ((w0, w0), (w0, w1), (w1, w1), (w1, w2), (w2, w2)))
    w3 = normal(2, w2)
    send_halo(3, w3)
    sum_middle(0)
    w4 = normal(3, w3)
    m0, m1, m2, m3, m4 = sum_close(0)[:5]

    alpha0 = m0 / m1
    gamma1 = m0 - 2.0 * alpha0 * m1 + alpha0 * alpha0 * m2
    s1w1 = m1 - alpha0 * m2
    beta0 = -s1w1 / m1
    curv1 = (m1 - 2.0 * alpha0 * m2 + alpha0 * alpha0 * m3) + 2.0 * beta0 * s1w1 + beta0 * beta0 * m1
    alpha1 = gamma1 / curv1
    lead = 1.0 + beta0
    s_one = -(alpha0 + alpha1 * lead)
    s_two = alpha0 * alpha1
    s2q1 = lead * (m1 + s_one * m2 + s_two * m3) - alpha0 * (m2 + s_one * m3 + s_two * m4)
    beta1 = -s2q1 / curv1
    p_zero = 1.0 + beta1 * lead
    p_one = s_one - beta1 * alpha0
    p_two = s_two

    one = jnp.ones((1, 128), f32)
    v = mix((one, s_one, s_two), (w0, w1, w2))
    t = mix((one, s_one, s_two), (w1, w2, w3))
    p = mix((p_zero, p_one, p_two), (w0, w1, w2))
    q = mix((p_zero, p_one, p_two), (w1, w2, w3))
    z = mix((p_zero, p_one, p_two), (w2, w3, w4))
    sum_open(1, ((v, p), (p, q), (v, q), (q, q), (v, v), (v, t), (q, t), (q, z)))
    sum_middle(1)
    vp, pq, vq, qq, vv, vt, qt, qz = sum_close(1)
    alpha2 = vp / pq
    left = vq - alpha2 * qq
    beta2 = -left / pq
    gamma3 = vv - 2.0 * alpha2 * vq + alpha2 * alpha2 * qq
    curv3 = (
        (vt - alpha2 * qt + beta2 * vq) - alpha2 * (qt - alpha2 * qz + beta2 * qq) + beta2 * (left + beta2 * pq)
    )
    alpha3 = gamma3 / curv3
    both = alpha2 + alpha3 * beta2
    factors = (
        alpha0 + alpha1 * lead + both * p_zero + alpha3,
        both * p_one - alpha1 * alpha0 + alpha3 * (s_one - alpha2 * p_zero),
        both * p_two + alpha3 * (s_two - alpha2 * p_one),
        -alpha3 * alpha2 * p_two,
    )
    x = mix(factors, (w0, w1, w2, w3))
    x_sec = mix(factors, [[next_sec[number, c] for c in range(3)] for number in range(4)])
    x_row = mix(factors, [[next_row[number, c] for c in range(3)] for number in range(4)])
    far = [ahead(x[c], x_sec[c], x_row[c]) for c in range(3)]

    stores = []
    for kind in range(4):
        u1, v1, u2, v2 = [pts[kind, number] for number in range(4)]
        inside = point < live[kind]
        for part_no in range(2):
            a0, a1, a2 = [x[c][part_no : part_no + 1, :] for c in range(3)]
            at = 2 * kind + part_no
            b0, b1, b2 = [far[c][at : at + 1, :] for c in range(3)]
            base = u2 - u1 if part_no == 0 else v2 - v1
            value = base - (a0 * u1 + a1 * v1) + (b0 * u2 + b1 * v2) + jnp.where(inside, b2 - a2, 0.0)
            out[kind, pl.ds(part_no, 128, stride=2), :] = value.T
        stores.append(pltpu.make_async_copy(out.at[kind], res.at[kind], store_sem.at[kind]))
        stores[-1].start()
    for part_no in range(2):
        for c in range(3):
            aff[pl.ds(3 * part_no + c, 1), :] = x[c][part_no : part_no + 1, :]

    @pl.when(has_prev_row)
    def _():
        sends[2].wait_send()
        sends[3].wait_send()

    @pl.when(has_prev_sec)
    def _():
        sends[0].wait_send()
        sends[1].wait_send()

    pl.when(has_next_row)(gram_row.wait_send)
    pl.when(has_next_sec)(gram_sec.wait_send)
    for number in range(4):
        for copy, wanted in zip(halo_copies(number), sent_to):
            pl.when(wanted)(copy.wait_send)
    for turn in range(2):
        each(n_row - 1, lambda d: row_copy(turn, d).wait_send())
        each(n_sec - 1, lambda d: sec_copy(turn, d).wait_send())
    for copy in stores:
        copy.wait()


def per_device(n_sec, n_row, first_pts, second_pts, counts):
    f = first_pts.reshape(4, 256, 128)
    g = second_pts.reshape(4, 256, 128)
    cnt = counts.reshape(4, 128)
    vmem = pl.BlockSpec(memory_space=pltpu.VMEM)
    hbm = pl.BlockSpec(memory_space=pl.ANY)
    sems = pltpu.SemaphoreType.DMA
    halo = pltpu.VMEM((4, 3, 8, 128), f32)
    aff, res = pl.pallas_call(
        functools.partial(kernel, n_sec, n_row),
        out_shape=(
            jax.ShapeDtypeStruct((6, 128), f32),
            jax.ShapeDtypeStruct((4, 256, 128), f32),
        ),
        in_specs=[hbm, hbm, vmem],
        out_specs=(vmem, hbm),
        scratch_shapes=[
            pltpu.VMEM((4, 256, 128), f32),
            pltpu.VMEM((4, 264, 128), f32),
            pltpu.VMEM((4, 4, 128, 128), f32),
            pltpu.VMEM((4, 256, 128), f32),
            pltpu.VMEM((4, 16, 128), f32),
            pltpu.VMEM((4, 16, 128), f32),
            pltpu.VMEM((16, 128), f32),
            pltpu.VMEM((2, 16, 128), f32),
            halo, halo, halo, halo, halo,
            pltpu.VMEM((2, 2, 8, 128), f32),
            pltpu.VMEM((2, n_row - 1, 8, 128), f32),
            pltpu.VMEM((2, n_sec - 1, 8, 128), f32),
            sems((8,)), sems((4,)), sems((4,)), sems((4,)), sems((2,)), sems((2,)),
            sems((4, 4)), sems((4, 4)),
            sems((2, n_row - 1)), sems((2, n_row - 1)), sems((2, n_sec - 1)), sems((2, n_sec - 1)),
        ],
        compiler_params=pltpu.CompilerParams(
            collective_id=0, has_side_effects=True, vmem_limit_bytes=24 * 1024 * 1024
        ),
    )(f, g, cnt)
    return aff.reshape((6,) + counts.shape[1:]), res.reshape(first_pts.shape)


def solution(mesh):
    in_specs = (
        P(None, "sec", "row", None, None, None),
        P(None, "sec", "row", None, None, None),
        P(None, "sec", "row", None),
    )
    out_specs = (P(None, "sec", "row", None), P(None, "sec", "row", None, None, None))
    return jax.shard_map(
        functools.partial(per_device, mesh.shape["sec"], mesh.shape["row"]),
        mesh=mesh, in_specs=in_specs, out_specs=out_specs, check_vma=False,
    )
```

```python
import functools

import jax
import jax.numpy as jnp
from jax import lax
from jax.experimental import pallas as pl
from jax.experimental.pallas import tpu as pltpu
from jax.sharding import PartitionSpec as P

MESH = pl.DeviceIdType.MESH
f32 = jnp.float32

CROSS = ((5, 6, 1), (7, 8, 2), (3, 4, 0))
SECOND = ((9, 10, 3), (10, 11, 4), (3, 4, 0))
FIRST = ((12, 13, 1), (13, 14, 2), (1, 2, 0))
REG = (0.7, 0.7, 0.3)


def each(count, body):
    if count <= 8:
        for number in range(count):
            body(number)
    else:

        def step(number, carry):
            body(number)
            return carry

        lax.fori_loop(0, count, step, 0)


def kernel(
    n_sec, n_row, f_hbm, g_hbm, cnt_hbm, pts_hbm, solved_hbm,
    pts, solved, cnt, first, second, grams, moved, got_row, got_sec,
    held, next_sec, prev_sec, next_row, prev_row,
    part, from_row, from_sec,
    load_sem, store_sem, pts_send, pts_recv, gram_send, gram_recv,
    halo_send, halo_recv, row_send, row_recv, sec_send, sec_recv,
):
    sec = lax.axis_index("sec")
    row = lax.axis_index("row")
    has_next_row = row < n_row - 1
    has_prev_row = row > 0
    up_sec = {"sec": lax.rem(sec + 1, n_sec)}
    down_sec = {"sec": lax.rem(sec + n_sec - 1, n_sec)}
    up_row = {"row": lax.rem(row + 1, n_row)}
    down_row = {"row": lax.rem(row + n_row - 1, n_row)}

    def remote(src, dst, send, recv, where):
        return pltpu.make_async_remote_copy(
            src_ref=src, dst_ref=dst, send_sem=send, recv_sem=recv, device_id=where, device_id_type=MESH
        )

    barrier = pltpu.get_barrier_semaphore()
    each(
        n_sec - 1,
        lambda d: pl.semaphore_signal(
            barrier, inc=1, device_id={"sec": lax.rem(sec + d + 1, n_sec)}, device_id_type=MESH
        ),
    )
    each(
        n_row - 1,
        lambda d: pl.semaphore_signal(
            barrier, inc=1, device_id={"row": lax.rem(row + d + 1, n_row)}, device_id_type=MESH
        ),
    )
    loads = [
        pltpu.make_async_copy(f_hbm.at[kind], first.at[kind], load_sem.at[kind]) for kind in range(4)
    ]
    loads.append(pltpu.make_async_copy(g_hbm.at[0], second.at[0, pl.ds(0, 256)], load_sem.at[4]))
    loads.append(
        pltpu.make_async_copy(g_hbm.at[1, pl.ds(64, 64)], second.at[1, pl.ds(0, 64)], load_sem.at[5])
    )
    loads.append(
        pltpu.make_async_copy(g_hbm.at[1, pl.ds(192, 64)], second.at[1, pl.ds(128, 64)], load_sem.at[6])
    )
    loads.append(
        pltpu.make_async_copy(g_hbm.at[2, pl.ds(128, 128)], second.at[2, pl.ds(0, 128)], load_sem.at[7])
    )
    loads.append(pltpu.make_async_copy(cnt_hbm, cnt, load_sem.at[8]))
    for copy in loads:
        copy.start()

    @pl.when(jnp.logical_not(has_next_row))
    def _():
        next_row[...] = jnp.zeros(next_row.shape, f32)

    @pl.when(jnp.logical_not(has_prev_row))
    def _():
        prev_row[...] = jnp.zeros(prev_row.shape, f32)
        got_row[...] = jnp.zeros((16, 128), f32)

    pl.semaphore_wait(barrier, n_sec + n_row - 2)

    sends = [
        remote(g_hbm.at[3], second.at[3, pl.ds(0, 256)], pts_send.at[0], pts_recv.at[0], down_sec),
        remote(
            g_hbm.at[2, pl.ds(0, 128)], second.at[2, pl.ds(128, 128)], pts_send.at[1], pts_recv.at[1], down_sec
        ),
        remote(
            g_hbm.at[1, pl.ds(0, 64)], second.at[1, pl.ds(64, 64)], pts_send.at[2], pts_recv.at[2], down_row
        ),
        remote(
            g_hbm.at[1, pl.ds(128, 64)], second.at[1, pl.ds(192, 64)], pts_send.at[3], pts_recv.at[3], down_row
        ),
    ]

    sends[1].start()
    sends[0].start()

    @pl.when(has_prev_row)
    def _():
        sends[2].start()
        sends[3].start()

    lane = lax.broadcasted_iota(jnp.int32, (1, 128), 1)
    col_of = lane % 32
    row_of = (lane // 32) % 2
    sec_of = lane // 64
    valid = (
        col_of < 31,
        row * 2 + row_of < n_row * 2 - 1,
        sec * 2 + sec_of < n_sec * 2 - 1,
        sec * 2 + sec_of < n_sec * 2 - 2,
    )
    loads[8].wait()
    live = []
    for kind in range(4):
        pieces = [cnt[kind, number // 2, pl.ds(number % 2, 1), :] for number in range(4)]
        live.append(jnp.where(valid[kind], jnp.concatenate(pieces, axis=1), 0))
    point = lax.broadcasted_iota(jnp.int32, (128, 128), 0)

    def turned(ref, kind, start):
        values = ref[kind, pl.ds(start, 128, stride=2), :].T
        return jnp.where(point < live[kind], values, 0.0)

    for kind in range(4):
        loads[kind].wait()
        pts[kind, 0] = turned(first, kind, 0)
        pts[kind, 1] = turned(first, kind, 1)

    stores = []
    for kind in range(4):
        if kind == 0:
            loads[4].wait()
        elif kind == 1:
            loads[5].wait()
            loads[6].wait()

            @pl.when(has_next_row)
            def _():
                sends[2].wait_recv()
                sends[3].wait_recv()
        elif kind == 2:
            loads[7].wait()
            sends[1].wait_recv()
        else:
            sends[0].wait_recv()
        shift = 2 if kind == 0 else 0
        pts[kind, 2] = turned(second, kind, shift)
        pts[kind, 3] = turned(second, kind, shift + 1)
        stores.append(pltpu.make_async_copy(pts.at[kind], pts_hbm.at[kind], store_sem.at[kind]))
        stores[-1].start()
        sums = [None] * 15
        for block in range(16):
            u1, v1, u2, v2 = [pts[kind, number, pl.ds(block * 8, 8), :] for number in range(4)]
            terms = (
                u1, v1, u2, v2, u1 * u2, u1 * v2, v1 * u2, v1 * v2,
                u2 * u2, u2 * v2, v2 * v2, u1 * u1, u1 * v1, v1 * v1,
            )
            for number, term in enumerate(terms):
                sums[number + 1] = term if block == 0 else sums[number + 1] + term
        grams[kind, pl.ds(0, 1), :] = live[kind].astype(f32)
        for number in range(1, 15):
            grams[kind, pl.ds(number, 1), :] = jnp.sum(sums[number], axis=0, keepdims=True)
        grams[kind, pl.ds(15, 1), :] = jnp.zeros((1, 128), f32)
        if kind == 1:
            gram_row = remote(grams.at[1], got_row, gram_send.at[0], gram_recv.at[0], up_row)

            @pl.when(has_next_row)
            def _():
                gram_row.start()
        if kind == 3:
            gram_sec = remote(grams.at[pl.ds(2, 2)], got_sec, gram_send.at[1], gram_recv.at[1], up_sec)
            gram_sec.start()

    sub = lax.broadcasted_iota(jnp.int32, (8, 128), 0)
    kind_of = sub // 2
    is_y = (sub % 2) == 1
    lanes = lax.broadcasted_iota(jnp.int32, (8, 128), 1)
    second_row = (lanes // 32) % 2 == 1
    second_sec = lanes // 64 == 1

    def by_kind(values):
        return jnp.where(
            kind_of == 0, values[0], jnp.where(kind_of == 1, values[1], jnp.where(kind_of == 2, values[2], values[3]))
        )

    def over_kinds(values):
        values = values + pltpu.roll(values, 4, 0)
        return values + pltpu.roll(values, 2, 0)

    def spread(ref, number):
        return by_kind([ref[kind, pl.ds(number, 1), :] for kind in range(4)])

    own = [spread(grams, number) for number in range(15)]

    @pl.when(has_prev_row)
    def _():
        gram_row.wait_recv()

    gram_sec.wait_recv()
    wide = lax.broadcasted_iota(jnp.int32, (16, 128), 1)
    moved[0] = pltpu.roll(grams[0], 1, 1)
    moved[1] = jnp.where(
        (wide // 32) % 2 == 1, pltpu.roll(grams[1], 32, 1), pltpu.roll(got_row[...], 96, 1)
    )
    moved[2] = pltpu.roll(jnp.where(wide // 64 == 1, got_sec[0], grams[2]), 64, 1)
    moved[3] = got_sec[1]
    other = [spread(moved, number) for number in range(12)]

    diag = [[None] * 3 for _ in range(3)]
    for a in range(3):
        for c in range(a, 3):
            diag[a][c] = over_kinds(own[FIRST[a][c]] + other[SECOND[a][c]])
            diag[c][a] = diag[a][c]
    cross = [[own[CROSS[a][c]] for c in range(3)] for a in range(3)]
    back = [[other[CROSS[c][a]] for c in range(3)] for a in range(3)]

    along = (jnp.where(is_y, 0.0, -1.0), jnp.where(is_y, -1.0, 0.0))
    start = []
    for a in range(3):
        there = (cross[a][0] + back[a][0]) * along[0] + (cross[a][1] + back[a][1]) * along[1]
        start.append(diag[a][0] * along[0] + diag[a][1] * along[1] - over_kinds(there))
    for a in range(3):
        diag[a][a] = diag[a][a] + f32(REG[a]) * f32(REG[a])

    def halo_copies(number):
        send, recv = halo_send.at[number], halo_recv.at[number]
        source = held.at[number]
        return (
            remote(source, next_sec.at[number], send.at[0], recv.at[0], down_sec),
            remote(source, prev_sec.at[number], send.at[1], recv.at[1], up_sec),
            remote(source, next_row.at[number], send.at[2], recv.at[2], down_row),
            remote(source, prev_row.at[number], send.at[3], recv.at[3], up_row),
        )

    sent_to = (None, None, has_prev_row, has_next_row)
    got_from = (None, None, has_next_row, has_prev_row)

    def where_wanted(wanted, body):
        if wanted is None:
            body()
        else:
            pl.when(wanted)(body)

    def send_halo(number, values):
        for c in range(3):
            held[number, c] = values[c]
        for copy, wanted in zip(halo_copies(number), sent_to):
            where_wanted(wanted, copy.start)

    def wait_halo(number):
        for copy, wanted in zip(halo_copies(number), got_from):
            where_wanted(wanted, copy.wait_recv)

    def ahead(values, of_sec, of_row):
        return by_kind(
            [
                pltpu.roll(values, 127, 1),
                jnp.where(second_row, pltpu.roll(of_row, 32, 1), pltpu.roll(values, 96, 1)),
                pltpu.roll(jnp.where(second_sec, values, of_sec), 64, 1),
                of_sec,
            ]
        )

    def behind(values, of_sec, of_row):
        return by_kind(
            [
                pltpu.roll(values, 1, 1),
                jnp.where(second_row, pltpu.roll(values, 32, 1), pltpu.roll(of_row, 96, 1)),
                pltpu.roll(jnp.where(second_sec, of_sec, values), 64, 1),
                of_sec,
            ]
        )

    def normal(number, values):
        wait_halo(number)
        front = [ahead(values[c], next_sec[number, c], next_row[number, c]) for c in range(3)]
        rear = [behind(values[c], prev_sec[number, c], prev_row[number, c]) for c in range(3)]
        result = []
        for a in range(3):
            here = diag[a][0] * values[0] + diag[a][1] * values[1] + diag[a][2] * values[2]
            there = cross[a][0] * front[0] + back[a][0] * rear[0]
            for c in (1, 2):
                there = there + cross[a][c] * front[c] + back[a][c] * rear[c]
            result.append(here - over_kinds(there))
        return result

    def dot_row(left, right):
        return jnp.sum(
            left[0] * right[0] + left[1] * right[1] + left[2] * right[2], axis=0, keepdims=True
        )

    def row_copy(turn, d):
        return remote(
            part.at[turn, 0], from_row.at[turn, d], row_send.at[turn, d], row_recv.at[turn, d],
            {"row": lax.rem(row + d + 1, n_row)},
        )

    def sec_copy(turn, d):
        return remote(
            part.at[turn, 1], from_sec.at[turn, d], sec_send.at[turn, d], sec_recv.at[turn, d],
            {"sec": lax.rem(sec + d + 1, n_sec)},
        )

    def sum_open(turn, pairs):
        for number, (left, right) in enumerate(pairs):
            part[turn, 0, pl.ds(number, 1), :] = dot_row(left, right)
        if len(pairs) < 8:
            part[turn, 0, pl.ds(len(pairs), 8 - len(pairs)), :] = jnp.zeros((8 - len(pairs), 128), f32)
        each(n_row - 1, lambda d: row_copy(turn, d).start())

    def sum_middle(turn):
        each(n_row - 1, lambda d: row_copy(turn, d).wait_recv())
        total = part[turn, 0]
        for d in range(n_row - 1):
            total = total + from_row[turn, d]
        part[turn, 1] = total
        each(n_sec - 1, lambda d: sec_copy(turn, d).start())

    def sum_close(turn):
        each(n_sec - 1, lambda d: sec_copy(turn, d).wait_recv())
        total = part[turn, 1]
        for d in range(n_sec - 1):
            total = total + from_sec[turn, d]
        total = jnp.broadcast_to(jnp.sum(total, axis=1, keepdims=True), (8, 128))
        return [total[number : number + 1, :] for number in range(8)]

    def mix(factors, vectors):
        result = []
        for c in range(3):
            value = factors[0] * vectors[0][c]
            for factor, vector in zip(factors[1:], vectors[1:]):
                value = value + factor * vector[c]
            result.append(value)
        return result

    w0 = start
    send_halo(0, w0)
    w1 = normal(0, w0)
    send_halo(1, w1)
    w2 = normal(1, w1)
    send_halo(2, w2)
    sum_open(0, ((w0, w0), (w0, w1), (w1, w1), (w1, w2), (w2, w2)))
    w3 = normal(2, w2)
    send_halo(3, w3)
    sum_middle(0)
    w4 = normal(3, w3)
    m0, m1, m2, m3, m4 = sum_close(0)[:5]

    alpha0 = m0 / m1
    gamma1 = m0 - 2.0 * alpha0 * m1 + alpha0 * alpha0 * m2
    s1w1 = m1 - alpha0 * m2
    beta0 = -s1w1 / m1
    curv1 = (m1 - 2.0 * alpha0 * m2 + alpha0 * alpha0 * m3) + 2.0 * beta0 * s1w1 + beta0 * beta0 * m1
    alpha1 = gamma1 / curv1
    lead = 1.0 + beta0
    s_one = -(alpha0 + alpha1 * lead)
    s_two = alpha0 * alpha1
    s2q1 = lead * (m1 + s_one * m2 + s_two * m3) - alpha0 * (m2 + s_one * m3 + s_two * m4)
    beta1 = -s2q1 / curv1
    p_zero = 1.0 + beta1 * lead
    p_one = s_one - beta1 * alpha0
    p_two = s_two

    one = jnp.ones((1, 128), f32)
    v = mix((one, s_one, s_two), (w0, w1, w2))
    t = mix((one, s_one, s_two), (w1, w2, w3))
    p = mix((p_zero, p_one, p_two), (w0, w1, w2))
    q = mix((p_zero, p_one, p_two), (w1, w2, w3))
    z = mix((p_zero, p_one, p_two), (w2, w3, w4))
    sum_open(1, ((v, p), (p, q), (v, q), (q, q), (v, v), (v, t), (q, t), (q, z)))
    sum_middle(1)
    vp, pq, vq, qq, vv, vt, qt, qz = sum_close(1)
    alpha2 = vp / pq
    left = vq - alpha2 * qq
    beta2 = -left / pq
    gamma3 = vv - 2.0 * alpha2 * vq + alpha2 * alpha2 * qq
    curv3 = (
        (vt - alpha2 * qt + beta2 * vq) - alpha2 * (qt - alpha2 * qz + beta2 * qq) + beta2 * (left + beta2 * pq)
    )
    alpha3 = gamma3 / curv3
    both = alpha2 + alpha3 * beta2
    factors = (
        alpha0 + alpha1 * lead + both * p_zero + alpha3,
        both * p_one - alpha1 * alpha0 + alpha3 * (s_one - alpha2 * p_zero),
        both * p_two + alpha3 * (s_two - alpha2 * p_one),
        -alpha3 * alpha2 * p_two,
    )
    x = mix(factors, (w0, w1, w2, w3))
    x_sec = mix(factors, [[next_sec[number, c] for c in range(3)] for number in range(4)])
    x_row = mix(factors, [[next_row[number, c] for c in range(3)] for number in range(4)])
    far = [ahead(x[c], x_sec[c], x_row[c]) for c in range(3)]

    for c in range(3):
        solved[c] = x[c]
        solved[3 + c] = far[c]
    for kind in range(4):
        solved[6, pl.ds(kind, 1), :] = live[kind].astype(f32)
    solved[6, pl.ds(4, 4), :] = jnp.zeros((4, 128), f32)
    stores.append(pltpu.make_async_copy(solved, solved_hbm, store_sem.at[4]))
    stores[-1].start()

    @pl.when(has_prev_row)
    def _():
        sends[2].wait_send()
        sends[3].wait_send()

    sends[0].wait_send()
    sends[1].wait_send()
    pl.when(has_next_row)(gram_row.wait_send)
    gram_sec.wait_send()
    for number in range(4):
        for copy, wanted in zip(halo_copies(number), sent_to):
            where_wanted(wanted, copy.wait_send)
    for turn in range(2):
        each(n_row - 1, lambda d: row_copy(turn, d).wait_send())
        each(n_sec - 1, lambda d: sec_copy(turn, d).wait_send())
    for copy in stores:
        copy.wait()


def finish(pts_hbm, solved_hbm, aff, res, pts, solved, out, small, store_sem, load_sem):
    loads = [pltpu.make_async_copy(solved_hbm, solved, load_sem.at[4])]
    for kind in range(4):
        loads.append(pltpu.make_async_copy(pts_hbm.at[kind], pts.at[kind], load_sem.at[kind]))
    for copy in loads:
        copy.start()
    loads[0].wait()
    point = lax.broadcasted_iota(jnp.int32, (128, 128), 0).astype(f32)
    for part_no in range(2):
        for c in range(3):
            for number in range(4):
                small[3 * part_no + c, number // 2, pl.ds(number % 2, 1), :] = solved[
                    c, pl.ds(part_no, 1), pl.ds(32 * number, 32)
                ]
    stores = [pltpu.make_async_copy(small, aff, store_sem.at[4])]
    stores[0].start()
    for kind in range(4):
        loads[1 + kind].wait()
        u1, v1, u2, v2 = [pts[kind, number] for number in range(4)]
        inside = point < solved[6, pl.ds(kind, 1), :]
        for part_no in range(2):
            a0, a1, a2 = [solved[c, pl.ds(part_no, 1), :] for c in range(3)]
            b0, b1, b2 = [solved[3 + c, pl.ds(2 * kind + part_no, 1), :] for c in range(3)]
            base = u2 - u1 if part_no == 0 else v2 - v1
            value = base - (a0 * u1 + a1 * v1) + (b0 * u2 + b1 * v2) + jnp.where(inside, b2 - a2, 0.0)
            out[kind, pl.ds(part_no, 128, stride=2), :] = value.T
        stores.append(pltpu.make_async_copy(out.at[kind], res.at[kind], store_sem.at[kind]))
        stores[-1].start()
    for copy in stores:
        copy.wait()


def per_device(n_sec, n_row, first_pts, second_pts, counts):
    f = first_pts.reshape(4, 256, 128)
    g = second_pts.reshape(4, 256, 128)
    hbm = pl.BlockSpec(memory_space=pl.ANY)
    sems = pltpu.SemaphoreType.DMA
    halo = pltpu.VMEM((4, 3, 8, 128), f32)
    pts, solved = pl.pallas_call(
        functools.partial(kernel, n_sec, n_row),
        out_shape=(
            jax.ShapeDtypeStruct((4, 4, 128, 128), f32),
            jax.ShapeDtypeStruct((7, 8, 128), f32),
        ),
        in_specs=[hbm, hbm, hbm],
        out_specs=(hbm, hbm),
        scratch_shapes=[
            pltpu.VMEM((4, 4, 128, 128), f32),
            pltpu.VMEM((7, 8, 128), f32),
            pltpu.VMEM(counts.shape, jnp.int32),
            pltpu.VMEM((4, 256, 128), f32),
            pltpu.VMEM((4, 264, 128), f32),
            pltpu.VMEM((4, 16, 128), f32),
            pltpu.VMEM((4, 16, 128), f32),
            pltpu.VMEM((16, 128), f32),
            pltpu.VMEM((2, 16, 128), f32),
            halo, halo, halo, halo, halo,
            pltpu.VMEM((2, 2, 8, 128), f32),
            pltpu.VMEM((2, n_row - 1, 8, 128), f32),
            pltpu.VMEM((2, n_sec - 1, 8, 128), f32),
            sems((9,)), sems((5,)), sems((4,)), sems((4,)), sems((2,)), sems((2,)),
            sems((4, 4)), sems((4, 4)),
            sems((2, n_row - 1)), sems((2, n_row - 1)), sems((2, n_sec - 1)), sems((2, n_sec - 1)),
        ],
        compiler_params=pltpu.CompilerParams(
            collective_id=0, has_side_effects=True, vmem_limit_bytes=60 * 1024 * 1024
        ),
    )(f, g, counts)
    aff, res = pl.pallas_call(
        finish,
        out_shape=(
            jax.ShapeDtypeStruct((6,) + counts.shape[1:], f32),
            jax.ShapeDtypeStruct((4, 256, 128), f32),
        ),
        in_specs=[hbm, hbm],
        out_specs=(hbm, hbm),
        scratch_shapes=[
            pltpu.VMEM((4, 4, 128, 128), f32),
            pltpu.VMEM((7, 8, 128), f32),
            pltpu.VMEM((4, 256, 128), f32),
            pltpu.VMEM((6,) + counts.shape[1:], f32),
            sems((5,)),
            sems((5,)),
        ],
        compiler_params=pltpu.CompilerParams(vmem_limit_bytes=60 * 1024 * 1024),
    )(pts, solved)
    return aff, res.reshape(first_pts.shape)


def solution(mesh):
    in_specs = (
        P(None, "sec", "row", None, None, None),
        P(None, "sec", "row", None, None, None),
        P(None, "sec", "row", None),
    )
    out_specs = (P(None, "sec", "row", None), P(None, "sec", "row", None, None, None))
    return jax.shard_map(
        functools.partial(per_device, mesh.shape["sec"], mesh.shape["row"]),
        mesh=mesh, in_specs=in_specs, out_specs=out_specs, check_vma=False,
    )
```

```python
import functools

import jax
import jax.numpy as jnp
from jax import lax
from jax.experimental import pallas as pl
from jax.experimental.pallas import tpu as pltpu
from jax.sharding import PartitionSpec as P

MESH = pl.DeviceIdType.MESH
f32 = jnp.float32

CROSS = ((5, 6, 1), (7, 8, 2), (3, 4, 0))
SECOND = ((9, 10, 3), (10, 11, 4), (3, 4, 0))
FIRST = ((12, 13, 1), (13, 14, 2), (1, 2, 0))
REG = (0.7, 0.7, 0.3)


def each(count, body):
    if count <= 8:
        for number in range(count):
            body(number)
    else:

        def step(number, carry):
            body(number)
            return carry

        lax.fori_loop(0, count, step, 0)


def kernel(
    n_sec, n_row, f_hbm, g_hbm, cnt_hbm, pts_hbm, solved_hbm,
    pts, solved, cnt, first, second, grams, ring, mats, halo, part, gathered, sec_total, row_total,
    load_sem, store_sem, pts_send, pts_recv, gram_send, gram_recv,
    halo_send, halo_recv, sum_send, sum_recv,
):
    sec = lax.axis_index("sec")
    row = lax.axis_index("row")
    total = n_sec * n_row
    flat = sec * n_row + row
    one_stage = total <= 64
    has_next_row = row < n_row - 1
    has_prev_row = row > 0
    up = lax.rem(sec + 1, n_sec)
    down = lax.rem(sec + n_sec - 1, n_sec)
    higher = lax.rem(row + 1, n_row)
    lower = lax.rem(row + n_row - 1, n_row)
    up_sec = {"sec": up, "row": row}
    down_sec = {"sec": down, "row": row}
    up_row = {"sec": sec, "row": higher}
    down_row = {"sec": sec, "row": lower}

    def remote(src, dst, send, recv, where):
        return pltpu.make_async_remote_copy(
            src_ref=src, dst_ref=dst, send_sem=send, recv_sem=recv, device_id=where, device_id_type=MESH
        )

    def any_device(d):
        there = lax.rem(flat + d + 1, total)
        return {"sec": there // n_row, "row": lax.rem(there, n_row)}

    barrier = pltpu.get_barrier_semaphore()

    def greet(where):
        pl.semaphore_signal(barrier, inc=1, device_id=where, device_id_type=MESH)

    if one_stage:
        each(total - 1, lambda d: greet(any_device(d)))
        greeted = total - 1
    else:
        each(n_sec - 1, lambda d: greet({"sec": lax.rem(sec + d + 1, n_sec), "row": row}))
        each(n_row - 1, lambda d: greet({"sec": sec, "row": lax.rem(row + d + 1, n_row)}))
        for a in (up, down):
            for b in (higher, lower):
                greet({"sec": a, "row": b})
        greeted = n_sec + n_row + 2

    loads = []

    def load(src, dst):
        loads.append(pltpu.make_async_copy(src, dst, load_sem.at[len(loads)]))

    load(cnt_hbm, cnt.at[0])
    for kind in range(4):
        load(f_hbm.at[kind], first.at[kind])
    load(g_hbm.at[0], second.at[0, pl.ds(0, 256)])
    load(g_hbm.at[1, pl.ds(64, 64)], second.at[1, pl.ds(0, 64)])
    load(g_hbm.at[1, pl.ds(192, 64)], second.at[1, pl.ds(128, 64)])
    load(g_hbm.at[2, pl.ds(128, 128)], second.at[2, pl.ds(0, 128)])
    load(g_hbm.at[3], second.at[4, pl.ds(0, 256)])
    load(g_hbm.at[2, pl.ds(0, 128)], second.at[5, pl.ds(0, 128)])
    load(g_hbm.at[1, pl.ds(0, 64)], second.at[5, pl.ds(128, 64)])
    load(g_hbm.at[1, pl.ds(128, 64)], second.at[5, pl.ds(192, 64)])
    for copy in loads:
        copy.start()

    @pl.when(jnp.logical_not(has_next_row))
    def _():
        ring[2] = jnp.zeros(ring.shape[1:], f32)
        for turn in range(2):
            for place in (3, 7, 9):
                halo[turn, place] = jnp.zeros((3, 8, 128), f32)

    @pl.when(jnp.logical_not(has_prev_row))
    def _():
        ring[3] = jnp.zeros(ring.shape[1:], f32)
        for turn in range(2):
            for place in (4, 8, 10):
                halo[turn, place] = jnp.zeros((3, 8, 128), f32)

    pl.semaphore_wait(barrier, greeted)

    sends = []

    def plan(src, dst, where):
        sends.append(remote(src, dst, pts_send.at[len(sends)], pts_recv.at[len(sends)], where))

    plan(cnt_hbm, cnt.at[1], up_sec)
    plan(g_hbm.at[2, pl.ds(0, 128)], second.at[2, pl.ds(128, 128)], down_sec)
    plan(f_hbm.at[2, pl.ds(128, 128)], first.at[5, pl.ds(0, 128)], up_sec)
    plan(g_hbm.at[3], second.at[3, pl.ds(0, 256)], down_sec)
    plan(f_hbm.at[3], first.at[4], up_sec)
    plan(g_hbm.at[1, pl.ds(0, 64)], second.at[1, pl.ds(64, 64)], down_row)
    plan(g_hbm.at[1, pl.ds(128, 64)], second.at[1, pl.ds(192, 64)], down_row)
    plan(cnt_hbm, cnt.at[2], up_row)
    plan(f_hbm.at[1, pl.ds(64, 64)], first.at[5, pl.ds(128, 64)], up_row)
    plan(f_hbm.at[1, pl.ds(192, 64)], first.at[5, pl.ds(192, 64)], up_row)
    for number in range(5):
        sends[number].start()

    @pl.when(has_prev_row)
    def _():
        sends[5].start()
        sends[6].start()

    @pl.when(has_next_row)
    def _():
        sends[7].start()
        sends[8].start()
        sends[9].start()

    lane = lax.broadcasted_iota(jnp.int32, (1, 128), 1)
    col_of = lane % 32
    row_of = (lane // 32) % 2
    sec_of = lane // 64
    valid = (
        col_of < 31,
        row * 2 + row_of < n_row * 2 - 1,
        sec * 2 + sec_of < n_sec * 2 - 1,
        sec * 2 + sec_of < n_sec * 2 - 2,
        sec + 0 * lane > 0,
        jnp.where(lane < 64, sec, row) > 0,
    )

    def count_row(block, places):
        pieces = [cnt[who, kind, a, pl.ds(b, 1), :] for who, kind, a, b in places]
        return jnp.where(valid[block], jnp.concatenate(pieces, axis=1), 0)

    live = {}
    loads[0].wait()
    for kind in range(4):
        live[kind] = count_row(kind, [(0, kind, number // 2, number % 2) for number in range(4)])
    point = lax.broadcasted_iota(jnp.int32, (128, 128), 0)

    def turned(ref, block, start):
        values = ref[block, pl.ds(start, 128, stride=2), :].T
        return jnp.where(point < live[block], values, 0.0)

    for kind in range(4):
        loads[1 + kind].wait()
        pts[kind, 0] = turned(first, kind, 0)
        pts[kind, 1] = turned(first, kind, 1)

    stores = []
    for block in (0, 1, 2, 5, 3, 4):
        if block == 0:
            loads[5].wait()
        elif block == 1:
            loads[6].wait()
            loads[7].wait()

            @pl.when(has_next_row)
            def _():
                sends[5].wait_recv()
                sends[6].wait_recv()
        elif block == 2:
            loads[8].wait()
            sends[1].wait_recv()
        elif block == 3:
            sends[3].wait_recv()
        elif block == 4:
            loads[9].wait()
            sends[4].wait_recv()
        else:
            loads[10].wait()
            loads[11].wait()
            loads[12].wait()
            sends[0].wait_recv()
            sends[2].wait_recv()

            @pl.when(has_prev_row)
            def _():
                sends[7].wait_recv()
                sends[8].wait_recv()
                sends[9].wait_recv()

            live[4] = count_row(4, [(1, 3, number // 2, number % 2) for number in range(4)])
            live[5] = count_row(5, [(1, 2, 1, 0), (1, 2, 1, 1), (2, 1, 0, 1), (2, 1, 1, 1)])
        if block >= 4:
            pts[block, 0] = turned(first, block, 0)
            pts[block, 1] = turned(first, block, 1)
        shift = 2 if block == 0 else 0
        pts[block, 2] = turned(second, block, shift)
        pts[block, 3] = turned(second, block, shift + 1)
        if block < 4:
            stores.append(pltpu.make_async_copy(pts.at[block], pts_hbm.at[block], store_sem.at[block]))
            stores[-1].start()
        wanted = 15 if block < 4 else 12
        sums = [None] * wanted
        for step in range(16):
            u1, v1, u2, v2 = [pts[block, number, pl.ds(step * 8, 8), :] for number in range(4)]
            terms = [
                u1, v1, u2, v2, u1 * u2, u1 * v2, v1 * u2, v1 * v2, u2 * u2, u2 * v2, v2 * v2,
            ]
            if block < 4:
                terms += [u1 * u1, u1 * v1, v1 * v1]
            for number, term in enumerate(terms):
                sums[number + 1] = term if step == 0 else sums[number + 1] + term
        place = grams.at[0, block] if block < 4 else grams.at[1, 3 if block == 4 else 2]
        place[pl.ds(0, 1), :] = live[block].astype(f32)
        for number in range(1, wanted):
            place[pl.ds(number, 1), :] = jnp.sum(sums[number], axis=0, keepdims=True)
        place[pl.ds(wanted, 16 - wanted), :] = jnp.zeros((16 - wanted, 128), f32)

    sub = lax.broadcasted_iota(jnp.int32, (8, 128), 0)
    kind_of = sub // 2
    is_y = (sub % 2) == 1
    lanes = lax.broadcasted_iota(jnp.int32, (8, 128), 1)
    second_row = (lanes // 32) % 2 == 1
    second_sec = lanes // 64 == 1

    def by_kind(values):
        return jnp.where(
            kind_of == 0, values[0], jnp.where(kind_of == 1, values[1], jnp.where(kind_of == 2, values[2], values[3]))
        )

    def over_kinds(values):
        values = values + pltpu.roll(values, 4, 0)
        return values + pltpu.roll(values, 2, 0)

    wide = lax.broadcasted_iota(jnp.int32, (16, 128), 1)
    crossing = grams[1, 2]
    grams[1, 0] = pltpu.roll(grams[0, 0], 1, 1)
    grams[1, 1] = jnp.where(
        (wide // 32) % 2 == 1,
        pltpu.roll(grams[0, 1], 32, 1),
        jnp.where(wide // 64 == 0, pltpu.roll(crossing, 64, 1), pltpu.roll(crossing, 96, 1)),
    )
    grams[1, 2] = jnp.where(wide // 64 == 0, crossing, pltpu.roll(grams[0, 2], 64, 1))

    ways = (down_sec, up_sec, down_row, up_row)
    sent_to = (None, None, has_prev_row, has_next_row)
    got_from = (None, None, has_next_row, has_prev_row)

    def where_wanted(wanted, body):
        if wanted is None:
            body()
        else:
            pl.when(wanted)(body)

    gram_copies = [
        remote(grams, ring.at[number], gram_send.at[number], gram_recv.at[number], ways[number])
        for number in range(4)
    ]
    for copy, wanted in zip(gram_copies, sent_to):
        where_wanted(wanted, copy.start)

    def spread(load_row, side, number):
        return by_kind([load_row(side, kind, number) for kind in range(4)])

    def matrices(load_row, regular):
        own = [spread(load_row, 0, number) for number in range(15)]
        other = [spread(load_row, 1, number) for number in range(12)]
        diag = [[None] * 3 for _ in range(3)]
        for a in range(3):
            for c in range(a, 3):
                diag[a][c] = over_kinds(own[FIRST[a][c]] + other[SECOND[a][c]])
                if regular and a == c:
                    diag[a][a] = diag[a][a] + f32(REG[a]) * f32(REG[a])
                diag[c][a] = diag[a][c]
        cross = [[own[CROSS[a][c]] for c in range(3)] for a in range(3)]
        back = [[other[CROSS[c][a]] for c in range(3)] for a in range(3)]
        return diag, cross, back

    def keep(place, blocks):
        for which in range(3):
            for a in range(3):
                for c in range(3):
                    mats[place, which * 9 + a * 3 + c] = blocks[which][a][c]

    diag, cross, back = matrices(lambda side, kind, number: grams[side, kind, pl.ds(number, 1), :], False)

    along = (jnp.where(is_y, 0.0, -1.0), jnp.where(is_y, -1.0, 0.0))
    start = []
    for a in range(3):
        there = (cross[a][0] + back[a][0]) * along[0] + (cross[a][1] + back[a][1]) * along[1]
        start.append(diag[a][0] * along[0] + diag[a][1] * along[1] - over_kinds(there))
    for a in range(3):
        diag[a][a] = diag[a][a] + f32(REG[a]) * f32(REG[a])
    keep(0, (diag, cross, back))

    up_two = lax.rem(sec + 2, n_sec)
    down_two = lax.rem(sec + n_sec - 2, n_sec)
    receivers = (
        (1, down_sec, None, None),
        (2, up_sec, None, None),
        (5, {"sec": down_two, "row": row}, None, None),
        (6, {"sec": up_two, "row": row}, None, None),
        (7, {"sec": down, "row": lower}, has_prev_row, has_next_row),
        (9, {"sec": up, "row": lower}, has_prev_row, has_next_row),
        (3, down_row, has_prev_row, has_next_row),
        (8, {"sec": down, "row": higher}, has_next_row, has_prev_row),
        (10, {"sec": up, "row": higher}, has_next_row, has_prev_row),
        (4, up_row, has_next_row, has_prev_row),
    )
    groups = (receivers[:4], receivers[4:7], receivers[7:])

    def halo_copy(turn, place, where):
        return remote(
            halo.at[turn, 0], halo.at[turn, place], halo_send.at[turn, place], halo_recv.at[turn, place], where
        )

    def send_halo(turn, values):
        for c in range(3):
            halo[turn, 0, c] = values[c]
        for group in groups:

            def start_all():
                for place, where, _, _ in group:
                    halo_copy(turn, place, where).start()

            where_wanted(group[0][2], start_all)

    def wait_halo(turn):
        for group in groups:

            def wait_all():
                for place, where, _, _ in group:
                    halo_copy(turn, place, where).wait_recv()

            where_wanted(group[0][3], wait_all)

    def wait_halo_sent(turn):
        for group in groups:

            def wait_all():
                for place, where, _, _ in group:
                    halo_copy(turn, place, where).wait_send()

            where_wanted(group[0][2], wait_all)

    def ahead(values, of_sec, of_row):
        return by_kind(
            [
                pltpu.roll(values, 127, 1),
                jnp.where(second_row, pltpu.roll(of_row, 32, 1), pltpu.roll(values, 96, 1)),
                pltpu.roll(jnp.where(second_sec, values, of_sec), 64, 1),
                of_sec,
            ]
        )

    def behind(values, of_sec, of_row):
        return by_kind(
            [
                pltpu.roll(values, 1, 1),
                jnp.where(second_row, pltpu.roll(values, 32, 1), pltpu.roll(of_row, 96, 1)),
                pltpu.roll(jnp.where(second_sec, of_sec, values), 64, 1),
                of_sec,
            ]
        )

    def normal(place, values, of_next_sec, of_prev_sec, of_next_row, of_prev_row):
        front = [ahead(values[c], of_next_sec[c], of_next_row[c]) for c in range(3)]
        rear = [behind(values[c], of_prev_sec[c], of_prev_row[c]) for c in range(3)]
        result = []
        for a in range(3):
            here = mats[place, 3 * a] * values[0]
            there = mats[place, 9 + 3 * a] * front[0] + mats[place, 18 + 3 * a] * rear[0]
            for c in (1, 2):
                here = here + mats[place, 3 * a + c] * values[c]
                there = there + mats[place, 9 + 3 * a + c] * front[c] + mats[place, 18 + 3 * a + c] * rear[c]
            result.append(here - over_kinds(there))
        return result

    def normal_around(turn):
        w = [[halo[turn, place, c] for c in range(3)] for place in range(11)]
        none = [jnp.zeros((8, 128), f32)] * 3
        return [
            normal(0, w[0], w[1], w[2], w[3], w[4]),
            normal(1, w[1], w[5], w[0], w[7], w[8]),
            normal(2, w[2], w[0], w[6], w[9], w[10]),
            normal(3, w[3], w[7], w[9], none, w[0]),
            normal(4, w[4], w[8], w[10], w[0], none),
        ]

    def dot_row(left, right):
        return jnp.sum(
            left[0] * right[0] + left[1] * right[1] + left[2] * right[2], axis=0, keepdims=True
        )

    def sum_copy(turn, d):
        return remote(
            part.at[turn, pl.ds(0, 1)], gathered.at[turn, pl.ds(d, 1)],
            sum_send.at[turn, d], sum_recv.at[turn, d], any_device(d),
        )

    def row_copy(turn, d):
        return remote(
            part.at[turn, pl.ds(0, 1)], row_total.at[turn, pl.ds(d, 1)],
            sum_send.at[turn, d], sum_recv.at[turn, d], {"sec": sec, "row": lax.rem(row + d + 1, n_row)},
        )

    def sec_copy(turn, d):
        return remote(
            part.at[turn, pl.ds(8, 1)], sec_total.at[turn, pl.ds(d, 1)],
            sum_send.at[turn, n_row + d], sum_recv.at[turn, n_row + d],
            {"sec": lax.rem(sec + d + 1, n_sec), "row": row},
        )

    def sum_open(turn, pairs):
        packed = jnp.zeros((1, 128), f32)
        for number, (left, right) in enumerate(pairs):
            packed = jnp.where(lane == number, jnp.sum(dot_row(left, right), axis=1, keepdims=True), packed)
        part[turn, pl.ds(0, 1), :] = packed
        if one_stage:
            gathered[turn, pl.ds(total - 1, 1), :] = packed
            each(total - 1, lambda d: sum_copy(turn, d).start())
        else:
            row_total[turn, pl.ds(n_row - 1, 1), :] = packed
            each(n_row - 1, lambda d: row_copy(turn, d).start())

    def sum_close(turn):
        if one_stage:
            each(total - 1, lambda d: sum_copy(turn, d).wait_recv())
            packed = jnp.sum(gathered[turn], axis=0, keepdims=True)
        else:
            each(n_row - 1, lambda d: row_copy(turn, d).wait_recv())
            middle = jnp.sum(row_total[turn], axis=0, keepdims=True)
            part[turn, pl.ds(8, 1), :] = middle
            sec_total[turn, pl.ds(n_sec - 1, 1), :] = middle
            each(n_sec - 1, lambda d: sec_copy(turn, d).start())
            each(n_sec - 1, lambda d: sec_copy(turn, d).wait_recv())
            packed = jnp.sum(sec_total[turn], axis=0, keepdims=True)
        return [
            jnp.broadcast_to(jnp.sum(jnp.where(lane == number, packed, 0.0), axis=1, keepdims=True), (1, 128))
            for number in range(8)
        ]

    def sum_sent(turn):
        if one_stage:
            each(total - 1, lambda d: sum_copy(turn, d).wait_send())
        else:
            each(n_row - 1, lambda d: row_copy(turn, d).wait_send())
            each(n_sec - 1, lambda d: sec_copy(turn, d).wait_send())

    def mix(factors, vectors):
        result = []
        for c in range(3):
            value = factors[0] * vectors[0][c]
            for factor, vector in zip(factors[1:], vectors[1:]):
                value = value + factor * vector[c]
            result.append(value)
        return result

    send_halo(0, start)
    for number in range(4):
        where_wanted(got_from[number], gram_copies[number].wait_recv)
        keep(
            number + 1,
            matrices(lambda side, kind, which: ring[number, side, kind, pl.ds(which, 1), :], True),
        )
    wait_halo(0)
    w0 = start
    first_ring = normal_around(0)
    w1 = first_ring[0]
    w2 = normal(0, *first_ring)
    send_halo(1, w2)
    sum_open(0, ((w0, w0), (w0, w1), (w1, w1), (w1, w2), (w2, w2)))
    wait_halo(1)
    third_ring = normal_around(1)
    w3 = third_ring[0]
    w4 = normal(0, *third_ring)
    m0, m1, m2, m3, m4 = sum_close(0)[:5]

    alpha0 = m0 / m1
    gamma1 = m0 - 2.0 * alpha0 * m1 + alpha0 * alpha0 * m2
    s1w1 = m1 - alpha0 * m2
    beta0 = -s1w1 / m1
    curv1 = (m1 - 2.0 * alpha0 * m2 + alpha0 * alpha0 * m3) + 2.0 * beta0 * s1w1 + beta0 * beta0 * m1
    alpha1 = gamma1 / curv1
    lead = 1.0 + beta0
    s_one = -(alpha0 + alpha1 * lead)
    s_two = alpha0 * alpha1
    s2q1 = lead * (m1 + s_one * m2 + s_two * m3) - alpha0 * (m2 + s_one * m3 + s_two * m4)
    beta1 = -s2q1 / curv1
    p_zero = 1.0 + beta1 * lead
    p_one = s_one - beta1 * alpha0
    p_two = s_two

    one = jnp.ones((1, 128), f32)
    v = mix((one, s_one, s_two), (w0, w1, w2))
    t = mix((one, s_one, s_two), (w1, w2, w3))
    p = mix((p_zero, p_one, p_two), (w0, w1, w2))
    q = mix((p_zero, p_one, p_two), (w1, w2, w3))
    z = mix((p_zero, p_one, p_two), (w2, w3, w4))
    sum_open(1, ((v, p), (p, q), (v, q), (q, q), (v, v), (v, t), (q, t), (q, z)))
    vp, pq, vq, qq, vv, vt, qt, qz = sum_close(1)
    alpha2 = vp / pq
    left = vq - alpha2 * qq
    beta2 = -left / pq
    gamma3 = vv - 2.0 * alpha2 * vq + alpha2 * alpha2 * qq
    curv3 = (
        (vt - alpha2 * qt + beta2 * vq) - alpha2 * (qt - alpha2 * qz + beta2 * qq) + beta2 * (left + beta2 * pq)
    )
    alpha3 = gamma3 / curv3
    both = alpha2 + alpha3 * beta2
    factors = (
        alpha0 + alpha1 * lead + both * p_zero + alpha3,
        both * p_one - alpha1 * alpha0 + alpha3 * (s_one - alpha2 * p_zero),
        both * p_two + alpha3 * (s_two - alpha2 * p_one),
        -alpha3 * alpha2 * p_two,
    )
    x = mix(factors, (w0, w1, w2, w3))
    beyond = []
    for place in (1, 3):
        beyond.append(
            mix(
                factors,
                (
                    [halo[0, place, c] for c in range(3)], first_ring[place],
                    [halo[1, place, c] for c in range(3)], third_ring[place],
                ),
            )
        )
    x_sec, x_row = beyond
    far = [ahead(x[c], x_sec[c], x_row[c]) for c in range(3)]

    for c in range(3):
        solved[c] = x[c]
        solved[3 + c] = far[c]
    for kind in range(4):
        solved[6, pl.ds(kind, 1), :] = live[kind].astype(f32)
    solved[6, pl.ds(4, 4), :] = jnp.zeros((4, 128), f32)
    stores.append(pltpu.make_async_copy(solved, solved_hbm, store_sem.at[4]))
    stores[-1].start()

    for number in range(5):
        sends[number].wait_send()

    @pl.when(has_prev_row)
    def _():
        sends[5].wait_send()
        sends[6].wait_send()

    @pl.when(has_next_row)
    def _():
        sends[7].wait_send()
        sends[8].wait_send()
        sends[9].wait_send()

    for copy, wanted in zip(gram_copies, sent_to):
        where_wanted(wanted, copy.wait_send)
    for turn in range(2):
        wait_halo_sent(turn)
        sum_sent(turn)
    for copy in stores:
        copy.wait()


def finish(pts_hbm, solved_hbm, aff, res, pts, solved, out, small, store_sem, load_sem):
    loads = [pltpu.make_async_copy(solved_hbm, solved, load_sem.at[4])]
    for kind in range(4):
        loads.append(pltpu.make_async_copy(pts_hbm.at[kind], pts.at[kind], load_sem.at[kind]))
    for copy in loads:
        copy.start()
    loads[0].wait()
    point = lax.broadcasted_iota(jnp.int32, (128, 128), 0).astype(f32)
    for part_no in range(2):
        for c in range(3):
            for number in range(4):
                small[3 * part_no + c, number // 2, pl.ds(number % 2, 1), :] = solved[
                    c, pl.ds(part_no, 1), pl.ds(32 * number, 32)
                ]
    stores = [pltpu.make_async_copy(small, aff, store_sem.at[4])]
    stores[0].start()
    for kind in range(4):
        loads[1 + kind].wait()
        u1, v1, u2, v2 = [pts[kind, number] for number in range(4)]
        inside = point < solved[6, pl.ds(kind, 1), :]
        for part_no in range(2):
            a0, a1, a2 = [solved[c, pl.ds(part_no, 1), :] for c in range(3)]
            b0, b1, b2 = [solved[3 + c, pl.ds(2 * kind + part_no, 1), :] for c in range(3)]
            base = u2 - u1 if part_no == 0 else v2 - v1
            value = base - (a0 * u1 + a1 * v1) + (b0 * u2 + b1 * v2) + jnp.where(inside, b2 - a2, 0.0)
            out[kind, pl.ds(part_no, 128, stride=2), :] = value.T
        stores.append(pltpu.make_async_copy(out.at[kind], res.at[kind], store_sem.at[kind]))
        stores[-1].start()
    for copy in stores:
        copy.wait()


def per_device(n_sec, n_row, first_pts, second_pts, counts):
    f = first_pts.reshape(4, 256, 128)
    g = second_pts.reshape(4, 256, 128)
    hbm = pl.BlockSpec(memory_space=pl.ANY)
    sems = pltpu.SemaphoreType.DMA
    sums = n_sec * n_row if n_sec * n_row <= 64 else n_sec + n_row
    pts, solved = pl.pallas_call(
        functools.partial(kernel, n_sec, n_row),
        out_shape=(
            jax.ShapeDtypeStruct((4, 4, 128, 128), f32),
            jax.ShapeDtypeStruct((7, 8, 128), f32),
        ),
        in_specs=[hbm, hbm, hbm],
        out_specs=(hbm, hbm),
        scratch_shapes=[
            pltpu.VMEM((6, 4, 128, 128), f32),
            pltpu.VMEM((7, 8, 128), f32),
            pltpu.VMEM((3,) + counts.shape, jnp.int32),
            pltpu.VMEM((6, 256, 128), f32),
            pltpu.VMEM((6, 264, 128), f32),
            pltpu.VMEM((2, 4, 16, 128), f32),
            pltpu.VMEM((4, 2, 4, 16, 128), f32),
            pltpu.VMEM((5, 27, 8, 128), f32),
            pltpu.VMEM((2, 11, 3, 8, 128), f32),
            pltpu.VMEM((2, 16, 128), f32),
            pltpu.VMEM((2, sums, 128), f32),
            pltpu.VMEM((2, n_sec, 128), f32),
            pltpu.VMEM((2, n_row, 128), f32),
            sems((13,)), sems((5,)), sems((10,)), sems((10,)), sems((4,)), sems((4,)),
            sems((2, 11)), sems((2, 11)), sems((2, sums)), sems((2, sums)),
        ],
        compiler_params=pltpu.CompilerParams(
            collective_id=0, has_side_effects=True, vmem_limit_bytes=60 * 1024 * 1024
        ),
    )(f, g, counts)
    aff, res = pl.pallas_call(
        finish,
        out_shape=(
            jax.ShapeDtypeStruct((6,) + counts.shape[1:], f32),
            jax.ShapeDtypeStruct((4, 256, 128), f32),
        ),
        in_specs=[hbm, hbm],
        out_specs=(hbm, hbm),
        scratch_shapes=[
            pltpu.VMEM((4, 4, 128, 128), f32),
            pltpu.VMEM((7, 8, 128), f32),
            pltpu.VMEM((4, 256, 128), f32),
            pltpu.VMEM((6,) + counts.shape[1:], f32),
            sems((5,)),
            sems((5,)),
        ],
        compiler_params=pltpu.CompilerParams(vmem_limit_bytes=60 * 1024 * 1024),
    )(pts, solved)
    return aff, res.reshape(first_pts.shape)


def solution(mesh):
    in_specs = (
        P(None, "sec", "row", None, None, None),
        P(None, "sec", "row", None, None, None),
        P(None, "sec", "row", None),
    )
    out_specs = (P(None, "sec", "row", None), P(None, "sec", "row", None, None, None))
    return jax.shard_map(
        functools.partial(per_device, mesh.shape["sec"], mesh.shape["row"]),
        mesh=mesh, in_specs=in_specs, out_specs=out_specs, check_vma=False,
    )
```

```python
import functools

import jax
import jax.numpy as jnp
from jax import lax
from jax.experimental import pallas as pl
from jax.experimental.pallas import tpu as pltpu
from jax.sharding import PartitionSpec as P

MESH = pl.DeviceIdType.MESH
f32 = jnp.float32

CROSS = ((5, 6, 1), (7, 8, 2), (3, 4, 0))
SECOND = ((9, 10, 3), (10, 11, 4), (3, 4, 0))
FIRST = ((12, 13, 1), (13, 14, 2), (1, 2, 0))
REG = (0.7, 0.7, 0.3)


UPPER = ((0, 0), (0, 1), (0, 2), (1, 1), (1, 2), (2, 2))


def each(count, body):
    if count <= 8:
        for number in range(count):
            body(number)
    else:

        def step(number, carry):
            body(number)
            return carry

        lax.fori_loop(0, count, step, 0)


def kernel(
    n_sec, n_row, f_hbm, g_hbm, cnt_hbm, pts_hbm, solved_hbm,
    pts, solved, cnt, first, second, grams, packed, ring, mats, halo, part, gathered, sec_total, row_total,
    load_sem, store_sem, pts_send, pts_recv, gram_send, gram_recv,
    halo_send, halo_recv, sum_send, sum_recv,
):
    sec = lax.axis_index("sec")
    row = lax.axis_index("row")
    total = n_sec * n_row
    flat = sec * n_row + row
    one_stage = total <= 64
    has_next_row = row < n_row - 1
    has_prev_row = row > 0
    up = lax.rem(sec + 1, n_sec)
    down = lax.rem(sec + n_sec - 1, n_sec)
    higher = lax.rem(row + 1, n_row)
    lower = lax.rem(row + n_row - 1, n_row)
    up_sec = {"sec": up, "row": row}
    down_sec = {"sec": down, "row": row}
    up_row = {"sec": sec, "row": higher}
    down_row = {"sec": sec, "row": lower}

    def remote(src, dst, send, recv, where):
        return pltpu.make_async_remote_copy(
            src_ref=src, dst_ref=dst, send_sem=send, recv_sem=recv, device_id=where, device_id_type=MESH
        )

    def any_device(d):
        there = lax.rem(flat + d + 1, total)
        return {"sec": there // n_row, "row": lax.rem(there, n_row)}

    barrier = pltpu.get_barrier_semaphore()

    def greet(where):
        pl.semaphore_signal(barrier, inc=1, device_id=where, device_id_type=MESH)

    if one_stage:
        each(total - 1, lambda d: greet(any_device(d)))
        greeted = total - 1
    else:
        each(n_sec - 1, lambda d: greet({"sec": lax.rem(sec + d + 1, n_sec), "row": row}))
        each(n_row - 1, lambda d: greet({"sec": sec, "row": lax.rem(row + d + 1, n_row)}))
        for a in (up, down):
            for b in (higher, lower):
                greet({"sec": a, "row": b})
        greeted = n_sec + n_row + 2

    loads = []

    def load(src, dst):
        loads.append(pltpu.make_async_copy(src, dst, load_sem.at[len(loads)]))

    load(cnt_hbm, cnt.at[0])
    for kind in range(4):
        load(f_hbm.at[kind], first.at[kind])
    load(g_hbm.at[0], second.at[0, pl.ds(0, 256)])
    load(g_hbm.at[1, pl.ds(64, 64)], second.at[1, pl.ds(0, 64)])
    load(g_hbm.at[1, pl.ds(192, 64)], second.at[1, pl.ds(128, 64)])
    load(g_hbm.at[2, pl.ds(128, 128)], second.at[2, pl.ds(0, 128)])
    load(g_hbm.at[3], second.at[4, pl.ds(0, 256)])
    load(g_hbm.at[2, pl.ds(0, 128)], second.at[5, pl.ds(0, 128)])
    load(g_hbm.at[1, pl.ds(0, 64)], second.at[5, pl.ds(128, 64)])
    load(g_hbm.at[1, pl.ds(128, 64)], second.at[5, pl.ds(192, 64)])
    pl.semaphore_wait(barrier, greeted)

    sends = []

    def plan(src, dst, where):
        sends.append(remote(src, dst, pts_send.at[len(sends)], pts_recv.at[len(sends)], where))

    plan(cnt_hbm, cnt.at[1], up_sec)
    plan(g_hbm.at[2, pl.ds(0, 128)], second.at[2, pl.ds(128, 128)], down_sec)
    plan(f_hbm.at[2, pl.ds(128, 128)], first.at[5, pl.ds(0, 128)], up_sec)
    plan(g_hbm.at[3], second.at[3, pl.ds(0, 256)], down_sec)
    plan(f_hbm.at[3], first.at[4], up_sec)
    plan(g_hbm.at[1, pl.ds(0, 64)], second.at[1, pl.ds(64, 64)], down_row)
    plan(g_hbm.at[1, pl.ds(128, 64)], second.at[1, pl.ds(192, 64)], down_row)
    plan(cnt_hbm, cnt.at[2], up_row)
    plan(f_hbm.at[1, pl.ds(64, 64)], first.at[5, pl.ds(128, 64)], up_row)
    plan(f_hbm.at[1, pl.ds(192, 64)], first.at[5, pl.ds(192, 64)], up_row)
    for number in range(5):
        sends[number].start()

    @pl.when(has_prev_row)
    def _():
        sends[5].start()
        sends[6].start()

    @pl.when(has_next_row)
    def _():
        sends[7].start()
        sends[8].start()
        sends[9].start()

    for copy in loads:
        copy.start()

    @pl.when(jnp.logical_not(has_next_row))
    def _():
        ring[2] = jnp.zeros(ring.shape[1:], f32)
        for turn in range(2):
            for place in (5, 6, 7):
                halo[turn, place] = jnp.zeros((3, 8, 128), f32)

    @pl.when(jnp.logical_not(has_prev_row))
    def _():
        ring[3] = jnp.zeros(ring.shape[1:], f32)
        for turn in range(2):
            for place in (8, 9, 10):
                halo[turn, place] = jnp.zeros((3, 8, 128), f32)

    lane = lax.broadcasted_iota(jnp.int32, (1, 128), 1)
    col_of = lane % 32
    row_of = (lane // 32) % 2
    sec_of = lane // 64
    valid = (
        col_of < 31,
        row * 2 + row_of < n_row * 2 - 1,
        sec * 2 + sec_of < n_sec * 2 - 1,
        sec * 2 + sec_of < n_sec * 2 - 2,
        sec + 0 * lane > 0,
        jnp.where(lane < 64, sec, row) > 0,
    )

    def count_row(block, places):
        pieces = [cnt[who, kind, a, pl.ds(b, 1), :] for who, kind, a, b in places]
        return jnp.where(valid[block], jnp.concatenate(pieces, axis=1), 0)

    live = {}
    loads[0].wait()
    for kind in range(4):
        live[kind] = count_row(kind, [(0, kind, number // 2, number % 2) for number in range(4)])
    point = lax.broadcasted_iota(jnp.int32, (128, 128), 0)

    def turned(ref, block, start):
        values = ref[block, pl.ds(start, 128, stride=2), :].T
        return jnp.where(point < live[block], values, 0.0)

    for kind in range(4):
        loads[1 + kind].wait()
        pts[kind, 0] = turned(first, kind, 0)
        pts[kind, 1] = turned(first, kind, 1)

    stores = []
    for block in (0, 1, 2, 5, 3, 4):
        if block == 0:
            loads[5].wait()
        elif block == 1:
            loads[6].wait()
            loads[7].wait()

            @pl.when(has_next_row)
            def _():
                sends[5].wait_recv()
                sends[6].wait_recv()
        elif block == 2:
            loads[8].wait()
            sends[1].wait_recv()
        elif block == 3:
            sends[3].wait_recv()
        elif block == 4:
            loads[9].wait()
            sends[4].wait_recv()
        else:
            loads[10].wait()
            loads[11].wait()
            loads[12].wait()
            sends[0].wait_recv()
            sends[2].wait_recv()

            @pl.when(has_prev_row)
            def _():
                sends[7].wait_recv()
                sends[8].wait_recv()
                sends[9].wait_recv()

            live[4] = count_row(4, [(1, 3, number // 2, number % 2) for number in range(4)])
            live[5] = count_row(5, [(1, 2, 1, 0), (1, 2, 1, 1), (2, 1, 0, 1), (2, 1, 1, 1)])
        if block >= 4:
            pts[block, 0] = turned(first, block, 0)
            pts[block, 1] = turned(first, block, 1)
        shift = 2 if block == 0 else 0
        pts[block, 2] = turned(second, block, shift)
        pts[block, 3] = turned(second, block, shift + 1)
        if block < 4:
            stores.append(pltpu.make_async_copy(pts.at[block], pts_hbm.at[block], store_sem.at[block]))
            stores[-1].start()
        wanted = 15 if block < 4 else 12
        sums = [None] * wanted
        for step in range(16):
            u1, v1, u2, v2 = [pts[block, number, pl.ds(step * 8, 8), :] for number in range(4)]
            terms = [
                u1, v1, u2, v2, u1 * u2, u1 * v2, v1 * u2, v1 * v2, u2 * u2, u2 * v2, v2 * v2,
            ]
            if block < 4:
                terms += [u1 * u1, u1 * v1, v1 * v1]
            for number, term in enumerate(terms):
                sums[number + 1] = term if step == 0 else sums[number + 1] + term
        place = grams.at[0, block] if block < 4 else grams.at[1, 3 if block == 4 else 2]
        place[pl.ds(0, 1), :] = live[block].astype(f32)
        for number in range(1, wanted):
            place[pl.ds(number, 1), :] = jnp.sum(sums[number], axis=0, keepdims=True)
        place[pl.ds(wanted, 16 - wanted), :] = jnp.zeros((16 - wanted, 128), f32)

    sub = lax.broadcasted_iota(jnp.int32, (8, 128), 0)
    kind_of = sub // 2
    is_y = (sub % 2) == 1
    lanes = lax.broadcasted_iota(jnp.int32, (8, 128), 1)
    second_row = (lanes // 32) % 2 == 1
    second_sec = lanes // 64 == 1

    def by_kind(values):
        return jnp.where(
            kind_of == 0, values[0], jnp.where(kind_of == 1, values[1], jnp.where(kind_of == 2, values[2], values[3]))
        )

    def over_kinds(values):
        values = values + pltpu.roll(values, 4, 0)
        return values + pltpu.roll(values, 2, 0)

    wide = lax.broadcasted_iota(jnp.int32, (16, 128), 1)
    crossing = grams[1, 2]
    grams[1, 0] = pltpu.roll(grams[0, 0], 1, 1)
    grams[1, 1] = jnp.where(
        (wide // 32) % 2 == 1,
        pltpu.roll(grams[0, 1], 32, 1),
        jnp.where(wide // 64 == 0, pltpu.roll(crossing, 64, 1), pltpu.roll(crossing, 96, 1)),
    )
    grams[1, 2] = jnp.where(wide // 64 == 0, crossing, pltpu.roll(grams[0, 2], 64, 1))

    ways = (down_sec, up_sec, down_row, up_row)
    sent_to = (None, None, has_prev_row, has_next_row)
    got_from = (None, None, has_next_row, has_prev_row)

    def where_wanted(wanted, body):
        if wanted is None:
            body()
        else:
            pl.when(wanted)(body)

    def send_grams(diag):
        for kind in range(4):
            packed[kind] = grams[0, kind, pl.ds(1, 8), :]
            packed[7, pl.ds(kind, 1), :] = grams[0, kind, pl.ds(0, 1), :]
        for kind in range(1, 4):
            packed[3 + kind] = grams[1, kind, pl.ds(1, 8), :]
            packed[7, pl.ds(3 + kind, 1), :] = grams[1, kind, pl.ds(0, 1), :]
        packed[7, pl.ds(7, 1), :] = jnp.zeros((1, 128), f32)
        for number, (a, c) in enumerate(UPPER):
            packed[8, pl.ds(number, 1), :] = diag[a][c][0:1, :]
        packed[8, pl.ds(6, 2), :] = jnp.zeros((2, 128), f32)
        for copy, wanted in zip(gram_copies, sent_to):
            where_wanted(wanted, copy.start)

    gram_copies = [
        remote(packed, ring.at[number], gram_send.at[number], gram_recv.at[number], ways[number])
        for number in range(4)
    ]

    def spread(load_row, side, number):
        return by_kind([load_row(side, kind, number) for kind in range(4)])

    def sides(load_row):
        own = [spread(load_row, 0, number) for number in range(9)]
        other = [spread(load_row, 1, number) for number in range(9)]
        cross = [[own[CROSS[a][c]] for c in range(3)] for a in range(3)]
        back = [[other[CROSS[c][a]] for c in range(3)] for a in range(3)]
        return cross, back

    def symmetric(values):
        full = [[None] * 3 for _ in range(3)]
        for (a, c), value in zip(UPPER, values):
            full[a][c] = value
            full[c][a] = value
        return full

    def received(number):
        rolled = pltpu.roll(ring[number, 0], 1, 1)
        rolled_count = pltpu.roll(ring[number, 7], 1, 1)

        def load_row(side, kind, which):
            if side == 1 and kind == 0:
                return rolled_count[0:1, :] if which == 0 else rolled[which - 1 : which, :]
            slot = kind + 3 * side
            if which == 0:
                return ring[number, 7, pl.ds(slot, 1), :]
            return ring[number, slot, pl.ds(which - 1, 1), :]

        cross, back = sides(load_row)
        diag = symmetric(
            [jnp.broadcast_to(ring[number, 8, pl.ds(which, 1), :], (8, 128)) for which in range(6)]
        )
        return diag, cross, back

    def keep(place, blocks):
        for which in range(3):
            for a in range(3):
                for c in range(3):
                    mats[place, which * 9 + a * 3 + c] = blocks[which][a][c]

    def own_row(side, kind, number):
        return grams[side, kind, pl.ds(number, 1), :]

    diag = symmetric(
        [
            over_kinds(spread(own_row, 0, FIRST[a][c]) + spread(own_row, 1, SECOND[a][c]))
            for a, c in UPPER
        ]
    )

    regular = [list(line) for line in diag]
    for a in range(3):
        regular[a][a] = diag[a][a] + f32(REG[a]) * f32(REG[a])
    send_grams(regular)
    cross, back = sides(own_row)

    along = (jnp.where(is_y, 0.0, -1.0), jnp.where(is_y, -1.0, 0.0))
    start = []
    for a in range(3):
        there = (cross[a][0] + back[a][0]) * along[0] + (cross[a][1] + back[a][1]) * along[1]
        start.append(diag[a][0] * along[0] + diag[a][1] * along[1] - over_kinds(there))
    up_two = lax.rem(sec + 2, n_sec)
    down_two = lax.rem(sec + n_sec - 2, n_sec)
    groups = (
        (None, None, 1, (down_sec, up_sec, {"sec": down_two, "row": row}, {"sec": up_two, "row": row})),
        (has_prev_row, has_next_row, 5, (down_row, {"sec": down, "row": lower}, {"sec": up, "row": lower})),
        (has_next_row, has_prev_row, 8, (up_row, {"sec": down, "row": higher}, {"sec": up, "row": higher})),
    )

    def halo_group(turn, number):
        _, _, base, targets = groups[number]
        region = halo.at[turn, pl.ds(base, len(targets))]
        return remote(region, region, halo_send.at[turn, number], halo_recv.at[turn, number], targets[0])

    def send_halo(turn, values):
        for c in range(3):
            halo[turn, 0, c] = values[c]
        for number, (wanted, _, base, targets) in enumerate(groups):

            def start_all():
                for place, where in enumerate(targets):
                    remote(
                        halo.at[turn, 0], halo.at[turn, base + place],
                        halo_send.at[turn, number], halo_recv.at[turn, number], where,
                    ).start()

            where_wanted(wanted, start_all)

    def wait_halo(turn):
        for number in range(3):
            where_wanted(groups[number][1], halo_group(turn, number).wait_recv)

    def wait_halo_sent(turn):
        for number in range(3):
            where_wanted(groups[number][0], halo_group(turn, number).wait_send)

    def ahead(values, of_sec, of_row):
        return by_kind(
            [
                pltpu.roll(values, 127, 1),
                jnp.where(second_row, pltpu.roll(of_row, 32, 1), pltpu.roll(values, 96, 1)),
                pltpu.roll(jnp.where(second_sec, values, of_sec), 64, 1),
                of_sec,
            ]
        )

    def behind(values, of_sec, of_row):
        return by_kind(
            [
                pltpu.roll(values, 1, 1),
                jnp.where(second_row, pltpu.roll(values, 32, 1), pltpu.roll(of_row, 96, 1)),
                pltpu.roll(jnp.where(second_sec, of_sec, values), 64, 1),
                of_sec,
            ]
        )

    def normal(place, values, of_next_sec, of_prev_sec, of_next_row, of_prev_row):
        front = [ahead(values[c], of_next_sec[c], of_next_row[c]) for c in range(3)]
        rear = [behind(values[c], of_prev_sec[c], of_prev_row[c]) for c in range(3)]
        result = []
        for a in range(3):
            here = mats[place, 3 * a] * values[0]
            there = mats[place, 9 + 3 * a] * front[0] + mats[place, 18 + 3 * a] * rear[0]
            for c in (1, 2):
                here = here + mats[place, 3 * a + c] * values[c]
                there = there + mats[place, 9 + 3 * a + c] * front[c] + mats[place, 18 + 3 * a + c] * rear[c]
            result.append(here - over_kinds(there))
        return result

    def normal_around(turn):
        w = [[halo[turn, place, c] for c in range(3)] for place in range(11)]
        none = [jnp.zeros((8, 128), f32)] * 3
        return [
            normal(0, w[0], w[1], w[2], w[5], w[8]),
            normal(1, w[1], w[3], w[0], w[6], w[9]),
            normal(2, w[2], w[0], w[4], w[7], w[10]),
            normal(3, w[5], w[6], w[7], none, w[0]),
            normal(4, w[8], w[9], w[10], w[0], none),
        ]

    def dot_row(left, right):
        return jnp.sum(
            left[0] * right[0] + left[1] * right[1] + left[2] * right[2], axis=0, keepdims=True
        )

    def sum_copy(turn, d):
        return remote(
            part.at[turn, pl.ds(0, 1)], gathered.at[turn, pl.ds(d, 1)],
            sum_send.at[turn, 0], sum_recv.at[turn, 0], any_device(d),
        )

    def sum_all(turn):
        region = gathered.at[turn, pl.ds(0, total - 1)]
        return remote(region, region, sum_send.at[turn, 0], sum_recv.at[turn, 0], any_device(0))

    def row_copy(turn, d):
        return remote(
            part.at[turn, pl.ds(0, 1)], row_total.at[turn, pl.ds(d, 1)],
            sum_send.at[turn, d], sum_recv.at[turn, d], {"sec": sec, "row": lax.rem(row + d + 1, n_row)},
        )

    def sec_copy(turn, d):
        return remote(
            part.at[turn, pl.ds(1, 1)], sec_total.at[turn, pl.ds(d, 1)],
            sum_send.at[turn, n_row + d], sum_recv.at[turn, n_row + d],
            {"sec": lax.rem(sec + d + 1, n_sec), "row": row},
        )

    def sum_open(turn, pairs):
        line = jnp.zeros((1, 128), f32)
        for number, (left, right) in enumerate(pairs):
            line = jnp.where(lane == number, jnp.sum(dot_row(left, right), axis=1, keepdims=True), line)
        part[turn, 0] = line
        if one_stage:
            gathered[turn, total - 1] = line
            each(total - 1, lambda d: sum_copy(turn, d).start())
        else:
            row_total[turn, n_row - 1] = line
            each(n_row - 1, lambda d: row_copy(turn, d).start())

    def sum_close(turn):
        if one_stage:
            sum_all(turn).wait_recv()
            line = jnp.sum(gathered[turn], axis=0)
        else:
            each(n_row - 1, lambda d: row_copy(turn, d).wait_recv())
            middle = jnp.sum(row_total[turn], axis=0)
            part[turn, 1] = middle
            sec_total[turn, n_sec - 1] = middle
            each(n_sec - 1, lambda d: sec_copy(turn, d).start())
            each(n_sec - 1, lambda d: sec_copy(turn, d).wait_recv())
            line = jnp.sum(sec_total[turn], axis=0)
        return [
            jnp.broadcast_to(jnp.sum(jnp.where(lane == number, line, 0.0), axis=1, keepdims=True), (1, 128))
            for number in range(8)
        ]

    def sum_sent(turn):
        if one_stage:
            sum_all(turn).wait_send()
        else:
            each(n_row - 1, lambda d: row_copy(turn, d).wait_send())
            each(n_sec - 1, lambda d: sec_copy(turn, d).wait_send())

    def mix(factors, vectors):
        result = []
        for c in range(3):
            value = factors[0] * vectors[0][c]
            for factor, vector in zip(factors[1:], vectors[1:]):
                value = value + factor * vector[c]
            result.append(value)
        return result

    send_halo(0, start)
    keep(0, (regular, cross, back))
    for number in range(4):
        where_wanted(got_from[number], gram_copies[number].wait_recv)
        keep(number + 1, received(number))
    wait_halo(0)
    w0 = start
    first_ring = normal_around(0)
    w1 = first_ring[0]
    w2 = normal(0, *first_ring)
    send_halo(1, w2)
    sum_open(0, ((w0, w0), (w0, w1), (w1, w1), (w1, w2), (w2, w2)))
    wait_halo(1)
    third_ring = normal_around(1)
    w3 = third_ring[0]
    w4 = normal(0, *third_ring)
    m0, m1, m2, m3, m4 = sum_close(0)[:5]

    alpha0 = m0 / m1
    gamma1 = m0 - 2.0 * alpha0 * m1 + alpha0 * alpha0 * m2
    s1w1 = m1 - alpha0 * m2
    beta0 = -s1w1 / m1
    curv1 = (m1 - 2.0 * alpha0 * m2 + alpha0 * alpha0 * m3) + 2.0 * beta0 * s1w1 + beta0 * beta0 * m1
    alpha1 = gamma1 / curv1
    lead = 1.0 + beta0
    s_one = -(alpha0 + alpha1 * lead)
    s_two = alpha0 * alpha1
    s2q1 = lead * (m1 + s_one * m2 + s_two * m3) - alpha0 * (m2 + s_one * m3 + s_two * m4)
    beta1 = -s2q1 / curv1
    p_zero = 1.0 + beta1 * lead
    p_one = s_one - beta1 * alpha0
    p_two = s_two

    one = jnp.ones((1, 128), f32)
    v = mix((one, s_one, s_two), (w0, w1, w2))
    t = mix((one, s_one, s_two), (w1, w2, w3))
    p = mix((p_zero, p_one, p_two), (w0, w1, w2))
    q = mix((p_zero, p_one, p_two), (w1, w2, w3))
    z = mix((p_zero, p_one, p_two), (w2, w3, w4))
    sum_open(1, ((v, p), (p, q), (v, q), (q, q), (v, v), (v, t), (q, t), (q, z)))
    for number in range(5):
        sends[number].wait_send()

    @pl.when(has_prev_row)
    def _():
        sends[5].wait_send()
        sends[6].wait_send()

    @pl.when(has_next_row)
    def _():
        sends[7].wait_send()
        sends[8].wait_send()
        sends[9].wait_send()

    for copy, wanted in zip(gram_copies, sent_to):
        where_wanted(wanted, copy.wait_send)
    wait_halo_sent(0)
    wait_halo_sent(1)
    sum_sent(0)
    for copy in stores:
        copy.wait()
    vp, pq, vq, qq, vv, vt, qt, qz = sum_close(1)
    alpha2 = vp / pq
    left = vq - alpha2 * qq
    beta2 = -left / pq
    gamma3 = vv - 2.0 * alpha2 * vq + alpha2 * alpha2 * qq
    curv3 = (
        (vt - alpha2 * qt + beta2 * vq) - alpha2 * (qt - alpha2 * qz + beta2 * qq) + beta2 * (left + beta2 * pq)
    )
    alpha3 = gamma3 / curv3
    both = alpha2 + alpha3 * beta2
    factors = (
        alpha0 + alpha1 * lead + both * p_zero + alpha3,
        both * p_one - alpha1 * alpha0 + alpha3 * (s_one - alpha2 * p_zero),
        both * p_two + alpha3 * (s_two - alpha2 * p_one),
        -alpha3 * alpha2 * p_two,
    )
    x = mix(factors, (w0, w1, w2, w3))
    beyond = []
    for place, slot in ((1, 1), (3, 5)):
        beyond.append(
            mix(
                factors,
                (
                    [halo[0, slot, c] for c in range(3)], first_ring[place],
                    [halo[1, slot, c] for c in range(3)], third_ring[place],
                ),
            )
        )
    x_sec, x_row = beyond
    far = [ahead(x[c], x_sec[c], x_row[c]) for c in range(3)]

    for c in range(3):
        solved[c] = x[c]
        solved[3 + c] = far[c]
    for kind in range(4):
        solved[6, pl.ds(kind, 1), :] = live[kind].astype(f32)
    solved[6, pl.ds(4, 4), :] = jnp.zeros((4, 128), f32)
    last = pltpu.make_async_copy(solved, solved_hbm, store_sem.at[4])
    last.start()

    sum_sent(1)
    last.wait()


def finish(pts_hbm, solved_hbm, aff, res, pts, solved, out, small, store_sem, load_sem):
    loads = [pltpu.make_async_copy(solved_hbm, solved, load_sem.at[4])]
    for kind in range(4):
        loads.append(pltpu.make_async_copy(pts_hbm.at[kind], pts.at[kind], load_sem.at[kind]))
    for copy in loads:
        copy.start()
    loads[0].wait()
    point = lax.broadcasted_iota(jnp.int32, (128, 128), 0).astype(f32)
    for part_no in range(2):
        for c in range(3):
            for number in range(4):
                small[3 * part_no + c, number // 2, pl.ds(number % 2, 1), :] = solved[
                    c, pl.ds(part_no, 1), pl.ds(32 * number, 32)
                ]
    stores = [pltpu.make_async_copy(small, aff, store_sem.at[4])]
    stores[0].start()
    for kind in range(4):
        loads[1 + kind].wait()
        u1, v1, u2, v2 = [pts[kind, number] for number in range(4)]
        inside = point < solved[6, pl.ds(kind, 1), :]
        for part_no in range(2):
            a0, a1, a2 = [solved[c, pl.ds(part_no, 1), :] for c in range(3)]
            b0, b1, b2 = [solved[3 + c, pl.ds(2 * kind + part_no, 1), :] for c in range(3)]
            base = u2 - u1 if part_no == 0 else v2 - v1
            value = base - (a0 * u1 + a1 * v1) + (b0 * u2 + b1 * v2) + jnp.where(inside, b2 - a2, 0.0)
            out[kind, pl.ds(part_no, 128, stride=2), :] = value.T
        stores.append(pltpu.make_async_copy(out.at[kind], res.at[kind], store_sem.at[kind]))
        stores[-1].start()
    for copy in stores:
        copy.wait()


def per_device(n_sec, n_row, first_pts, second_pts, counts):
    f = first_pts.reshape(4, 256, 128)
    g = second_pts.reshape(4, 256, 128)
    hbm = pl.BlockSpec(memory_space=pl.ANY)
    sems = pltpu.SemaphoreType.DMA
    sums = n_sec * n_row if n_sec * n_row <= 64 else n_sec + n_row
    pts, solved = pl.pallas_call(
        functools.partial(kernel, n_sec, n_row),
        out_shape=(
            jax.ShapeDtypeStruct((4, 4, 128, 128), f32),
            jax.ShapeDtypeStruct((7, 8, 128), f32),
        ),
        in_specs=[hbm, hbm, hbm],
        out_specs=(hbm, hbm),
        scratch_shapes=[
            pltpu.VMEM((6, 4, 128, 128), f32),
            pltpu.VMEM((7, 8, 128), f32),
            pltpu.VMEM((3,) + counts.shape, jnp.int32),
            pltpu.VMEM((6, 256, 128), f32),
            pltpu.VMEM((6, 264, 128), f32),
            pltpu.VMEM((2, 4, 16, 128), f32),
            pltpu.VMEM((9, 8, 128), f32),
            pltpu.VMEM((4, 9, 8, 128), f32),
            pltpu.VMEM((5, 27, 8, 128), f32),
            pltpu.VMEM((2, 11, 3, 8, 128), f32),
            pltpu.VMEM((2, 2, 1, 128), f32),
            pltpu.VMEM((2, sums, 1, 128), f32),
            pltpu.VMEM((2, n_sec, 1, 128), f32),
            pltpu.VMEM((2, n_row, 1, 128), f32),
            sems((13,)), sems((5,)), sems((10,)), sems((10,)), sems((4,)), sems((4,)),
            sems((2, 3)), sems((2, 3)), sems((2, sums)), sems((2, sums)),
        ],
        compiler_params=pltpu.CompilerParams(
            collective_id=0, has_side_effects=True, vmem_limit_bytes=60 * 1024 * 1024
        ),
    )(f, g, counts)
    aff, res = pl.pallas_call(
        finish,
        out_shape=(
            jax.ShapeDtypeStruct((6,) + counts.shape[1:], f32),
            jax.ShapeDtypeStruct((4, 256, 128), f32),
        ),
        in_specs=[hbm, hbm],
        out_specs=(hbm, hbm),
        scratch_shapes=[
            pltpu.VMEM((4, 4, 128, 128), f32),
            pltpu.VMEM((7, 8, 128), f32),
            pltpu.VMEM((4, 256, 128), f32),
            pltpu.VMEM((6,) + counts.shape[1:], f32),
            sems((5,)),
            sems((5,)),
        ],
        compiler_params=pltpu.CompilerParams(vmem_limit_bytes=60 * 1024 * 1024),
    )(pts, solved)
    return aff, res.reshape(first_pts.shape)


def solution(mesh):
    in_specs = (
        P(None, "sec", "row", None, None, None),
        P(None, "sec", "row", None, None, None),
        P(None, "sec", "row", None),
    )
    out_specs = (P(None, "sec", "row", None), P(None, "sec", "row", None, None, None))
    return jax.shard_map(
        functools.partial(per_device, mesh.shape["sec"], mesh.shape["row"]),
        mesh=mesh, in_specs=in_specs, out_specs=out_specs, check_vma=False,
    )
```

```python
import functools

import jax
import jax.numpy as jnp
from jax import lax
from jax.experimental import pallas as pl
from jax.experimental.pallas import tpu as pltpu
from jax.sharding import PartitionSpec as P

MESH = pl.DeviceIdType.MESH
f32 = jnp.float32

CROSS = ((5, 6, 1), (7, 8, 2), (3, 4, 0))
SECOND = ((9, 10, 3), (10, 11, 4), (3, 4, 0))
FIRST = ((12, 13, 1), (13, 14, 2), (1, 2, 0))
REG = (0.7, 0.7, 0.3)


BLOCK = (0, 1, 2, 4)
UPPER = ((0, 0), (0, 1), (0, 2), (1, 1), (1, 2), (2, 2))


def each(count, body):
    if count <= 8:
        for number in range(count):
            body(number)
    else:

        def step(number, carry):
            body(number)
            return carry

        lax.fori_loop(0, count, step, 0)


def kernel(
    n_sec, n_row, f_hbm, g_hbm, cnt_hbm, pts_hbm, solved_hbm,
    pts, solved, cnt, first, second, live, blocks, grams, packed, ring, mats, halo, part, gathered, sec_total, row_total,
    load_sem, store_sem, pts_send, pts_recv, gram_send, gram_recv,
    halo_send, halo_recv, sum_send, sum_recv,
):
    sec = lax.axis_index("sec")
    row = lax.axis_index("row")
    total = n_sec * n_row
    flat = sec * n_row + row
    one_stage = total <= 64
    has_next_row = row < n_row - 1
    has_prev_row = row > 0
    up = lax.rem(sec + 1, n_sec)
    down = lax.rem(sec + n_sec - 1, n_sec)
    higher = lax.rem(row + 1, n_row)
    lower = lax.rem(row + n_row - 1, n_row)
    up_sec = {"sec": up, "row": row}
    down_sec = {"sec": down, "row": row}
    up_row = {"sec": sec, "row": higher}
    down_row = {"sec": sec, "row": lower}

    def remote(src, dst, send, recv, where):
        return pltpu.make_async_remote_copy(
            src_ref=src, dst_ref=dst, send_sem=send, recv_sem=recv, device_id=where, device_id_type=MESH
        )

    def any_device(d):
        there = lax.rem(flat + d + 1, total)
        return {"sec": there // n_row, "row": lax.rem(there, n_row)}

    barrier = pltpu.get_barrier_semaphore()

    def greet(where):
        pl.semaphore_signal(barrier, inc=1, device_id=where, device_id_type=MESH)

    if one_stage:
        each(total - 1, lambda d: greet(any_device(d)))
        greeted = total - 1
    else:
        each(n_sec - 1, lambda d: greet({"sec": lax.rem(sec + d + 1, n_sec), "row": row}))
        each(n_row - 1, lambda d: greet({"sec": sec, "row": lax.rem(row + d + 1, n_row)}))
        for a in (up, down):
            for b in (higher, lower):
                greet({"sec": a, "row": b})
        greeted = n_sec + n_row + 2

    loads = []

    def load(src, dst):
        loads.append(pltpu.make_async_copy(src, dst, load_sem.at[len(loads)]))

    load(cnt_hbm, cnt.at[0])
    for kind in range(4):
        load(f_hbm.at[kind], first.at[BLOCK[kind]])
    load(g_hbm.at[0], second.at[0, pl.ds(0, 256)])
    load(g_hbm.at[1, pl.ds(64, 64)], second.at[1, pl.ds(0, 64)])
    load(g_hbm.at[1, pl.ds(192, 64)], second.at[1, pl.ds(128, 64)])
    load(g_hbm.at[2, pl.ds(128, 128)], second.at[2, pl.ds(0, 128)])
    load(g_hbm.at[3], second.at[5, pl.ds(0, 256)])
    load(g_hbm.at[2, pl.ds(0, 128)], second.at[3, pl.ds(0, 128)])
    load(g_hbm.at[1, pl.ds(0, 64)], second.at[3, pl.ds(128, 64)])
    load(g_hbm.at[1, pl.ds(128, 64)], second.at[3, pl.ds(192, 64)])
    pl.semaphore_wait(barrier, greeted)

    sends = []

    def plan(src, dst, where):
        sends.append(remote(src, dst, pts_send.at[len(sends)], pts_recv.at[len(sends)], where))

    plan(cnt_hbm, cnt.at[1], up_sec)
    plan(g_hbm.at[2, pl.ds(0, 128)], second.at[2, pl.ds(128, 128)], down_sec)
    plan(f_hbm.at[2, pl.ds(128, 128)], first.at[3, pl.ds(0, 128)], up_sec)
    plan(g_hbm.at[3], second.at[4, pl.ds(0, 256)], down_sec)
    plan(f_hbm.at[3], first.at[5], up_sec)
    plan(g_hbm.at[1, pl.ds(0, 64)], second.at[1, pl.ds(64, 64)], down_row)
    plan(g_hbm.at[1, pl.ds(128, 64)], second.at[1, pl.ds(192, 64)], down_row)
    plan(cnt_hbm, cnt.at[2], up_row)
    plan(f_hbm.at[1, pl.ds(64, 64)], first.at[3, pl.ds(128, 64)], up_row)
    plan(f_hbm.at[1, pl.ds(192, 64)], first.at[3, pl.ds(192, 64)], up_row)
    for number in range(5):
        sends[number].start()

    @pl.when(has_prev_row)
    def _():
        sends[5].start()
        sends[6].start()

    @pl.when(has_next_row)
    def _():
        sends[7].start()
        sends[8].start()
        sends[9].start()

    for copy in loads:
        copy.start()

    @pl.when(jnp.logical_not(has_next_row))
    def _():
        ring[2] = jnp.zeros(ring.shape[1:], f32)
        for turn in range(2):
            for place in (5, 6, 7):
                halo[turn, place] = jnp.zeros((3, 8, 128), f32)

    @pl.when(jnp.logical_not(has_prev_row))
    def _():
        ring[3] = jnp.zeros(ring.shape[1:], f32)
        for turn in range(2):
            for place in (8, 9, 10):
                halo[turn, place] = jnp.zeros((3, 8, 128), f32)

    lane = lax.broadcasted_iota(jnp.int32, (1, 128), 1)
    col_of = lane % 32
    row_of = (lane // 32) % 2
    sec_of = lane // 64
    valid = (
        col_of < 31,
        row * 2 + row_of < n_row * 2 - 1,
        sec * 2 + sec_of < n_sec * 2 - 1,
        sec * 2 + sec_of < n_sec * 2 - 2,
        sec + 0 * lane > 0,
        jnp.where(lane < 64, sec, row) > 0,
    )

    def count_row(block, places):
        pieces = [cnt[who, kind, a, pl.ds(b, 1), :] for who, kind, a, b in places]
        return jnp.where(valid[block], jnp.concatenate(pieces, axis=1), 0)

    loads[0].wait()
    for kind in range(4):
        live[BLOCK[kind]] = count_row(kind, [(0, kind, number // 2, number % 2) for number in range(4)])
    point = lax.broadcasted_iota(jnp.int32, (128, 128), 0)

    def turned(ref, block, start):
        values = ref[block, pl.ds(start, 128, stride=2), :].T
        return jnp.where(point < live[block], values, 0.0)

    def turn_first(block):
        pts[block, 0] = turned(first, block, 0)
        pts[block, 1] = turned(first, block, 1)

    def turn_second(block, shift):
        pts[block, 2] = turned(second, block, shift)
        pts[block, 3] = turned(second, block, shift + 1)

    for kind in range(4):
        loads[1 + kind].wait()

    def first_step(kind, carry):
        turn_first(kind + kind // 3)
        return carry

    lax.fori_loop(0, 4, first_step, 0)
    loads[5].wait()
    turn_second(0, 2)

    def block_step(block, carry):
        @pl.when(block == 1)
        def _():
            loads[6].wait()
            loads[7].wait()

            @pl.when(has_next_row)
            def _():
                sends[5].wait_recv()
                sends[6].wait_recv()

        @pl.when(block == 2)
        def _():
            loads[8].wait()
            sends[1].wait_recv()

        @pl.when(block == 3)
        def _():
            loads[10].wait()
            loads[11].wait()
            loads[12].wait()
            sends[0].wait_recv()
            sends[2].wait_recv()

            @pl.when(has_prev_row)
            def _():
                sends[7].wait_recv()
                sends[8].wait_recv()
                sends[9].wait_recv()

            live[5] = count_row(4, [(1, 3, number // 2, number % 2) for number in range(4)])
            live[3] = count_row(5, [(1, 2, 1, 0), (1, 2, 1, 1), (2, 1, 0, 1), (2, 1, 1, 1)])

        @pl.when(block == 4)
        def _():
            sends[3].wait_recv()

        @pl.when(block == 5)
        def _():
            loads[9].wait()
            sends[4].wait_recv()

        @pl.when(block % 2 * (block // 3) == 1)
        def _():
            turn_first(block)

        @pl.when(block > 0)
        def _():
            turn_second(block, 0)

        def point_step(step, sums):
            base = pl.multiple_of(step * 8, 8)
            u1, v1, u2, v2 = [pts[block, number, pl.ds(base, 8), :] for number in range(4)]
            terms = (
                u1, v1, u2, v2, u1 * u2, u1 * v2, v1 * u2, v1 * v2, u2 * u2, u2 * v2, v2 * v2,
                u1 * u1, u1 * v1, v1 * v1,
            )
            return tuple(total_so_far + term for total_so_far, term in zip(sums, terms))

        sums = lax.fori_loop(0, 16, point_step, (jnp.zeros((8, 128), f32),) * 14, unroll=4)
        blocks[block, pl.ds(0, 1), :] = live[block].astype(f32)
        for number in range(14):
            blocks[block, pl.ds(number + 1, 1), :] = jnp.sum(sums[number], axis=0, keepdims=True)
        blocks[block, pl.ds(15, 1), :] = jnp.zeros((1, 128), f32)
        return carry

    lax.fori_loop(0, 6, block_step, 0)
    stores = []
    for kind in range(4):
        grams[0, kind] = blocks[BLOCK[kind]]
        stores.append(pltpu.make_async_copy(pts.at[BLOCK[kind]], pts_hbm.at[kind], store_sem.at[kind]))
        stores[-1].start()

    sub = lax.broadcasted_iota(jnp.int32, (8, 128), 0)
    kind_of = sub // 2
    is_y = (sub % 2) == 1
    lanes = lax.broadcasted_iota(jnp.int32, (8, 128), 1)
    second_row = (lanes // 32) % 2 == 1
    second_sec = lanes // 64 == 1

    def by_kind(values):
        return jnp.where(
            kind_of == 0, values[0], jnp.where(kind_of == 1, values[1], jnp.where(kind_of == 2, values[2], values[3]))
        )

    def over_kinds(values):
        values = values + pltpu.roll(values, 4, 0)
        return values + pltpu.roll(values, 2, 0)

    wide = lax.broadcasted_iota(jnp.int32, (16, 128), 1)
    crossing = blocks[3]
    grams[1, 3] = blocks[5]
    grams[1, 0] = pltpu.roll(grams[0, 0], 1, 1)
    grams[1, 1] = jnp.where(
        (wide // 32) % 2 == 1,
        pltpu.roll(grams[0, 1], 32, 1),
        jnp.where(wide // 64 == 0, pltpu.roll(crossing, 64, 1), pltpu.roll(crossing, 96, 1)),
    )
    grams[1, 2] = jnp.where(wide // 64 == 0, crossing, pltpu.roll(grams[0, 2], 64, 1))

    ways = (down_sec, up_sec, down_row, up_row)
    sent_to = (None, None, has_prev_row, has_next_row)
    got_from = (None, None, has_next_row, has_prev_row)

    def where_wanted(wanted, body):
        if wanted is None:
            body()
        else:
            pl.when(wanted)(body)

    def send_grams(diag):
        for kind in range(4):
            packed[kind] = grams[0, kind, pl.ds(1, 8), :]
            packed[7, pl.ds(kind, 1), :] = grams[0, kind, pl.ds(0, 1), :]
        for kind in range(1, 4):
            packed[3 + kind] = grams[1, kind, pl.ds(1, 8), :]
            packed[7, pl.ds(3 + kind, 1), :] = grams[1, kind, pl.ds(0, 1), :]
        packed[7, pl.ds(7, 1), :] = jnp.zeros((1, 128), f32)
        for number, (a, c) in enumerate(UPPER):
            packed[8, pl.ds(number, 1), :] = diag[a][c][0:1, :]
        packed[8, pl.ds(6, 2), :] = jnp.zeros((2, 128), f32)
        for copy, wanted in zip(gram_copies, sent_to):
            where_wanted(wanted, copy.start)

    gram_copies = [
        remote(packed, ring.at[number], gram_send.at[number], gram_recv.at[number], ways[number])
        for number in range(4)
    ]

    def spread(load_row, side, number):
        return by_kind([load_row(side, kind, number) for kind in range(4)])

    def sides(load_row):
        own = [spread(load_row, 0, number) for number in range(9)]
        other = [spread(load_row, 1, number) for number in range(9)]
        cross = [[own[CROSS[a][c]] for c in range(3)] for a in range(3)]
        back = [[other[CROSS[c][a]] for c in range(3)] for a in range(3)]
        return cross, back

    def symmetric(values):
        full = [[None] * 3 for _ in range(3)]
        for (a, c), value in zip(UPPER, values):
            full[a][c] = value
            full[c][a] = value
        return full

    def received(number):
        rolled = pltpu.roll(ring[number, 0], 1, 1)
        rolled_count = pltpu.roll(ring[number, 7], 1, 1)

        def load_row(side, kind, which):
            if side == 1 and kind == 0:
                return rolled_count[0:1, :] if which == 0 else rolled[which - 1 : which, :]
            slot = kind + 3 * side
            if which == 0:
                return ring[number, 7, pl.ds(slot, 1), :]
            return ring[number, slot, pl.ds(which - 1, 1), :]

        cross, back = sides(load_row)
        diag = symmetric(
            [jnp.broadcast_to(ring[number, 8, pl.ds(which, 1), :], (8, 128)) for which in range(6)]
        )
        return diag, cross, back

    def keep(place, blocks):
        for which in range(3):
            for a in range(3):
                for c in range(3):
                    mats[place, which * 9 + a * 3 + c] = blocks[which][a][c]

    def own_row(side, kind, number):
        return grams[side, kind, pl.ds(number, 1), :]

    diag = symmetric(
        [
            over_kinds(spread(own_row, 0, FIRST[a][c]) + spread(own_row, 1, SECOND[a][c]))
            for a, c in UPPER
        ]
    )

    regular = [list(line) for line in diag]
    for a in range(3):
        regular[a][a] = diag[a][a] + f32(REG[a]) * f32(REG[a])
    send_grams(regular)
    cross, back = sides(own_row)

    along = (jnp.where(is_y, 0.0, -1.0), jnp.where(is_y, -1.0, 0.0))
    start = []
    for a in range(3):
        there = (cross[a][0] + back[a][0]) * along[0] + (cross[a][1] + back[a][1]) * along[1]
        start.append(diag[a][0] * along[0] + diag[a][1] * along[1] - over_kinds(there))
    up_two = lax.rem(sec + 2, n_sec)
    down_two = lax.rem(sec + n_sec - 2, n_sec)
    groups = (
        (None, None, 1, (down_sec, up_sec, {"sec": down_two, "row": row}, {"sec": up_two, "row": row})),
        (has_prev_row, has_next_row, 5, (down_row, {"sec": down, "row": lower}, {"sec": up, "row": lower})),
        (has_next_row, has_prev_row, 8, (up_row, {"sec": down, "row": higher}, {"sec": up, "row": higher})),
    )

    def halo_group(turn, number):
        _, _, base, targets = groups[number]
        region = halo.at[turn, pl.ds(base, len(targets))]
        return remote(region, region, halo_send.at[turn, number], halo_recv.at[turn, number], targets[0])

    def send_halo(turn, values):
        for c in range(3):
            halo[turn, 0, c] = values[c]
        for number, (wanted, _, base, targets) in enumerate(groups):

            def start_all():
                for place, where in enumerate(targets):
                    remote(
                        halo.at[turn, 0], halo.at[turn, base + place],
                        halo_send.at[turn, number], halo_recv.at[turn, number], where,
                    ).start()

            where_wanted(wanted, start_all)

    def wait_halo(turn):
        for number in range(3):
            where_wanted(groups[number][1], halo_group(turn, number).wait_recv)

    def wait_halo_sent(turn):
        for number in range(3):
            where_wanted(groups[number][0], halo_group(turn, number).wait_send)

    def ahead(values, of_sec, of_row):
        return by_kind(
            [
                pltpu.roll(values, 127, 1),
                jnp.where(second_row, pltpu.roll(of_row, 32, 1), pltpu.roll(values, 96, 1)),
                pltpu.roll(jnp.where(second_sec, values, of_sec), 64, 1),
                of_sec,
            ]
        )

    def behind(values, of_sec, of_row):
        return by_kind(
            [
                pltpu.roll(values, 1, 1),
                jnp.where(second_row, pltpu.roll(values, 32, 1), pltpu.roll(of_row, 96, 1)),
                pltpu.roll(jnp.where(second_sec, of_sec, values), 64, 1),
                of_sec,
            ]
        )

    def normal(place, values, of_next_sec, of_prev_sec, of_next_row, of_prev_row):
        front = [ahead(values[c], of_next_sec[c], of_next_row[c]) for c in range(3)]
        rear = [behind(values[c], of_prev_sec[c], of_prev_row[c]) for c in range(3)]
        result = []
        for a in range(3):
            here = mats[place, 3 * a] * values[0]
            there = mats[place, 9 + 3 * a] * front[0] + mats[place, 18 + 3 * a] * rear[0]
            for c in (1, 2):
                here = here + mats[place, 3 * a + c] * values[c]
                there = there + mats[place, 9 + 3 * a + c] * front[c] + mats[place, 18 + 3 * a + c] * rear[c]
            result.append(here - over_kinds(there))
        return result

    def normal_around(turn):
        w = [[halo[turn, place, c] for c in range(3)] for place in range(11)]
        none = [jnp.zeros((8, 128), f32)] * 3
        return [
            normal(0, w[0], w[1], w[2], w[5], w[8]),
            normal(1, w[1], w[3], w[0], w[6], w[9]),
            normal(2, w[2], w[0], w[4], w[7], w[10]),
            normal(3, w[5], w[6], w[7], none, w[0]),
            normal(4, w[8], w[9], w[10], w[0], none),
        ]

    def dot_row(left, right):
        return jnp.sum(
            left[0] * right[0] + left[1] * right[1] + left[2] * right[2], axis=0, keepdims=True
        )

    def sum_copy(turn, d):
        return remote(
            part.at[turn, pl.ds(0, 1)], gathered.at[turn, pl.ds(d, 1)],
            sum_send.at[turn, 0], sum_recv.at[turn, 0], any_device(d),
        )

    def sum_all(turn):
        region = gathered.at[turn, pl.ds(0, total - 1)]
        return remote(region, region, sum_send.at[turn, 0], sum_recv.at[turn, 0], any_device(0))

    def row_copy(turn, d):
        return remote(
            part.at[turn, pl.ds(0, 1)], row_total.at[turn, pl.ds(d, 1)],
            sum_send.at[turn, d], sum_recv.at[turn, d], {"sec": sec, "row": lax.rem(row + d + 1, n_row)},
        )

    def sec_copy(turn, d):
        return remote(
            part.at[turn, pl.ds(1, 1)], sec_total.at[turn, pl.ds(d, 1)],
            sum_send.at[turn, n_row + d], sum_recv.at[turn, n_row + d],
            {"sec": lax.rem(sec + d + 1, n_sec), "row": row},
        )

    def sum_open(turn, pairs):
        line = jnp.zeros((1, 128), f32)
        for number, (left, right) in enumerate(pairs):
            line = jnp.where(lane == number, jnp.sum(dot_row(left, right), axis=1, keepdims=True), line)
        part[turn, 0] = line
        if one_stage:
            gathered[turn, total - 1] = line
            each(total - 1, lambda d: sum_copy(turn, d).start())
        else:
            row_total[turn, n_row - 1] = line
            each(n_row - 1, lambda d: row_copy(turn, d).start())

    def sum_close(turn):
        if one_stage:
            sum_all(turn).wait_recv()
            line = jnp.sum(gathered[turn], axis=0)
        else:
            each(n_row - 1, lambda d: row_copy(turn, d).wait_recv())
            middle = jnp.sum(row_total[turn], axis=0)
            part[turn, 1] = middle
            sec_total[turn, n_sec - 1] = middle
            each(n_sec - 1, lambda d: sec_copy(turn, d).start())
            each(n_sec - 1, lambda d: sec_copy(turn, d).wait_recv())
            line = jnp.sum(sec_total[turn], axis=0)
        return [
            jnp.broadcast_to(jnp.sum(jnp.where(lane == number, line, 0.0), axis=1, keepdims=True), (1, 128))
            for number in range(8)
        ]

    def sum_sent(turn):
        if one_stage:
            sum_all(turn).wait_send()
        else:
            each(n_row - 1, lambda d: row_copy(turn, d).wait_send())
            each(n_sec - 1, lambda d: sec_copy(turn, d).wait_send())

    def mix(factors, vectors):
        result = []
        for c in range(3):
            value = factors[0] * vectors[0][c]
            for factor, vector in zip(factors[1:], vectors[1:]):
                value = value + factor * vector[c]
            result.append(value)
        return result

    send_halo(0, start)
    keep(0, (regular, cross, back))
    for number in range(4):
        where_wanted(got_from[number], gram_copies[number].wait_recv)

    def unpack(number, carry):
        keep(number + 1, received(number))
        return carry

    lax.fori_loop(0, 4, unpack, 0)
    wait_halo(0)
    w0 = start
    first_ring = normal_around(0)
    w1 = first_ring[0]
    w2 = normal(0, *first_ring)
    send_halo(1, w2)
    sum_open(0, ((w0, w0), (w0, w1), (w1, w1), (w1, w2), (w2, w2)))
    wait_halo(1)
    third_ring = normal_around(1)
    w3 = third_ring[0]
    w4 = normal(0, *third_ring)
    m0, m1, m2, m3, m4 = sum_close(0)[:5]

    alpha0 = m0 / m1
    gamma1 = m0 - 2.0 * alpha0 * m1 + alpha0 * alpha0 * m2
    s1w1 = m1 - alpha0 * m2
    beta0 = -s1w1 / m1
    curv1 = (m1 - 2.0 * alpha0 * m2 + alpha0 * alpha0 * m3) + 2.0 * beta0 * s1w1 + beta0 * beta0 * m1
    alpha1 = gamma1 / curv1
    lead = 1.0 + beta0
    s_one = -(alpha0 + alpha1 * lead)
    s_two = alpha0 * alpha1
    s2q1 = lead * (m1 + s_one * m2 + s_two * m3) - alpha0 * (m2 + s_one * m3 + s_two * m4)
    beta1 = -s2q1 / curv1
    p_zero = 1.0 + beta1 * lead
    p_one = s_one - beta1 * alpha0
    p_two = s_two

    one = jnp.ones((1, 128), f32)
    v = mix((one, s_one, s_two), (w0, w1, w2))
    t = mix((one, s_one, s_two), (w1, w2, w3))
    p = mix((p_zero, p_one, p_two), (w0, w1, w2))
    q = mix((p_zero, p_one, p_two), (w1, w2, w3))
    z = mix((p_zero, p_one, p_two), (w2, w3, w4))
    sum_open(1, ((v, p), (p, q), (v, q), (q, q), (v, v), (v, t), (q, t), (q, z)))
    for number in range(5):
        sends[number].wait_send()

    @pl.when(has_prev_row)
    def _():
        sends[5].wait_send()
        sends[6].wait_send()

    @pl.when(has_next_row)
    def _():
        sends[7].wait_send()
        sends[8].wait_send()
        sends[9].wait_send()

    for copy, wanted in zip(gram_copies, sent_to):
        where_wanted(wanted, copy.wait_send)
    wait_halo_sent(0)
    wait_halo_sent(1)
    sum_sent(0)
    for copy in stores:
        copy.wait()
    vp, pq, vq, qq, vv, vt, qt, qz = sum_close(1)
    alpha2 = vp / pq
    left = vq - alpha2 * qq
    beta2 = -left / pq
    gamma3 = vv - 2.0 * alpha2 * vq + alpha2 * alpha2 * qq
    curv3 = (
        (vt - alpha2 * qt + beta2 * vq) - alpha2 * (qt - alpha2 * qz + beta2 * qq) + beta2 * (left + beta2 * pq)
    )
    alpha3 = gamma3 / curv3
    both = alpha2 + alpha3 * beta2
    factors = (
        alpha0 + alpha1 * lead + both * p_zero + alpha3,
        both * p_one - alpha1 * alpha0 + alpha3 * (s_one - alpha2 * p_zero),
        both * p_two + alpha3 * (s_two - alpha2 * p_one),
        -alpha3 * alpha2 * p_two,
    )
    x = mix(factors, (w0, w1, w2, w3))
    beyond = []
    for place, slot in ((1, 1), (3, 5)):
        beyond.append(
            mix(
                factors,
                (
                    [halo[0, slot, c] for c in range(3)], first_ring[place],
                    [halo[1, slot, c] for c in range(3)], third_ring[place],
                ),
            )
        )
    x_sec, x_row = beyond
    far = [ahead(x[c], x_sec[c], x_row[c]) for c in range(3)]

    for c in range(3):
        solved[c] = x[c]
        solved[3 + c] = far[c]
    for kind in range(4):
        solved[6, pl.ds(kind, 1), :] = live[BLOCK[kind]].astype(f32)
    solved[6, pl.ds(4, 4), :] = jnp.zeros((4, 128), f32)
    last = pltpu.make_async_copy(solved, solved_hbm, store_sem.at[4])
    last.start()

    sum_sent(1)
    last.wait()


def finish(pts_hbm, solved_hbm, aff, res, pts, solved, out, small, store_sem, load_sem):
    loads = [pltpu.make_async_copy(solved_hbm, solved, load_sem.at[4])]
    for kind in range(4):
        loads.append(pltpu.make_async_copy(pts_hbm.at[kind], pts.at[kind], load_sem.at[kind]))
    for copy in loads:
        copy.start()
    loads[0].wait()
    point = lax.broadcasted_iota(jnp.int32, (128, 128), 0).astype(f32)
    for part_no in range(2):
        for c in range(3):
            for number in range(4):
                small[3 * part_no + c, number // 2, pl.ds(number % 2, 1), :] = solved[
                    c, pl.ds(part_no, 1), pl.ds(32 * number, 32)
                ]
    stores = [pltpu.make_async_copy(small, aff, store_sem.at[4])]
    stores[0].start()
    for kind in range(4):
        loads[1 + kind].wait()
        u1, v1, u2, v2 = [pts[kind, number] for number in range(4)]
        inside = point < solved[6, pl.ds(kind, 1), :]
        for part_no in range(2):
            a0, a1, a2 = [solved[c, pl.ds(part_no, 1), :] for c in range(3)]
            b0, b1, b2 = [solved[3 + c, pl.ds(2 * kind + part_no, 1), :] for c in range(3)]
            base = u2 - u1 if part_no == 0 else v2 - v1
            value = base - (a0 * u1 + a1 * v1) + (b0 * u2 + b1 * v2) + jnp.where(inside, b2 - a2, 0.0)
            out[kind, pl.ds(part_no, 128, stride=2), :] = value.T
        stores.append(pltpu.make_async_copy(out.at[kind], res.at[kind], store_sem.at[kind]))
        stores[-1].start()
    for copy in stores:
        copy.wait()


def per_device(n_sec, n_row, first_pts, second_pts, counts):
    f = first_pts.reshape(4, 256, 128)
    g = second_pts.reshape(4, 256, 128)
    hbm = pl.BlockSpec(memory_space=pl.ANY)
    sems = pltpu.SemaphoreType.DMA
    sums = n_sec * n_row if n_sec * n_row <= 64 else n_sec + n_row
    pts, solved = pl.pallas_call(
        functools.partial(kernel, n_sec, n_row),
        out_shape=(
            jax.ShapeDtypeStruct((4, 4, 128, 128), f32),
            jax.ShapeDtypeStruct((7, 8, 128), f32),
        ),
        in_specs=[hbm, hbm, hbm],
        out_specs=(hbm, hbm),
        scratch_shapes=[
            pltpu.VMEM((6, 4, 128, 128), f32),
            pltpu.VMEM((7, 8, 128), f32),
            pltpu.VMEM((3,) + counts.shape, jnp.int32),
            pltpu.VMEM((6, 256, 128), f32),
            pltpu.VMEM((6, 264, 128), f32),
            pltpu.VMEM((6, 1, 128), jnp.int32),
            pltpu.VMEM((6, 16, 128), f32),
            pltpu.VMEM((2, 4, 16, 128), f32),
            pltpu.VMEM((9, 8, 128), f32),
            pltpu.VMEM((4, 9, 8, 128), f32),
            pltpu.VMEM((5, 27, 8, 128), f32),
            pltpu.VMEM((2, 11, 3, 8, 128), f32),
            pltpu.VMEM((2, 2, 1, 128), f32),
            pltpu.VMEM((2, sums, 1, 128), f32),
            pltpu.VMEM((2, n_sec, 1, 128), f32),
            pltpu.VMEM((2, n_row, 1, 128), f32),
            sems((13,)), sems((5,)), sems((10,)), sems((10,)), sems((4,)), sems((4,)),
            sems((2, 3)), sems((2, 3)), sems((2, sums)), sems((2, sums)),
        ],
        compiler_params=pltpu.CompilerParams(
            collective_id=0, has_side_effects=True, vmem_limit_bytes=60 * 1024 * 1024
        ),
    )(f, g, counts)
    aff, res = pl.pallas_call(
        finish,
        out_shape=(
            jax.ShapeDtypeStruct((6,) + counts.shape[1:], f32),
            jax.ShapeDtypeStruct((4, 256, 128), f32),
        ),
        in_specs=[hbm, hbm],
        out_specs=(hbm, hbm),
        scratch_shapes=[
            pltpu.VMEM((4, 4, 128, 128), f32),
            pltpu.VMEM((7, 8, 128), f32),
            pltpu.VMEM((4, 256, 128), f32),
            pltpu.VMEM((6,) + counts.shape[1:], f32),
            sems((5,)),
            sems((5,)),
        ],
        compiler_params=pltpu.CompilerParams(vmem_limit_bytes=60 * 1024 * 1024),
    )(pts, solved)
    return aff, res.reshape(first_pts.shape)


def solution(mesh):
    in_specs = (
        P(None, "sec", "row", None, None, None),
        P(None, "sec", "row", None, None, None),
        P(None, "sec", "row", None),
    )
    out_specs = (P(None, "sec", "row", None), P(None, "sec", "row", None, None, None))
    return jax.shard_map(
        functools.partial(per_device, mesh.shape["sec"], mesh.shape["row"]),
        mesh=mesh, in_specs=in_specs, out_specs=out_specs, check_vma=False,
    )
```

```python
import functools

import jax
import jax.numpy as jnp
from jax import lax
from jax.experimental import pallas as pl
from jax.experimental.pallas import tpu as pltpu
from jax.sharding import PartitionSpec as P

MESH = pl.DeviceIdType.MESH
f32 = jnp.float32

CROSS = ((5, 6, 1), (7, 8, 2), (3, 4, 0))
SECOND = ((9, 10, 3), (10, 11, 4), (3, 4, 0))
FIRST = ((12, 13, 1), (13, 14, 2), (1, 2, 0))
REG = (0.7, 0.7, 0.3)


UPPER = ((0, 0), (0, 1), (0, 2), (1, 1), (1, 2), (2, 2))


def each(count, body):
    if count <= 8:
        for number in range(count):
            body(number)
    else:

        def step(number, carry):
            body(number)
            return carry

        lax.fori_loop(0, count, step, 0)


def kernel(
    n_sec, n_row, f_hbm, g_hbm, cnt_hbm, pts_hbm, solved_hbm,
    pts, solved, cnt, first, second, grams, packed, ring, mats, halo, part, gathered, sec_total, row_total,
    load_sem, store_sem, pts_send, pts_recv, gram_send, gram_recv,
    halo_send, halo_recv, sum_send, sum_recv,
):
    sec = lax.axis_index("sec")
    row = lax.axis_index("row")
    total = n_sec * n_row
    flat = sec * n_row + row
    one_stage = total <= 64
    has_next_row = row < n_row - 1
    has_prev_row = row > 0
    up = lax.rem(sec + 1, n_sec)
    down = lax.rem(sec + n_sec - 1, n_sec)
    higher = lax.rem(row + 1, n_row)
    lower = lax.rem(row + n_row - 1, n_row)
    up_sec = {"sec": up, "row": row}
    down_sec = {"sec": down, "row": row}
    up_row = {"sec": sec, "row": higher}
    down_row = {"sec": sec, "row": lower}

    def remote(src, dst, send, recv, where):
        return pltpu.make_async_remote_copy(
            src_ref=src, dst_ref=dst, send_sem=send, recv_sem=recv, device_id=where, device_id_type=MESH
        )

    def any_device(d):
        there = lax.rem(flat + d + 1, total)
        return {"sec": there // n_row, "row": lax.rem(there, n_row)}

    barrier = pltpu.get_barrier_semaphore()

    def greet(where):
        pl.semaphore_signal(barrier, inc=1, device_id=where, device_id_type=MESH)

    if one_stage:
        each(total - 1, lambda d: greet(any_device(d)))
        greeted = total - 1
    else:
        each(n_sec - 1, lambda d: greet({"sec": lax.rem(sec + d + 1, n_sec), "row": row}))
        each(n_row - 1, lambda d: greet({"sec": sec, "row": lax.rem(row + d + 1, n_row)}))
        for a in (up, down):
            for b in (higher, lower):
                greet({"sec": a, "row": b})
        greeted = n_sec + n_row + 2

    loads = []

    def load(src, dst):
        loads.append(pltpu.make_async_copy(src, dst, load_sem.at[len(loads)]))

    load(cnt_hbm, cnt.at[0])
    for kind in range(4):
        load(f_hbm.at[kind], first.at[kind])
    load(g_hbm.at[0], second.at[0, pl.ds(0, 256)])
    load(g_hbm.at[1, pl.ds(64, 64)], second.at[1, pl.ds(0, 64)])
    load(g_hbm.at[1, pl.ds(192, 64)], second.at[1, pl.ds(128, 64)])
    load(g_hbm.at[2, pl.ds(128, 128)], second.at[2, pl.ds(0, 128)])
    load(g_hbm.at[3], second.at[4, pl.ds(0, 256)])
    load(g_hbm.at[2, pl.ds(0, 128)], second.at[5, pl.ds(0, 128)])
    load(g_hbm.at[1, pl.ds(0, 64)], second.at[5, pl.ds(128, 64)])
    load(g_hbm.at[1, pl.ds(128, 64)], second.at[5, pl.ds(192, 64)])
    pl.semaphore_wait(barrier, greeted)

    sends = []

    def plan(src, dst, where):
        sends.append(remote(src, dst, pts_send.at[len(sends)], pts_recv.at[len(sends)], where))

    plan(cnt_hbm, cnt.at[1], up_sec)
    plan(g_hbm.at[2, pl.ds(0, 128)], second.at[2, pl.ds(128, 128)], down_sec)
    plan(f_hbm.at[2, pl.ds(128, 128)], first.at[5, pl.ds(0, 128)], up_sec)
    plan(g_hbm.at[3], second.at[3, pl.ds(0, 256)], down_sec)
    plan(f_hbm.at[3], first.at[4], up_sec)
    plan(g_hbm.at[1, pl.ds(0, 64)], second.at[1, pl.ds(64, 64)], down_row)
    plan(g_hbm.at[1, pl.ds(128, 64)], second.at[1, pl.ds(192, 64)], down_row)
    plan(cnt_hbm, cnt.at[2], up_row)
    plan(f_hbm.at[1, pl.ds(64, 64)], first.at[5, pl.ds(128, 64)], up_row)
    plan(f_hbm.at[1, pl.ds(192, 64)], first.at[5, pl.ds(192, 64)], up_row)
    for number in range(5):
        sends[number].start()

    @pl.when(has_prev_row)
    def _():
        sends[5].start()
        sends[6].start()

    @pl.when(has_next_row)
    def _():
        sends[7].start()
        sends[8].start()
        sends[9].start()

    for copy in loads:
        copy.start()

    @pl.when(jnp.logical_not(has_next_row))
    def _():
        ring[2] = jnp.zeros(ring.shape[1:], f32)
        for turn in range(2):
            for place in (5, 6, 7):
                halo[turn, place] = jnp.zeros((8, 128), f32)

    @pl.when(jnp.logical_not(has_prev_row))
    def _():
        ring[3] = jnp.zeros(ring.shape[1:], f32)
        for turn in range(2):
            for place in (8, 9, 10):
                halo[turn, place] = jnp.zeros((8, 128), f32)

    lane = lax.broadcasted_iota(jnp.int32, (1, 128), 1)
    col_of = lane % 32
    row_of = (lane // 32) % 2
    sec_of = lane // 64
    valid = (
        col_of < 31,
        row * 2 + row_of < n_row * 2 - 1,
        sec * 2 + sec_of < n_sec * 2 - 1,
        sec * 2 + sec_of < n_sec * 2 - 2,
        sec + 0 * lane > 0,
        jnp.where(lane < 64, sec, row) > 0,
    )

    def count_row(block, places):
        pieces = [cnt[who, kind, a, pl.ds(b, 1), :] for who, kind, a, b in places]
        return jnp.where(valid[block], jnp.concatenate(pieces, axis=1), 0)

    live = {}
    loads[0].wait()
    for kind in range(4):
        live[kind] = count_row(kind, [(0, kind, number // 2, number % 2) for number in range(4)])
    point = lax.broadcasted_iota(jnp.int32, (128, 128), 0)

    def turned(ref, block, start):
        values = ref[block, pl.ds(start, 128, stride=2), :].T
        return jnp.where(point < live[block], values, 0.0)

    for kind in range(4):
        loads[1 + kind].wait()
        pts[kind, 0] = turned(first, kind, 0)
        pts[kind, 1] = turned(first, kind, 1)

    stores = []
    for block in (0, 1, 2, 5, 3, 4):
        if block == 0:
            loads[5].wait()
        elif block == 1:
            loads[6].wait()
            loads[7].wait()

            @pl.when(has_next_row)
            def _():
                sends[5].wait_recv()
                sends[6].wait_recv()
        elif block == 2:
            loads[8].wait()
            sends[1].wait_recv()
        elif block == 3:
            sends[3].wait_recv()
        elif block == 4:
            loads[9].wait()
            sends[4].wait_recv()
        else:
            loads[10].wait()
            loads[11].wait()
            loads[12].wait()
            sends[0].wait_recv()
            sends[2].wait_recv()

            @pl.when(has_prev_row)
            def _():
                sends[7].wait_recv()
                sends[8].wait_recv()
                sends[9].wait_recv()

            live[4] = count_row(4, [(1, 3, number // 2, number % 2) for number in range(4)])
            live[5] = count_row(5, [(1, 2, 1, 0), (1, 2, 1, 1), (2, 1, 0, 1), (2, 1, 1, 1)])
        if block >= 4:
            pts[block, 0] = turned(first, block, 0)
            pts[block, 1] = turned(first, block, 1)
        shift = 2 if block == 0 else 0
        pts[block, 2] = turned(second, block, shift)
        pts[block, 3] = turned(second, block, shift + 1)
        if block < 4:
            stores.append(pltpu.make_async_copy(pts.at[block], pts_hbm.at[block], store_sem.at[block]))
            stores[-1].start()
        wanted = 15 if block < 4 else 12
        sums = [None] * wanted
        for step in range(16):
            u1, v1, u2, v2 = [pts[block, number, pl.ds(step * 8, 8), :] for number in range(4)]
            terms = [
                u1, v1, u2, v2, u1 * u2, u1 * v2, v1 * u2, v1 * v2, u2 * u2, u2 * v2, v2 * v2,
            ]
            if block < 4:
                terms += [u1 * u1, u1 * v1, v1 * v1]
            for number, term in enumerate(terms):
                sums[number + 1] = term if step == 0 else sums[number + 1] + term
        place = grams.at[0, block] if block < 4 else grams.at[1, 3 if block == 4 else 2]
        place[pl.ds(0, 1), :] = live[block].astype(f32)
        for number in range(1, wanted):
            place[pl.ds(number, 1), :] = jnp.sum(sums[number], axis=0, keepdims=True)
        place[pl.ds(wanted, 16 - wanted), :] = jnp.zeros((16 - wanted, 128), f32)

    sub = lax.broadcasted_iota(jnp.int32, (8, 128), 0)
    kind_of = sub // 2
    is_y = (sub % 2) == 1
    lanes = lax.broadcasted_iota(jnp.int32, (8, 128), 1)
    second_row = (lanes // 32) % 2 == 1
    second_sec = lanes // 64 == 1

    def by_kind(values):
        return jnp.where(
            kind_of == 0, values[0], jnp.where(kind_of == 1, values[1], jnp.where(kind_of == 2, values[2], values[3]))
        )

    def over_kinds(values):
        values = values + pltpu.roll(values, 4, 0)
        return values + pltpu.roll(values, 2, 0)

    wide = lax.broadcasted_iota(jnp.int32, (16, 128), 1)
    crossing = grams[1, 2]
    grams[1, 0] = pltpu.roll(grams[0, 0], 1, 1)
    grams[1, 1] = jnp.where(
        (wide // 32) % 2 == 1,
        pltpu.roll(grams[0, 1], 32, 1),
        jnp.where(wide // 64 == 0, pltpu.roll(crossing, 64, 1), pltpu.roll(crossing, 96, 1)),
    )
    grams[1, 2] = jnp.where(wide // 64 == 0, crossing, pltpu.roll(grams[0, 2], 64, 1))

    ways = (down_sec, up_sec, down_row, up_row)
    sent_to = (None, None, has_prev_row, has_next_row)
    got_from = (None, None, has_next_row, has_prev_row)

    def where_wanted(wanted, body):
        if wanted is None:
            body()
        else:
            pl.when(wanted)(body)

    def send_grams(diag):
        for kind in range(4):
            packed[kind] = grams[0, kind, pl.ds(1, 8), :]
            packed[7, pl.ds(kind, 1), :] = grams[0, kind, pl.ds(0, 1), :]
        for kind in range(1, 4):
            packed[3 + kind] = grams[1, kind, pl.ds(1, 8), :]
            packed[7, pl.ds(3 + kind, 1), :] = grams[1, kind, pl.ds(0, 1), :]
        packed[7, pl.ds(7, 1), :] = jnp.zeros((1, 128), f32)
        for number, (a, c) in enumerate(UPPER):
            packed[8, pl.ds(number, 1), :] = diag[a][c][0:1, :]
        packed[8, pl.ds(6, 2), :] = jnp.zeros((2, 128), f32)
        for copy, wanted in zip(gram_copies, sent_to):
            where_wanted(wanted, copy.start)

    gram_copies = [
        remote(packed, ring.at[number], gram_send.at[number], gram_recv.at[number], ways[number])
        for number in range(4)
    ]

    def spread(load_row, side, number):
        return by_kind([load_row(side, kind, number) for kind in range(4)])

    def sides(load_row):
        own = [spread(load_row, 0, number) for number in range(9)]
        other = [spread(load_row, 1, number) for number in range(9)]
        cross = [[own[CROSS[a][c]] for c in range(3)] for a in range(3)]
        back = [[other[CROSS[c][a]] for c in range(3)] for a in range(3)]
        return cross, back

    def symmetric(values):
        full = [[None] * 3 for _ in range(3)]
        for (a, c), value in zip(UPPER, values):
            full[a][c] = value
            full[c][a] = value
        return full

    def received(number):
        rolled = pltpu.roll(ring[number, 0], 1, 1)
        rolled_count = pltpu.roll(ring[number, 7], 1, 1)

        def load_row(side, kind, which):
            if side == 1 and kind == 0:
                return rolled_count[0:1, :] if which == 0 else rolled[which - 1 : which, :]
            slot = kind + 3 * side
            if which == 0:
                return ring[number, 7, pl.ds(slot, 1), :]
            return ring[number, slot, pl.ds(which - 1, 1), :]

        cross, back = sides(load_row)
        diag = symmetric(
            [jnp.broadcast_to(ring[number, 8, pl.ds(which, 1), :], (8, 128)) for which in range(6)]
        )
        return diag, cross, back

    def keep(place, blocks):
        for which in range(3):
            for a in range(3):
                for c in range(3):
                    mats[place, which * 9 + a * 3 + c] = blocks[which][a][c]

    def own_row(side, kind, number):
        return grams[side, kind, pl.ds(number, 1), :]

    diag = symmetric(
        [
            over_kinds(spread(own_row, 0, FIRST[a][c]) + spread(own_row, 1, SECOND[a][c]))
            for a, c in UPPER
        ]
    )

    regular = [list(line) for line in diag]
    for a in range(3):
        regular[a][a] = diag[a][a] + f32(REG[a]) * f32(REG[a])
    send_grams(regular)
    cross, back = sides(own_row)

    along = (jnp.where(is_y, 0.0, -1.0), jnp.where(is_y, -1.0, 0.0))
    start = []
    for a in range(3):
        there = (cross[a][0] + back[a][0]) * along[0] + (cross[a][1] + back[a][1]) * along[1]
        start.append(diag[a][0] * along[0] + diag[a][1] * along[1] - over_kinds(there))
    up_two = lax.rem(sec + 2, n_sec)
    down_two = lax.rem(sec + n_sec - 2, n_sec)
    groups = (
        (None, None, 1, (down_sec, up_sec, {"sec": down_two, "row": row}, {"sec": up_two, "row": row})),
        (has_prev_row, has_next_row, 5, (down_row, {"sec": down, "row": lower}, {"sec": up, "row": lower})),
        (has_next_row, has_prev_row, 8, (up_row, {"sec": down, "row": higher}, {"sec": up, "row": higher})),
    )

    def halo_group(turn, number):
        _, _, base, targets = groups[number]
        region = halo.at[turn, pl.ds(base, len(targets))]
        return remote(region, region, halo_send.at[turn, number], halo_recv.at[turn, number], targets[0])

    def send_halo(turn, values):
        halo[turn, 0] = jnp.where(kind_of == 0, values[0], jnp.where(kind_of == 1, values[1], values[2]))
        for number, (wanted, _, base, targets) in enumerate(groups):

            def start_all():
                for place, where in enumerate(targets):
                    remote(
                        halo.at[turn, 0], halo.at[turn, base + place],
                        halo_send.at[turn, number], halo_recv.at[turn, number], where,
                    ).start()

            where_wanted(wanted, start_all)

    def wait_halo(turn):
        for number in range(3):
            where_wanted(groups[number][1], halo_group(turn, number).wait_recv)

    def wait_halo_sent(turn):
        for number in range(3):
            where_wanted(groups[number][0], halo_group(turn, number).wait_send)

    def ahead(values, of_sec, of_row):
        return by_kind(
            [
                pltpu.roll(values, 127, 1),
                jnp.where(second_row, pltpu.roll(of_row, 32, 1), pltpu.roll(values, 96, 1)),
                pltpu.roll(jnp.where(second_sec, values, of_sec), 64, 1),
                of_sec,
            ]
        )

    def behind(values, of_sec, of_row):
        return by_kind(
            [
                pltpu.roll(values, 1, 1),
                jnp.where(second_row, pltpu.roll(values, 32, 1), pltpu.roll(of_row, 96, 1)),
                pltpu.roll(jnp.where(second_sec, of_sec, values), 64, 1),
                of_sec,
            ]
        )

    def normal(place, values, of_next_sec, of_prev_sec, of_next_row, of_prev_row):
        front = [ahead(values[c], of_next_sec[c], of_next_row[c]) for c in range(3)]
        rear = [behind(values[c], of_prev_sec[c], of_prev_row[c]) for c in range(3)]
        result = []
        for a in range(3):
            here = mats[place, 3 * a] * values[0]
            there = mats[place, 9 + 3 * a] * front[0] + mats[place, 18 + 3 * a] * rear[0]
            for c in (1, 2):
                here = here + mats[place, 3 * a + c] * values[c]
                there = there + mats[place, 9 + 3 * a + c] * front[c] + mats[place, 18 + 3 * a + c] * rear[c]
            result.append(here - over_kinds(there))
        return result

    def unpacked(turn, place):
        return [
            jnp.where(is_y, halo[turn, place, pl.ds(2 * c + 1, 1), :], halo[turn, place, pl.ds(2 * c, 1), :])
            for c in range(3)
        ]

    def normal_around(turn, here):
        w = [here] + [unpacked(turn, place) for place in range(1, 11)]
        none = [jnp.zeros((8, 128), f32)] * 3
        return [
            normal(0, w[0], w[1], w[2], w[5], w[8]),
            normal(1, w[1], w[3], w[0], w[6], w[9]),
            normal(2, w[2], w[0], w[4], w[7], w[10]),
            normal(3, w[5], w[6], w[7], none, w[0]),
            normal(4, w[8], w[9], w[10], w[0], none),
        ]

    def dot_row(left, right):
        return jnp.sum(
            left[0] * right[0] + left[1] * right[1] + left[2] * right[2], axis=0, keepdims=True
        )

    def sum_copy(turn, d):
        return remote(
            part.at[turn, pl.ds(0, 1)], gathered.at[turn, pl.ds(d, 1)],
            sum_send.at[turn, 0], sum_recv.at[turn, 0], any_device(d),
        )

    def sum_all(turn):
        region = gathered.at[turn, pl.ds(0, total - 1)]
        return remote(region, region, sum_send.at[turn, 0], sum_recv.at[turn, 0], any_device(0))

    def row_copy(turn, d):
        return remote(
            part.at[turn, pl.ds(0, 1)], row_total.at[turn, pl.ds(d, 1)],
            sum_send.at[turn, d], sum_recv.at[turn, d], {"sec": sec, "row": lax.rem(row + d + 1, n_row)},
        )

    def sec_copy(turn, d):
        return remote(
            part.at[turn, pl.ds(1, 1)], sec_total.at[turn, pl.ds(d, 1)],
            sum_send.at[turn, n_row + d], sum_recv.at[turn, n_row + d],
            {"sec": lax.rem(sec + d + 1, n_sec), "row": row},
        )

    def sum_open(turn, pairs):
        line = jnp.zeros((1, 128), f32)
        for number, (left, right) in enumerate(pairs):
            line = jnp.where(lane == number, jnp.sum(dot_row(left, right), axis=1, keepdims=True), line)
        part[turn, 0] = line
        if one_stage:
            gathered[turn, total - 1] = line
            each(total - 1, lambda d: sum_copy(turn, d).start())
        else:
            row_total[turn, n_row - 1] = line
            each(n_row - 1, lambda d: row_copy(turn, d).start())

    def sum_close(turn):
        if one_stage:
            sum_all(turn).wait_recv()
            line = jnp.sum(gathered[turn], axis=0)
        else:
            each(n_row - 1, lambda d: row_copy(turn, d).wait_recv())
            middle = jnp.sum(row_total[turn], axis=0)
            part[turn, 1] = middle
            sec_total[turn, n_sec - 1] = middle
            each(n_sec - 1, lambda d: sec_copy(turn, d).start())
            each(n_sec - 1, lambda d: sec_copy(turn, d).wait_recv())
            line = jnp.sum(sec_total[turn], axis=0)
        return [
            jnp.broadcast_to(jnp.sum(jnp.where(lane == number, line, 0.0), axis=1, keepdims=True), (1, 128))
            for number in range(8)
        ]

    def sum_sent(turn):
        if one_stage:
            sum_all(turn).wait_send()
        else:
            each(n_row - 1, lambda d: row_copy(turn, d).wait_send())
            each(n_sec - 1, lambda d: sec_copy(turn, d).wait_send())

    def mix(factors, vectors):
        result = []
        for c in range(3):
            value = factors[0] * vectors[0][c]
            for factor, vector in zip(factors[1:], vectors[1:]):
                value = value + factor * vector[c]
            result.append(value)
        return result

    send_halo(0, start)
    keep(0, (regular, cross, back))
    for number in range(4):
        where_wanted(got_from[number], gram_copies[number].wait_recv)
        keep(number + 1, received(number))
    wait_halo(0)
    w0 = start
    first_ring = normal_around(0, w0)
    w1 = first_ring[0]
    w2 = normal(0, *first_ring)
    send_halo(1, w2)
    sum_open(0, ((w0, w0), (w0, w1), (w1, w1), (w1, w2), (w2, w2)))
    wait_halo(1)
    third_ring = normal_around(1, w2)
    w3 = third_ring[0]
    w4 = normal(0, *third_ring)
    m0, m1, m2, m3, m4 = sum_close(0)[:5]

    alpha0 = m0 / m1
    gamma1 = m0 - 2.0 * alpha0 * m1 + alpha0 * alpha0 * m2
    s1w1 = m1 - alpha0 * m2
    beta0 = -s1w1 / m1
    curv1 = (m1 - 2.0 * alpha0 * m2 + alpha0 * alpha0 * m3) + 2.0 * beta0 * s1w1 + beta0 * beta0 * m1
    alpha1 = gamma1 / curv1
    lead = 1.0 + beta0
    s_one = -(alpha0 + alpha1 * lead)
    s_two = alpha0 * alpha1
    s2q1 = lead * (m1 + s_one * m2 + s_two * m3) - alpha0 * (m2 + s_one * m3 + s_two * m4)
    beta1 = -s2q1 / curv1
    p_zero = 1.0 + beta1 * lead
    p_one = s_one - beta1 * alpha0
    p_two = s_two

    one = jnp.ones((1, 128), f32)
    v = mix((one, s_one, s_two), (w0, w1, w2))
    t = mix((one, s_one, s_two), (w1, w2, w3))
    p = mix((p_zero, p_one, p_two), (w0, w1, w2))
    q = mix((p_zero, p_one, p_two), (w1, w2, w3))
    z = mix((p_zero, p_one, p_two), (w2, w3, w4))
    sum_open(1, ((v, p), (p, q), (v, q), (q, q), (v, v), (v, t), (q, t), (q, z)))
    for number in range(5):
        sends[number].wait_send()

    @pl.when(has_prev_row)
    def _():
        sends[5].wait_send()
        sends[6].wait_send()

    @pl.when(has_next_row)
    def _():
        sends[7].wait_send()
        sends[8].wait_send()
        sends[9].wait_send()

    for copy, wanted in zip(gram_copies, sent_to):
        where_wanted(wanted, copy.wait_send)
    wait_halo_sent(0)
    wait_halo_sent(1)
    sum_sent(0)
    for copy in stores:
        copy.wait()
    vp, pq, vq, qq, vv, vt, qt, qz = sum_close(1)
    alpha2 = vp / pq
    left = vq - alpha2 * qq
    beta2 = -left / pq
    gamma3 = vv - 2.0 * alpha2 * vq + alpha2 * alpha2 * qq
    curv3 = (
        (vt - alpha2 * qt + beta2 * vq) - alpha2 * (qt - alpha2 * qz + beta2 * qq) + beta2 * (left + beta2 * pq)
    )
    alpha3 = gamma3 / curv3
    both = alpha2 + alpha3 * beta2
    factors = (
        alpha0 + alpha1 * lead + both * p_zero + alpha3,
        both * p_one - alpha1 * alpha0 + alpha3 * (s_one - alpha2 * p_zero),
        both * p_two + alpha3 * (s_two - alpha2 * p_one),
        -alpha3 * alpha2 * p_two,
    )
    x = mix(factors, (w0, w1, w2, w3))
    beyond = []
    for place, slot in ((1, 1), (3, 5)):
        beyond.append(
            mix(
                factors,
                (
                    unpacked(0, slot), first_ring[place],
                    unpacked(1, slot), third_ring[place],
                ),
            )
        )
    x_sec, x_row = beyond
    far = [ahead(x[c], x_sec[c], x_row[c]) for c in range(3)]

    for c in range(3):
        solved[c] = x[c]
        solved[3 + c] = far[c]
    for kind in range(4):
        solved[6, pl.ds(kind, 1), :] = live[kind].astype(f32)
    solved[6, pl.ds(4, 4), :] = jnp.zeros((4, 128), f32)
    last = pltpu.make_async_copy(solved, solved_hbm, store_sem.at[4])
    last.start()

    sum_sent(1)
    last.wait()


def finish(pts_hbm, solved_hbm, aff, res, pts, solved, out, small, store_sem, load_sem):
    loads = [pltpu.make_async_copy(solved_hbm, solved, load_sem.at[4])]
    for kind in range(4):
        loads.append(pltpu.make_async_copy(pts_hbm.at[kind], pts.at[kind], load_sem.at[kind]))
    for copy in loads:
        copy.start()
    loads[0].wait()
    point = lax.broadcasted_iota(jnp.int32, (128, 128), 0).astype(f32)
    for part_no in range(2):
        for c in range(3):
            for number in range(4):
                small[3 * part_no + c, number // 2, pl.ds(number % 2, 1), :] = solved[
                    c, pl.ds(part_no, 1), pl.ds(32 * number, 32)
                ]
    stores = [pltpu.make_async_copy(small, aff, store_sem.at[4])]
    stores[0].start()
    for kind in range(4):
        loads[1 + kind].wait()
        u1, v1, u2, v2 = [pts[kind, number] for number in range(4)]
        inside = point < solved[6, pl.ds(kind, 1), :]
        for part_no in range(2):
            a0, a1, a2 = [solved[c, pl.ds(part_no, 1), :] for c in range(3)]
            b0, b1, b2 = [solved[3 + c, pl.ds(2 * kind + part_no, 1), :] for c in range(3)]
            base = u2 - u1 if part_no == 0 else v2 - v1
            value = base - (a0 * u1 + a1 * v1) + (b0 * u2 + b1 * v2) + jnp.where(inside, b2 - a2, 0.0)
            out[kind, pl.ds(part_no, 128, stride=2), :] = value.T
        stores.append(pltpu.make_async_copy(out.at[kind], res.at[kind], store_sem.at[kind]))
        stores[-1].start()
    for copy in stores:
        copy.wait()


def per_device(n_sec, n_row, first_pts, second_pts, counts):
    f = first_pts.reshape(4, 256, 128)
    g = second_pts.reshape(4, 256, 128)
    hbm = pl.BlockSpec(memory_space=pl.ANY)
    sems = pltpu.SemaphoreType.DMA
    sums = n_sec * n_row if n_sec * n_row <= 64 else n_sec + n_row
    pts, solved = pl.pallas_call(
        functools.partial(kernel, n_sec, n_row),
        out_shape=(
            jax.ShapeDtypeStruct((4, 4, 128, 128), f32),
            jax.ShapeDtypeStruct((7, 8, 128), f32),
        ),
        in_specs=[hbm, hbm, hbm],
        out_specs=(hbm, hbm),
        scratch_shapes=[
            pltpu.VMEM((6, 4, 128, 128), f32),
            pltpu.VMEM((7, 8, 128), f32),
            pltpu.VMEM((3,) + counts.shape, jnp.int32),
            pltpu.VMEM((6, 256, 128), f32),
            pltpu.VMEM((6, 264, 128), f32),
            pltpu.VMEM((2, 4, 16, 128), f32),
            pltpu.VMEM((9, 8, 128), f32),
            pltpu.VMEM((4, 9, 8, 128), f32),
            pltpu.VMEM((5, 27, 8, 128), f32),
            pltpu.VMEM((2, 11, 8, 128), f32),
            pltpu.VMEM((2, 2, 1, 128), f32),
            pltpu.VMEM((2, sums, 1, 128), f32),
            pltpu.VMEM((2, n_sec, 1, 128), f32),
            pltpu.VMEM((2, n_row, 1, 128), f32),
            sems((13,)), sems((5,)), sems((10,)), sems((10,)), sems((4,)), sems((4,)),
            sems((2, 3)), sems((2, 3)), sems((2, sums)), sems((2, sums)),
        ],
        compiler_params=pltpu.CompilerParams(
            collective_id=0, has_side_effects=True, vmem_limit_bytes=60 * 1024 * 1024
        ),
    )(f, g, counts)
    aff, res = pl.pallas_call(
        finish,
        out_shape=(
            jax.ShapeDtypeStruct((6,) + counts.shape[1:], f32),
            jax.ShapeDtypeStruct((4, 256, 128), f32),
        ),
        in_specs=[hbm, hbm],
        out_specs=(hbm, hbm),
        scratch_shapes=[
            pltpu.VMEM((4, 4, 128, 128), f32),
            pltpu.VMEM((7, 8, 128), f32),
            pltpu.VMEM((4, 256, 128), f32),
            pltpu.VMEM((6,) + counts.shape[1:], f32),
            sems((5,)),
            sems((5,)),
        ],
        compiler_params=pltpu.CompilerParams(vmem_limit_bytes=60 * 1024 * 1024),
    )(pts, solved)
    return aff, res.reshape(first_pts.shape)


def solution(mesh):
    in_specs = (
        P(None, "sec", "row", None, None, None),
        P(None, "sec", "row", None, None, None),
        P(None, "sec", "row", None),
    )
    out_specs = (P(None, "sec", "row", None), P(None, "sec", "row", None, None, None))
    return jax.shard_map(
        functools.partial(per_device, mesh.shape["sec"], mesh.shape["row"]),
        mesh=mesh, in_specs=in_specs, out_specs=out_specs, check_vma=False,
    )
```

```python
import functools

import jax
import jax.numpy as jnp
from jax import lax
from jax.experimental import pallas as pl
from jax.experimental.pallas import tpu as pltpu
from jax.sharding import PartitionSpec as P

MESH = pl.DeviceIdType.MESH
f32 = jnp.float32

CROSS = ((5, 6, 1), (7, 8, 2), (3, 4, 0))
SECOND = ((9, 10, 3), (10, 11, 4), (3, 4, 0))
FIRST = ((12, 13, 1), (13, 14, 2), (1, 2, 0))
REG = (0.7, 0.7, 0.3)


UPPER = ((0, 0), (0, 1), (0, 2), (1, 1), (1, 2), (2, 2))


def each(count, body):
    if count <= 8:
        for number in range(count):
            body(number)
    else:

        def step(number, carry):
            body(number)
            return carry

        lax.fori_loop(0, count, step, 0)


def kernel(
    n_sec, n_row, f_hbm, g_hbm, cnt_hbm, pts_hbm, solved_hbm,
    pts, solved, cnt, first, second, grams, packed, ring, mats, halo, part, gathered, sec_total, row_total,
    load_sem, store_sem, pts_send, pts_recv, gram_send, gram_recv,
    halo_send, halo_recv, sum_send, sum_recv,
):
    sec = lax.axis_index("sec")
    row = lax.axis_index("row")
    total = n_sec * n_row
    flat = sec * n_row + row
    one_stage = total <= 8
    has_next_row = row < n_row - 1
    has_prev_row = row > 0
    up = lax.rem(sec + 1, n_sec)
    down = lax.rem(sec + n_sec - 1, n_sec)
    higher = lax.rem(row + 1, n_row)
    lower = lax.rem(row + n_row - 1, n_row)
    up_sec = {"sec": up, "row": row}
    down_sec = {"sec": down, "row": row}
    up_row = {"sec": sec, "row": higher}
    down_row = {"sec": sec, "row": lower}

    def remote(src, dst, send, recv, where):
        return pltpu.make_async_remote_copy(
            src_ref=src, dst_ref=dst, send_sem=send, recv_sem=recv, device_id=where, device_id_type=MESH
        )

    def any_device(d):
        there = lax.rem(flat + d + 1, total)
        return {"sec": there // n_row, "row": lax.rem(there, n_row)}

    barrier = pltpu.get_barrier_semaphore()

    def greet(where):
        pl.semaphore_signal(barrier, inc=1, device_id=where, device_id_type=MESH)

    if one_stage:
        each(total - 1, lambda d: greet(any_device(d)))
        greeted = total - 1
    else:
        each(n_sec - 1, lambda d: greet({"sec": lax.rem(sec + d + 1, n_sec), "row": row}))
        each(n_row - 1, lambda d: greet({"sec": sec, "row": lax.rem(row + d + 1, n_row)}))
        for a in (up, down):
            for b in (higher, lower):
                greet({"sec": a, "row": b})
        greeted = n_sec + n_row + 2

    loads = []

    def load(src, dst):
        loads.append(pltpu.make_async_copy(src, dst, load_sem.at[len(loads)]))

    load(cnt_hbm, cnt.at[0])
    for kind in range(4):
        load(f_hbm.at[kind], first.at[kind])
    load(g_hbm.at[0], second.at[0, pl.ds(0, 256)])
    load(g_hbm.at[1, pl.ds(64, 64)], second.at[1, pl.ds(0, 64)])
    load(g_hbm.at[1, pl.ds(192, 64)], second.at[1, pl.ds(128, 64)])
    load(g_hbm.at[2, pl.ds(128, 128)], second.at[2, pl.ds(0, 128)])
    load(g_hbm.at[3], second.at[4, pl.ds(0, 256)])
    load(g_hbm.at[2, pl.ds(0, 128)], second.at[5, pl.ds(0, 128)])
    load(g_hbm.at[1, pl.ds(0, 64)], second.at[5, pl.ds(128, 64)])
    load(g_hbm.at[1, pl.ds(128, 64)], second.at[5, pl.ds(192, 64)])
    pl.semaphore_wait(barrier, greeted)

    sends = []

    def plan(src, dst, where):
        sends.append(remote(src, dst, pts_send.at[len(sends)], pts_recv.at[len(sends)], where))

    plan(cnt_hbm, cnt.at[1], up_sec)
    plan(g_hbm.at[2, pl.ds(0, 128)], second.at[2, pl.ds(128, 128)], down_sec)
    plan(f_hbm.at[2, pl.ds(128, 128)], first.at[5, pl.ds(0, 128)], up_sec)
    plan(g_hbm.at[3], second.at[3, pl.ds(0, 256)], down_sec)
    plan(f_hbm.at[3], first.at[4], up_sec)
    plan(g_hbm.at[1, pl.ds(0, 64)], second.at[1, pl.ds(64, 64)], down_row)
    plan(g_hbm.at[1, pl.ds(128, 64)], second.at[1, pl.ds(192, 64)], down_row)
    plan(cnt_hbm, cnt.at[2], up_row)
    plan(f_hbm.at[1, pl.ds(64, 64)], first.at[5, pl.ds(128, 64)], up_row)
    plan(f_hbm.at[1, pl.ds(192, 64)], first.at[5, pl.ds(192, 64)], up_row)
    for number in range(5):
        sends[number].start()

    @pl.when(has_prev_row)
    def _():
        sends[5].start()
        sends[6].start()

    @pl.when(has_next_row)
    def _():
        sends[7].start()
        sends[8].start()
        sends[9].start()

    for copy in loads:
        copy.start()

    @pl.when(jnp.logical_not(has_next_row))
    def _():
        ring[2] = jnp.zeros(ring.shape[1:], f32)
        for turn in range(2):
            for place in (5, 6, 7):
                halo[turn, place] = jnp.zeros((8, 128), f32)

    @pl.when(jnp.logical_not(has_prev_row))
    def _():
        ring[3] = jnp.zeros(ring.shape[1:], f32)
        for turn in range(2):
            for place in (8, 9, 10):
                halo[turn, place] = jnp.zeros((8, 128), f32)

    lane = lax.broadcasted_iota(jnp.int32, (1, 128), 1)
    col_of = lane % 32
    row_of = (lane // 32) % 2
    sec_of = lane // 64
    valid = (
        col_of < 31,
        row * 2 + row_of < n_row * 2 - 1,
        sec * 2 + sec_of < n_sec * 2 - 1,
        sec * 2 + sec_of < n_sec * 2 - 2,
        sec + 0 * lane > 0,
        jnp.where(lane < 64, sec, row) > 0,
    )

    def count_row(block, places):
        pieces = [cnt[who, kind, a, pl.ds(b, 1), :] for who, kind, a, b in places]
        return jnp.where(valid[block], jnp.concatenate(pieces, axis=1), 0)

    live = {}
    loads[0].wait()
    for kind in range(4):
        live[kind] = count_row(kind, [(0, kind, number // 2, number % 2) for number in range(4)])
    point = lax.broadcasted_iota(jnp.int32, (128, 128), 0)

    def turned(ref, block, start):
        values = ref[block, pl.ds(start, 128, stride=2), :].T
        return jnp.where(point < live[block], values, 0.0)

    for kind in range(4):
        loads[1 + kind].wait()
        pts[kind, 0] = turned(first, kind, 0)
        pts[kind, 1] = turned(first, kind, 1)

    stores = []
    for block in (0, 1, 2, 5, 3, 4):
        if block == 0:
            loads[5].wait()
        elif block == 1:
            loads[6].wait()
            loads[7].wait()

            @pl.when(has_next_row)
            def _():
                sends[5].wait_recv()
                sends[6].wait_recv()
        elif block == 2:
            loads[8].wait()
            sends[1].wait_recv()
        elif block == 3:
            sends[3].wait_recv()
        elif block == 4:
            loads[9].wait()
            sends[4].wait_recv()
        else:
            loads[10].wait()
            loads[11].wait()
            loads[12].wait()
            sends[0].wait_recv()
            sends[2].wait_recv()

            @pl.when(has_prev_row)
            def _():
                sends[7].wait_recv()
                sends[8].wait_recv()
                sends[9].wait_recv()

            live[4] = count_row(4, [(1, 3, number // 2, number % 2) for number in range(4)])
            live[5] = count_row(5, [(1, 2, 1, 0), (1, 2, 1, 1), (2, 1, 0, 1), (2, 1, 1, 1)])
        if block >= 4:
            pts[block, 0] = turned(first, block, 0)
            pts[block, 1] = turned(first, block, 1)
        shift = 2 if block == 0 else 0
        pts[block, 2] = turned(second, block, shift)
        pts[block, 3] = turned(second, block, shift + 1)
        if block < 4:
            stores.append(pltpu.make_async_copy(pts.at[block], pts_hbm.at[block], store_sem.at[block]))
            stores[-1].start()
        wanted = 15 if block < 4 else 12
        sums = [None] * wanted
        for step in range(16):
            u1, v1, u2, v2 = [pts[block, number, pl.ds(step * 8, 8), :] for number in range(4)]
            terms = [
                u1, v1, u2, v2, u1 * u2, u1 * v2, v1 * u2, v1 * v2, u2 * u2, u2 * v2, v2 * v2,
            ]
            if block < 4:
                terms += [u1 * u1, u1 * v1, v1 * v1]
            for number, term in enumerate(terms):
                sums[number + 1] = term if step == 0 else sums[number + 1] + term
        place = grams.at[0, block] if block < 4 else grams.at[1, 3 if block == 4 else 2]
        place[pl.ds(0, 1), :] = live[block].astype(f32)
        for number in range(1, wanted):
            place[pl.ds(number, 1), :] = jnp.sum(sums[number], axis=0, keepdims=True)
        place[pl.ds(wanted, 16 - wanted), :] = jnp.zeros((16 - wanted, 128), f32)

    sub = lax.broadcasted_iota(jnp.int32, (8, 128), 0)
    kind_of = sub // 2
    is_y = (sub % 2) == 1
    lanes = lax.broadcasted_iota(jnp.int32, (8, 128), 1)
    second_row = (lanes // 32) % 2 == 1
    second_sec = lanes // 64 == 1

    def by_kind(values):
        return jnp.where(
            kind_of == 0, values[0], jnp.where(kind_of == 1, values[1], jnp.where(kind_of == 2, values[2], values[3]))
        )

    def over_kinds(values):
        values = values + pltpu.roll(values, 4, 0)
        return values + pltpu.roll(values, 2, 0)

    wide = lax.broadcasted_iota(jnp.int32, (16, 128), 1)
    crossing = grams[1, 2]
    grams[1, 0] = pltpu.roll(grams[0, 0], 1, 1)
    grams[1, 1] = jnp.where(
        (wide // 32) % 2 == 1,
        pltpu.roll(grams[0, 1], 32, 1),
        jnp.where(wide // 64 == 0, pltpu.roll(crossing, 64, 1), pltpu.roll(crossing, 96, 1)),
    )
    grams[1, 2] = jnp.where(wide // 64 == 0, crossing, pltpu.roll(grams[0, 2], 64, 1))

    ways = (down_sec, up_sec, down_row, up_row)
    sent_to = (None, None, has_prev_row, has_next_row)
    got_from = (None, None, has_next_row, has_prev_row)

    def where_wanted(wanted, body):
        if wanted is None:
            body()
        else:
            pl.when(wanted)(body)

    def send_grams(diag):
        for kind in range(4):
            packed[kind] = grams[0, kind, pl.ds(1, 8), :]
            packed[7, pl.ds(kind, 1), :] = grams[0, kind, pl.ds(0, 1), :]
        for kind in range(1, 4):
            packed[3 + kind] = grams[1, kind, pl.ds(1, 8), :]
            packed[7, pl.ds(3 + kind, 1), :] = grams[1, kind, pl.ds(0, 1), :]
        packed[7, pl.ds(7, 1), :] = jnp.zeros((1, 128), f32)
        for number, (a, c) in enumerate(UPPER):
            packed[8, pl.ds(number, 1), :] = diag[a][c][0:1, :]
        packed[8, pl.ds(6, 2), :] = jnp.zeros((2, 128), f32)
        for copy, wanted in zip(gram_copies, sent_to):
            where_wanted(wanted, copy.start)

    gram_copies = [
        remote(packed, ring.at[number], gram_send.at[number], gram_recv.at[number], ways[number])
        for number in range(4)
    ]

    def spread(load_row, side, number):
        return by_kind([load_row(side, kind, number) for kind in range(4)])

    def sides(load_row):
        own = [spread(load_row, 0, number) for number in range(9)]
        other = [spread(load_row, 1, number) for number in range(9)]
        cross = [[own[CROSS[a][c]] for c in range(3)] for a in range(3)]
        back = [[other[CROSS[c][a]] for c in range(3)] for a in range(3)]
        return cross, back

    def symmetric(values):
        full = [[None] * 3 for _ in range(3)]
        for (a, c), value in zip(UPPER, values):
            full[a][c] = value
            full[c][a] = value
        return full

    def received(number):
        rolled = pltpu.roll(ring[number, 0], 1, 1)
        rolled_count = pltpu.roll(ring[number, 7], 1, 1)

        def load_row(side, kind, which):
            if side == 1 and kind == 0:
                return rolled_count[0:1, :] if which == 0 else rolled[which - 1 : which, :]
            slot = kind + 3 * side
            if which == 0:
                return ring[number, 7, pl.ds(slot, 1), :]
            return ring[number, slot, pl.ds(which - 1, 1), :]

        cross, back = sides(load_row)
        diag = symmetric(
            [jnp.broadcast_to(ring[number, 8, pl.ds(which, 1), :], (8, 128)) for which in range(6)]
        )
        return diag, cross, back

    def keep(place, blocks):
        for which in range(3):
            for a in range(3):
                for c in range(3):
                    mats[place, which * 9 + a * 3 + c] = blocks[which][a][c]

    def own_row(side, kind, number):
        return grams[side, kind, pl.ds(number, 1), :]

    diag = symmetric(
        [
            over_kinds(spread(own_row, 0, FIRST[a][c]) + spread(own_row, 1, SECOND[a][c]))
            for a, c in UPPER
        ]
    )

    regular = [list(line) for line in diag]
    for a in range(3):
        regular[a][a] = diag[a][a] + f32(REG[a]) * f32(REG[a])
    send_grams(regular)
    cross, back = sides(own_row)

    along = (jnp.where(is_y, 0.0, -1.0), jnp.where(is_y, -1.0, 0.0))
    start = []
    for a in range(3):
        there = (cross[a][0] + back[a][0]) * along[0] + (cross[a][1] + back[a][1]) * along[1]
        start.append(diag[a][0] * along[0] + diag[a][1] * along[1] - over_kinds(there))
    up_two = lax.rem(sec + 2, n_sec)
    down_two = lax.rem(sec + n_sec - 2, n_sec)
    groups = (
        (None, None, 1, (down_sec, up_sec, {"sec": down_two, "row": row}, {"sec": up_two, "row": row})),
        (has_prev_row, has_next_row, 5, (down_row, {"sec": down, "row": lower}, {"sec": up, "row": lower})),
        (has_next_row, has_prev_row, 8, (up_row, {"sec": down, "row": higher}, {"sec": up, "row": higher})),
    )

    def halo_group(turn, number):
        _, _, base, targets = groups[number]
        region = halo.at[turn, pl.ds(base, len(targets))]
        return remote(region, region, halo_send.at[turn, number], halo_recv.at[turn, number], targets[0])

    def send_halo(turn, values):
        halo[turn, 0] = jnp.where(kind_of == 0, values[0], jnp.where(kind_of == 1, values[1], values[2]))
        for number, (wanted, _, base, targets) in enumerate(groups):

            def start_all():
                for place, where in enumerate(targets):
                    remote(
                        halo.at[turn, 0], halo.at[turn, base + place],
                        halo_send.at[turn, number], halo_recv.at[turn, number], where,
                    ).start()

            where_wanted(wanted, start_all)

    def wait_halo(turn):
        for number in range(3):
            where_wanted(groups[number][1], halo_group(turn, number).wait_recv)

    def wait_halo_sent(turn):
        for number in range(3):
            where_wanted(groups[number][0], halo_group(turn, number).wait_send)

    def ahead(values, of_sec, of_row):
        return by_kind(
            [
                pltpu.roll(values, 127, 1),
                jnp.where(second_row, pltpu.roll(of_row, 32, 1), pltpu.roll(values, 96, 1)),
                pltpu.roll(jnp.where(second_sec, values, of_sec), 64, 1),
                of_sec,
            ]
        )

    def behind(values, of_sec, of_row):
        return by_kind(
            [
                pltpu.roll(values, 1, 1),
                jnp.where(second_row, pltpu.roll(values, 32, 1), pltpu.roll(of_row, 96, 1)),
                pltpu.roll(jnp.where(second_sec, of_sec, values), 64, 1),
                of_sec,
            ]
        )

    def normal(place, values, of_next_sec, of_prev_sec, of_next_row, of_prev_row):
        front = [ahead(values[c], of_next_sec[c], of_next_row[c]) for c in range(3)]
        rear = [behind(values[c], of_prev_sec[c], of_prev_row[c]) for c in range(3)]
        result = []
        for a in range(3):
            here = mats[place, 3 * a] * values[0]
            there = mats[place, 9 + 3 * a] * front[0] + mats[place, 18 + 3 * a] * rear[0]
            for c in (1, 2):
                here = here + mats[place, 3 * a + c] * values[c]
                there = there + mats[place, 9 + 3 * a + c] * front[c] + mats[place, 18 + 3 * a + c] * rear[c]
            result.append(here - over_kinds(there))
        return result

    def unpacked(turn, place):
        return [
            jnp.where(is_y, halo[turn, place, pl.ds(2 * c + 1, 1), :], halo[turn, place, pl.ds(2 * c, 1), :])
            for c in range(3)
        ]

    def normal_around(turn, here):
        w = [here] + [unpacked(turn, place) for place in range(1, 11)]
        none = [jnp.zeros((8, 128), f32)] * 3
        return [
            normal(0, w[0], w[1], w[2], w[5], w[8]),
            normal(1, w[1], w[3], w[0], w[6], w[9]),
            normal(2, w[2], w[0], w[4], w[7], w[10]),
            normal(3, w[5], w[6], w[7], none, w[0]),
            normal(4, w[8], w[9], w[10], w[0], none),
        ]

    def dot_row(left, right):
        return jnp.sum(
            left[0] * right[0] + left[1] * right[1] + left[2] * right[2], axis=0, keepdims=True
        )

    def sum_copy(turn, d):
        return remote(
            part.at[turn, pl.ds(0, 1)], gathered.at[turn, pl.ds(d, 1)],
            sum_send.at[turn, 0], sum_recv.at[turn, 0], any_device(d),
        )

    def sum_all(turn):
        region = gathered.at[turn, pl.ds(0, total - 1)]
        return remote(region, region, sum_send.at[turn, 0], sum_recv.at[turn, 0], any_device(0))

    def row_copy(turn, d):
        return remote(
            part.at[turn, pl.ds(0, 1)], row_total.at[turn, pl.ds(d, 1)],
            sum_send.at[turn, d], sum_recv.at[turn, d], {"sec": sec, "row": lax.rem(row + d + 1, n_row)},
        )

    def sec_copy(turn, d):
        return remote(
            part.at[turn, pl.ds(1, 1)], sec_total.at[turn, pl.ds(d, 1)],
            sum_send.at[turn, n_row + d], sum_recv.at[turn, n_row + d],
            {"sec": lax.rem(sec + d + 1, n_sec), "row": row},
        )

    def sum_open(turn, pairs):
        line = jnp.zeros((1, 128), f32)
        for number, (left, right) in enumerate(pairs):
            line = jnp.where(lane == number, jnp.sum(dot_row(left, right), axis=1, keepdims=True), line)
        part[turn, 0] = line
        if one_stage:
            gathered[turn, total - 1] = line
            each(total - 1, lambda d: sum_copy(turn, d).start())
        else:
            row_total[turn, n_row - 1] = line
            each(n_row - 1, lambda d: row_copy(turn, d).start())

    def sum_close(turn):
        if one_stage:
            sum_all(turn).wait_recv()
            line = jnp.sum(gathered[turn], axis=0)
        else:
            each(n_row - 1, lambda d: row_copy(turn, d).wait_recv())
            middle = jnp.sum(row_total[turn], axis=0)
            part[turn, 1] = middle
            sec_total[turn, n_sec - 1] = middle
            each(n_sec - 1, lambda d: sec_copy(turn, d).start())
            each(n_sec - 1, lambda d: sec_copy(turn, d).wait_recv())
            line = jnp.sum(sec_total[turn], axis=0)
        return [
            jnp.broadcast_to(jnp.sum(jnp.where(lane == number, line, 0.0), axis=1, keepdims=True), (1, 128))
            for number in range(8)
        ]

    def sum_sent(turn):
        if one_stage:
            sum_all(turn).wait_send()
        else:
            each(n_row - 1, lambda d: row_copy(turn, d).wait_send())
            each(n_sec - 1, lambda d: sec_copy(turn, d).wait_send())

    def mix(factors, vectors):
        result = []
        for c in range(3):
            value = factors[0] * vectors[0][c]
            for factor, vector in zip(factors[1:], vectors[1:]):
                value = value + factor * vector[c]
            result.append(value)
        return result

    send_halo(0, start)
    keep(0, (regular, cross, back))
    for number in range(4):
        where_wanted(got_from[number], gram_copies[number].wait_recv)
        keep(number + 1, received(number))
    wait_halo(0)
    w0 = start
    first_ring = normal_around(0, w0)
    w1 = first_ring[0]
    w2 = normal(0, *first_ring)
    send_halo(1, w2)
    sum_open(0, ((w0, w0), (w0, w1), (w1, w1), (w1, w2), (w2, w2)))
    wait_halo(1)
    third_ring = normal_around(1, w2)
    w3 = third_ring[0]
    w4 = normal(0, *third_ring)
    m0, m1, m2, m3, m4 = sum_close(0)[:5]

    alpha0 = m0 / m1
    gamma1 = m0 - 2.0 * alpha0 * m1 + alpha0 * alpha0 * m2
    s1w1 = m1 - alpha0 * m2
    beta0 = -s1w1 / m1
    curv1 = (m1 - 2.0 * alpha0 * m2 + alpha0 * alpha0 * m3) + 2.0 * beta0 * s1w1 + beta0 * beta0 * m1
    alpha1 = gamma1 / curv1
    lead = 1.0 + beta0
    s_one = -(alpha0 + alpha1 * lead)
    s_two = alpha0 * alpha1
    s2q1 = lead * (m1 + s_one * m2 + s_two * m3) - alpha0 * (m2 + s_one * m3 + s_two * m4)
    beta1 = -s2q1 / curv1
    p_zero = 1.0 + beta1 * lead
    p_one = s_one - beta1 * alpha0
    p_two = s_two

    one = jnp.ones((1, 128), f32)
    v = mix((one, s_one, s_two), (w0, w1, w2))
    t = mix((one, s_one, s_two), (w1, w2, w3))
    p = mix((p_zero, p_one, p_two), (w0, w1, w2))
    q = mix((p_zero, p_one, p_two), (w1, w2, w3))
    z = mix((p_zero, p_one, p_two), (w2, w3, w4))
    sum_open(1, ((v, p), (p, q), (v, q), (q, q), (v, v), (v, t), (q, t), (q, z)))
    for number in range(5):
        sends[number].wait_send()

    @pl.when(has_prev_row)
    def _():
        sends[5].wait_send()
        sends[6].wait_send()

    @pl.when(has_next_row)
    def _():
        sends[7].wait_send()
        sends[8].wait_send()
        sends[9].wait_send()

    for copy, wanted in zip(gram_copies, sent_to):
        where_wanted(wanted, copy.wait_send)
    wait_halo_sent(0)
    wait_halo_sent(1)
    sum_sent(0)
    for copy in stores:
        copy.wait()
    vp, pq, vq, qq, vv, vt, qt, qz = sum_close(1)
    alpha2 = vp / pq
    left = vq - alpha2 * qq
    beta2 = -left / pq
    gamma3 = vv - 2.0 * alpha2 * vq + alpha2 * alpha2 * qq
    curv3 = (
        (vt - alpha2 * qt + beta2 * vq) - alpha2 * (qt - alpha2 * qz + beta2 * qq) + beta2 * (left + beta2 * pq)
    )
    alpha3 = gamma3 / curv3
    both = alpha2 + alpha3 * beta2
    factors = (
        alpha0 + alpha1 * lead + both * p_zero + alpha3,
        both * p_one - alpha1 * alpha0 + alpha3 * (s_one - alpha2 * p_zero),
        both * p_two + alpha3 * (s_two - alpha2 * p_one),
        -alpha3 * alpha2 * p_two,
    )
    x = mix(factors, (w0, w1, w2, w3))
    beyond = []
    for place, slot in ((1, 1), (3, 5)):
        beyond.append(
            mix(
                factors,
                (
                    unpacked(0, slot), first_ring[place],
                    unpacked(1, slot), third_ring[place],
                ),
            )
        )
    x_sec, x_row = beyond
    far = [ahead(x[c], x_sec[c], x_row[c]) for c in range(3)]

    for c in range(3):
        solved[c] = x[c]
        solved[3 + c] = far[c]
    for kind in range(4):
        solved[6, pl.ds(kind, 1), :] = live[kind].astype(f32)
    solved[6, pl.ds(4, 4), :] = jnp.zeros((4, 128), f32)
    last = pltpu.make_async_copy(solved, solved_hbm, store_sem.at[4])
    last.start()

    sum_sent(1)
    last.wait()


def finish(pts_hbm, solved_hbm, aff, res, pts, solved, out, small, store_sem, load_sem):
    loads = [pltpu.make_async_copy(solved_hbm, solved, load_sem.at[4])]
    for kind in range(4):
        loads.append(pltpu.make_async_copy(pts_hbm.at[kind], pts.at[kind], load_sem.at[kind]))
    for copy in loads:
        copy.start()
    loads[0].wait()
    point = lax.broadcasted_iota(jnp.int32, (128, 128), 0).astype(f32)
    for part_no in range(2):
        for c in range(3):
            for number in range(4):
                small[3 * part_no + c, number // 2, pl.ds(number % 2, 1), :] = solved[
                    c, pl.ds(part_no, 1), pl.ds(32 * number, 32)
                ]
    stores = [pltpu.make_async_copy(small, aff, store_sem.at[4])]
    stores[0].start()
    for kind in range(4):
        loads[1 + kind].wait()
        u1, v1, u2, v2 = [pts[kind, number] for number in range(4)]
        inside = point < solved[6, pl.ds(kind, 1), :]
        for part_no in range(2):
            a0, a1, a2 = [solved[c, pl.ds(part_no, 1), :] for c in range(3)]
            b0, b1, b2 = [solved[3 + c, pl.ds(2 * kind + part_no, 1), :] for c in range(3)]
            base = u2 - u1 if part_no == 0 else v2 - v1
            value = base - (a0 * u1 + a1 * v1) + (b0 * u2 + b1 * v2) + jnp.where(inside, b2 - a2, 0.0)
            out[kind, pl.ds(part_no, 128, stride=2), :] = value.T
        stores.append(pltpu.make_async_copy(out.at[kind], res.at[kind], store_sem.at[kind]))
        stores[-1].start()
    for copy in stores:
        copy.wait()


def per_device(n_sec, n_row, first_pts, second_pts, counts):
    f = first_pts.reshape(4, 256, 128)
    g = second_pts.reshape(4, 256, 128)
    hbm = pl.BlockSpec(memory_space=pl.ANY)
    sems = pltpu.SemaphoreType.DMA
    sums = n_sec * n_row if n_sec * n_row <= 8 else n_sec + n_row
    pts, solved = pl.pallas_call(
        functools.partial(kernel, n_sec, n_row),
        out_shape=(
            jax.ShapeDtypeStruct((4, 4, 128, 128), f32),
            jax.ShapeDtypeStruct((7, 8, 128), f32),
        ),
        in_specs=[hbm, hbm, hbm],
        out_specs=(hbm, hbm),
        scratch_shapes=[
            pltpu.VMEM((6, 4, 128, 128), f32),
            pltpu.VMEM((7, 8, 128), f32),
            pltpu.VMEM((3,) + counts.shape, jnp.int32),
            pltpu.VMEM((6, 256, 128), f32),
            pltpu.VMEM((6, 264, 128), f32),
            pltpu.VMEM((2, 4, 16, 128), f32),
            pltpu.VMEM((9, 8, 128), f32),
            pltpu.VMEM((4, 9, 8, 128), f32),
            pltpu.VMEM((5, 27, 8, 128), f32),
            pltpu.VMEM((2, 11, 8, 128), f32),
            pltpu.VMEM((2, 2, 1, 128), f32),
            pltpu.VMEM((2, sums, 1, 128), f32),
            pltpu.VMEM((2, n_sec, 1, 128), f32),
            pltpu.VMEM((2, n_row, 1, 128), f32),
            sems((13,)), sems((5,)), sems((10,)), sems((10,)), sems((4,)), sems((4,)),
            sems((2, 3)), sems((2, 3)), sems((2, sums)), sems((2, sums)),
        ],
        compiler_params=pltpu.CompilerParams(
            collective_id=0, has_side_effects=True, vmem_limit_bytes=60 * 1024 * 1024
        ),
    )(f, g, counts)
    aff, res = pl.pallas_call(
        finish,
        out_shape=(
            jax.ShapeDtypeStruct((6,) + counts.shape[1:], f32),
            jax.ShapeDtypeStruct((4, 256, 128), f32),
        ),
        in_specs=[hbm, hbm],
        out_specs=(hbm, hbm),
        scratch_shapes=[
            pltpu.VMEM((4, 4, 128, 128), f32),
            pltpu.VMEM((7, 8, 128), f32),
            pltpu.VMEM((4, 256, 128), f32),
            pltpu.VMEM((6,) + counts.shape[1:], f32),
            sems((5,)),
            sems((5,)),
        ],
        compiler_params=pltpu.CompilerParams(vmem_limit_bytes=60 * 1024 * 1024),
    )(pts, solved)
    return aff, res.reshape(first_pts.shape)


def solution(mesh):
    in_specs = (
        P(None, "sec", "row", None, None, None),
        P(None, "sec", "row", None, None, None),
        P(None, "sec", "row", None),
    )
    out_specs = (P(None, "sec", "row", None), P(None, "sec", "row", None, None, None))
    return jax.shard_map(
        functools.partial(per_device, mesh.shape["sec"], mesh.shape["row"]),
        mesh=mesh, in_specs=in_specs, out_specs=out_specs, check_vma=False,
    )
```

```python
import functools

import jax
import jax.numpy as jnp
from jax import lax
from jax.experimental import pallas as pl
from jax.experimental.pallas import tpu as pltpu
from jax.sharding import PartitionSpec as P

MESH = pl.DeviceIdType.MESH
f32 = jnp.float32

CROSS = ((5, 6, 1), (7, 8, 2), (3, 4, 0))
SECOND = ((9, 10, 3), (10, 11, 4), (3, 4, 0))
FIRST = ((12, 13, 1), (13, 14, 2), (1, 2, 0))
REG = (0.7, 0.7, 0.3)


UPPER = ((0, 0), (0, 1), (0, 2), (1, 1), (1, 2), (2, 2))


def each(count, body):
    if count <= 8:
        for number in range(count):
            body(number)
    else:

        def step(number, carry):
            body(number)
            return carry

        lax.fori_loop(0, count, step, 0)


def kernel(
    n_sec, n_row, f_hbm, g_hbm, cnt_hbm, pts_hbm, solved_hbm,
    pts, solved, cnt, first, second, grams, packed, ring, mats, halo, part, gathered, sec_total, row_total,
    load_sem, store_sem, pts_send, pts_recv, gram_send, gram_recv,
    halo_send, halo_recv, sum_send, sum_recv,
):
    sec = lax.axis_index("sec")
    row = lax.axis_index("row")
    total = n_sec * n_row
    flat = sec * n_row + row
    one_stage = total <= 64
    has_next_row = row < n_row - 1
    has_prev_row = row > 0
    up = lax.rem(sec + 1, n_sec)
    down = lax.rem(sec + n_sec - 1, n_sec)
    higher = lax.rem(row + 1, n_row)
    lower = lax.rem(row + n_row - 1, n_row)
    up_sec = {"sec": up, "row": row}
    down_sec = {"sec": down, "row": row}
    up_row = {"sec": sec, "row": higher}
    down_row = {"sec": sec, "row": lower}

    def remote(src, dst, send, recv, where):
        return pltpu.make_async_remote_copy(
            src_ref=src, dst_ref=dst, send_sem=send, recv_sem=recv, device_id=where, device_id_type=MESH
        )

    def any_device(d):
        there = lax.rem(flat + d + 1, total)
        return {"sec": there // n_row, "row": lax.rem(there, n_row)}

    barrier = pltpu.get_barrier_semaphore()

    def greet(where):
        pl.semaphore_signal(barrier, inc=1, device_id=where, device_id_type=MESH)

    if one_stage:
        each(total - 1, lambda d: greet(any_device(d)))
        greeted = total - 1
    else:
        each(n_sec - 1, lambda d: greet({"sec": lax.rem(sec + d + 1, n_sec), "row": row}))
        each(n_row - 1, lambda d: greet({"sec": sec, "row": lax.rem(row + d + 1, n_row)}))
        for a in (up, down):
            for b in (higher, lower):
                greet({"sec": a, "row": b})
        greeted = n_sec + n_row + 2

    loads = []

    def load(src, dst):
        loads.append(pltpu.make_async_copy(src, dst, load_sem.at[len(loads)]))

    load(cnt_hbm, cnt.at[0])
    for kind in range(4):
        load(f_hbm.at[kind], first.at[kind])
    load(g_hbm.at[0], second.at[0, pl.ds(0, 256)])
    load(g_hbm.at[1, pl.ds(64, 64)], second.at[1, pl.ds(0, 64)])
    load(g_hbm.at[1, pl.ds(192, 64)], second.at[1, pl.ds(128, 64)])
    load(g_hbm.at[2, pl.ds(128, 128)], second.at[2, pl.ds(0, 128)])
    load(g_hbm.at[3], second.at[4, pl.ds(0, 256)])
    load(g_hbm.at[2, pl.ds(0, 128)], second.at[5, pl.ds(0, 128)])
    load(g_hbm.at[1, pl.ds(0, 64)], second.at[5, pl.ds(128, 64)])
    load(g_hbm.at[1, pl.ds(128, 64)], second.at[5, pl.ds(192, 64)])
    pl.semaphore_wait(barrier, greeted)

    sends = []

    def plan(src, dst, where):
        sends.append(remote(src, dst, pts_send.at[len(sends)], pts_recv.at[len(sends)], where))

    plan(cnt_hbm, cnt.at[1], up_sec)
    plan(g_hbm.at[2, pl.ds(0, 128)], second.at[2, pl.ds(128, 128)], down_sec)
    plan(f_hbm.at[2, pl.ds(128, 128)], first.at[5, pl.ds(0, 128)], up_sec)
    plan(g_hbm.at[3], second.at[3, pl.ds(0, 256)], down_sec)
    plan(f_hbm.at[3], first.at[4], up_sec)
    plan(g_hbm.at[1, pl.ds(0, 64)], second.at[1, pl.ds(64, 64)], down_row)
    plan(g_hbm.at[1, pl.ds(128, 64)], second.at[1, pl.ds(192, 64)], down_row)
    plan(cnt_hbm, cnt.at[2], up_row)
    plan(f_hbm.at[1, pl.ds(64, 64)], first.at[5, pl.ds(128, 64)], up_row)
    plan(f_hbm.at[1, pl.ds(192, 64)], first.at[5, pl.ds(192, 64)], up_row)
    for number in range(5):
        sends[number].start()

    @pl.when(has_prev_row)
    def _():
        sends[5].start()
        sends[6].start()

    @pl.when(has_next_row)
    def _():
        sends[7].start()
        sends[8].start()
        sends[9].start()

    for copy in loads:
        copy.start()

    @pl.when(jnp.logical_not(has_next_row))
    def _():
        ring[2] = jnp.zeros(ring.shape[1:], f32)
        for turn in range(2):
            for place in (5, 6, 7):
                halo[turn, place] = jnp.zeros((8, 128), f32)

    @pl.when(jnp.logical_not(has_prev_row))
    def _():
        ring[3] = jnp.zeros(ring.shape[1:], f32)
        for turn in range(2):
            for place in (8, 9, 10):
                halo[turn, place] = jnp.zeros((8, 128), f32)

    lane = lax.broadcasted_iota(jnp.int32, (1, 128), 1)
    col_of = lane % 32
    row_of = (lane // 32) % 2
    sec_of = lane // 64
    valid = (
        col_of < 31,
        row * 2 + row_of < n_row * 2 - 1,
        sec * 2 + sec_of < n_sec * 2 - 1,
        sec * 2 + sec_of < n_sec * 2 - 2,
        sec + 0 * lane > 0,
        jnp.where(lane < 64, sec, row) > 0,
    )

    def count_row(block, places):
        pieces = [cnt[who, kind, a, pl.ds(b, 1), :] for who, kind, a, b in places]
        return jnp.where(valid[block], jnp.concatenate(pieces, axis=1), 0)

    live = {}
    loads[0].wait()
    for kind in range(4):
        live[kind] = count_row(kind, [(0, kind, number // 2, number % 2) for number in range(4)])
    point = lax.broadcasted_iota(jnp.int32, (128, 128), 0)

    def turned(ref, block, start):
        values = ref[block, pl.ds(start, 128, stride=2), :].T
        return jnp.where(point < live[block], values, 0.0)

    for kind in range(4):
        loads[1 + kind].wait()
        pts[kind, 0] = turned(first, kind, 0)
        pts[kind, 1] = turned(first, kind, 1)

    stores = []
    for block in (0, 1, 2, 5, 3, 4):
        if block == 0:
            loads[5].wait()
        elif block == 1:
            loads[6].wait()
            loads[7].wait()

            @pl.when(has_next_row)
            def _():
                sends[5].wait_recv()
                sends[6].wait_recv()
        elif block == 2:
            loads[8].wait()
            sends[1].wait_recv()
        elif block == 3:
            sends[3].wait_recv()
        elif block == 4:
            loads[9].wait()
            sends[4].wait_recv()
        else:
            loads[10].wait()
            loads[11].wait()
            loads[12].wait()
            sends[0].wait_recv()
            sends[2].wait_recv()

            @pl.when(has_prev_row)
            def _():
                sends[7].wait_recv()
                sends[8].wait_recv()
                sends[9].wait_recv()

            live[4] = count_row(4, [(1, 3, number // 2, number % 2) for number in range(4)])
            live[5] = count_row(5, [(1, 2, 1, 0), (1, 2, 1, 1), (2, 1, 0, 1), (2, 1, 1, 1)])
        if block >= 4:
            pts[block, 0] = turned(first, block, 0)
            pts[block, 1] = turned(first, block, 1)
        shift = 2 if block == 0 else 0
        pts[block, 2] = turned(second, block, shift)
        pts[block, 3] = turned(second, block, shift + 1)
        if block < 4:
            stores.append(pltpu.make_async_copy(pts.at[block], pts_hbm.at[block], store_sem.at[block]))
            stores[-1].start()
        wanted = 15 if block < 4 else 12
        sums = [None] * wanted
        for step in range(16):
            u1, v1, u2, v2 = [pts[block, number, pl.ds(step * 8, 8), :] for number in range(4)]
            terms = [
                u1, v1, u2, v2, u1 * u2, u1 * v2, v1 * u2, v1 * v2, u2 * u2, u2 * v2, v2 * v2,
            ]
            if block < 4:
                terms += [u1 * u1, u1 * v1, v1 * v1]
            for number, term in enumerate(terms):
                sums[number + 1] = term if step == 0 else sums[number + 1] + term
        place = grams.at[0, block] if block < 4 else grams.at[1, 3 if block == 4 else 2]
        place[pl.ds(0, 1), :] = live[block].astype(f32)
        for number in range(1, wanted):
            place[pl.ds(number, 1), :] = jnp.sum(sums[number], axis=0, keepdims=True)
        place[pl.ds(wanted, 16 - wanted), :] = jnp.zeros((16 - wanted, 128), f32)

    sub = lax.broadcasted_iota(jnp.int32, (8, 128), 0)
    kind_of = sub // 2
    is_y = (sub % 2) == 1
    lanes = lax.broadcasted_iota(jnp.int32, (8, 128), 1)
    second_row = (lanes // 32) % 2 == 1
    second_sec = lanes // 64 == 1

    def by_kind(values):
        return jnp.where(
            kind_of == 0, values[0], jnp.where(kind_of == 1, values[1], jnp.where(kind_of == 2, values[2], values[3]))
        )

    def over_kinds(values):
        values = values + pltpu.roll(values, 4, 0)
        return values + pltpu.roll(values, 2, 0)

    wide = lax.broadcasted_iota(jnp.int32, (16, 128), 1)
    crossing = grams[1, 2]
    grams[1, 0] = pltpu.roll(grams[0, 0], 1, 1)
    grams[1, 1] = jnp.where(
        (wide // 32) % 2 == 1,
        pltpu.roll(grams[0, 1], 32, 1),
        jnp.where(wide // 64 == 0, pltpu.roll(crossing, 64, 1), pltpu.roll(crossing, 96, 1)),
    )
    grams[1, 2] = jnp.where(wide // 64 == 0, crossing, pltpu.roll(grams[0, 2], 64, 1))

    ways = (down_sec, up_sec, down_row, up_row)
    sent_to = (None, None, has_prev_row, has_next_row)
    got_from = (None, None, has_next_row, has_prev_row)

    def where_wanted(wanted, body):
        if wanted is None:
            body()
        else:
            pl.when(wanted)(body)

    def send_grams(diag):
        for kind in range(4):
            packed[kind] = grams[0, kind, pl.ds(1, 8), :]
            packed[7, pl.ds(kind, 1), :] = grams[0, kind, pl.ds(0, 1), :]
        for kind in range(1, 4):
            packed[3 + kind] = grams[1, kind, pl.ds(1, 8), :]
            packed[7, pl.ds(3 + kind, 1), :] = grams[1, kind, pl.ds(0, 1), :]
        packed[7, pl.ds(7, 1), :] = jnp.zeros((1, 128), f32)
        for number, (a, c) in enumerate(UPPER):
            packed[8, pl.ds(number, 1), :] = diag[a][c][0:1, :]
        packed[8, pl.ds(6, 2), :] = jnp.zeros((2, 128), f32)
        for copy, wanted in zip(gram_copies, sent_to):
            where_wanted(wanted, copy.start)

    gram_copies = [
        remote(packed, ring.at[number], gram_send.at[number], gram_recv.at[number], ways[number])
        for number in range(4)
    ]

    def spread(load_row, side, number):
        return by_kind([load_row(side, kind, number) for kind in range(4)])

    def sides(load_row):
        own = [spread(load_row, 0, number) for number in range(9)]
        other = [spread(load_row, 1, number) for number in range(9)]
        cross = [[own[CROSS[a][c]] for c in range(3)] for a in range(3)]
        back = [[other[CROSS[c][a]] for c in range(3)] for a in range(3)]
        return cross, back

    def symmetric(values):
        full = [[None] * 3 for _ in range(3)]
        for (a, c), value in zip(UPPER, values):
            full[a][c] = value
            full[c][a] = value
        return full

    def received(number):
        rolled = pltpu.roll(ring[number, 0], 1, 1)
        rolled_count = pltpu.roll(ring[number, 7], 1, 1)

        def load_row(side, kind, which):
            if side == 1 and kind == 0:
                return rolled_count[0:1, :] if which == 0 else rolled[which - 1 : which, :]
            slot = kind + 3 * side
            if which == 0:
                return ring[number, 7, pl.ds(slot, 1), :]
            return ring[number, slot, pl.ds(which - 1, 1), :]

        cross, back = sides(load_row)
        diag = symmetric(
            [jnp.broadcast_to(ring[number, 8, pl.ds(which, 1), :], (8, 128)) for which in range(6)]
        )
        return diag, cross, back

    def keep(place, blocks):
        for which in range(3):
            for a in range(3):
                for c in range(3):
                    mats[place, which * 9 + a * 3 + c] = blocks[which][a][c]

    def own_row(side, kind, number):
        return grams[side, kind, pl.ds(number, 1), :]

    diag = symmetric(
        [
            over_kinds(spread(own_row, 0, FIRST[a][c]) + spread(own_row, 1, SECOND[a][c]))
            for a, c in UPPER
        ]
    )

    regular = [list(line) for line in diag]
    for a in range(3):
        regular[a][a] = diag[a][a] + f32(REG[a]) * f32(REG[a])
    send_grams(regular)
    cross, back = sides(own_row)

    along = (jnp.where(is_y, 0.0, -1.0), jnp.where(is_y, -1.0, 0.0))
    start = []
    for a in range(3):
        there = (cross[a][0] + back[a][0]) * along[0] + (cross[a][1] + back[a][1]) * along[1]
        start.append(diag[a][0] * along[0] + diag[a][1] * along[1] - over_kinds(there))
    up_two = lax.rem(sec + 2, n_sec)
    down_two = lax.rem(sec + n_sec - 2, n_sec)
    groups = (
        (None, None, 1, (down_sec, up_sec, {"sec": down_two, "row": row}, {"sec": up_two, "row": row})),
        (has_prev_row, has_next_row, 5, (down_row, {"sec": down, "row": lower}, {"sec": up, "row": lower})),
        (has_next_row, has_prev_row, 8, (up_row, {"sec": down, "row": higher}, {"sec": up, "row": higher})),
    )

    def halo_group(turn, number):
        _, _, base, targets = groups[number]
        region = halo.at[turn, pl.ds(base, len(targets))]
        return remote(region, region, halo_send.at[turn, number], halo_recv.at[turn, number], targets[0])

    def send_halo(turn, values):
        halo[turn, 0] = jnp.where(kind_of == 0, values[0], jnp.where(kind_of == 1, values[1], values[2]))
        for number, (wanted, _, base, targets) in enumerate(groups):

            def start_all():
                for place, where in enumerate(targets):
                    remote(
                        halo.at[turn, 0], halo.at[turn, base + place],
                        halo_send.at[turn, number], halo_recv.at[turn, number], where,
                    ).start()

            where_wanted(wanted, start_all)

    def wait_halo(turn):
        for number in range(3):
            where_wanted(groups[number][1], halo_group(turn, number).wait_recv)

    def wait_halo_sent(turn):
        for number in range(3):
            where_wanted(groups[number][0], halo_group(turn, number).wait_send)

    def ahead(values, of_sec, of_row):
        return by_kind(
            [
                pltpu.roll(values, 127, 1),
                jnp.where(second_row, pltpu.roll(of_row, 32, 1), pltpu.roll(values, 96, 1)),
                pltpu.roll(jnp.where(second_sec, values, of_sec), 64, 1),
                of_sec,
            ]
        )

    def behind(values, of_sec, of_row):
        return by_kind(
            [
                pltpu.roll(values, 1, 1),
                jnp.where(second_row, pltpu.roll(values, 32, 1), pltpu.roll(of_row, 96, 1)),
                pltpu.roll(jnp.where(second_sec, of_sec, values), 64, 1),
                of_sec,
            ]
        )

    def normal(place, values, of_next_sec, of_prev_sec, of_next_row, of_prev_row):
        front = [ahead(values[c], of_next_sec[c], of_next_row[c]) for c in range(3)]
        rear = [behind(values[c], of_prev_sec[c], of_prev_row[c]) for c in range(3)]
        result = []
        for a in range(3):
            here = mats[place, 3 * a] * values[0]
            there = mats[place, 9 + 3 * a] * front[0] + mats[place, 18 + 3 * a] * rear[0]
            for c in (1, 2):
                here = here + mats[place, 3 * a + c] * values[c]
                there = there + mats[place, 9 + 3 * a + c] * front[c] + mats[place, 18 + 3 * a + c] * rear[c]
            result.append(here - over_kinds(there))
        return result

    def unpacked(turn, place):
        return [
            jnp.where(is_y, halo[turn, place, pl.ds(2 * c + 1, 1), :], halo[turn, place, pl.ds(2 * c, 1), :])
            for c in range(3)
        ]

    def normal_around(turn, here):
        w = [here] + [unpacked(turn, place) for place in range(1, 11)]
        none = [jnp.zeros((8, 128), f32)] * 3
        return [
            normal(0, w[0], w[1], w[2], w[5], w[8]),
            normal(1, w[1], w[3], w[0], w[6], w[9]),
            normal(2, w[2], w[0], w[4], w[7], w[10]),
            normal(3, w[5], w[6], w[7], none, w[0]),
            normal(4, w[8], w[9], w[10], w[0], none),
        ]

    def dot_row(left, right):
        return jnp.sum(
            left[0] * right[0] + left[1] * right[1] + left[2] * right[2], axis=0, keepdims=True
        )

    def sum_copy(turn, d):
        return remote(
            part.at[turn, pl.ds(0, 1)], gathered.at[turn, pl.ds(d, 1)],
            sum_send.at[turn, 0], sum_recv.at[turn, 0], any_device(d),
        )

    def sum_all(turn):
        region = gathered.at[turn, pl.ds(0, total - 1)]
        return remote(region, region, sum_send.at[turn, 0], sum_recv.at[turn, 0], any_device(0))

    def row_copy(turn, d):
        return remote(
            part.at[turn, pl.ds(0, 1)], row_total.at[turn, pl.ds(d, 1)],
            sum_send.at[turn, d], sum_recv.at[turn, d], {"sec": sec, "row": lax.rem(row + d + 1, n_row)},
        )

    def sec_copy(turn, d):
        return remote(
            part.at[turn, pl.ds(1, 1)], sec_total.at[turn, pl.ds(d, 1)],
            sum_send.at[turn, n_row + d], sum_recv.at[turn, n_row + d],
            {"sec": lax.rem(sec + d + 1, n_sec), "row": row},
        )

    def sum_open(turn, pairs):
        line = jnp.zeros((1, 128), f32)
        for number, (left, right) in enumerate(pairs):
            line = jnp.where(lane == number, jnp.sum(dot_row(left, right), axis=1, keepdims=True), line)
        part[turn, 0] = line
        if one_stage:
            gathered[turn, total - 1] = line
            each(total - 1, lambda d: sum_copy(turn, d).start())
        else:
            row_total[turn, n_row - 1] = line
            each(n_row - 1, lambda d: row_copy(turn, d).start())

    def sum_close(turn):
        if one_stage:
            sum_all(turn).wait_recv()
            line = jnp.sum(gathered[turn], axis=0)
        else:
            each(n_row - 1, lambda d: row_copy(turn, d).wait_recv())
            middle = jnp.sum(row_total[turn], axis=0)
            part[turn, 1] = middle
            sec_total[turn, n_sec - 1] = middle
            each(n_sec - 1, lambda d: sec_copy(turn, d).start())
            each(n_sec - 1, lambda d: sec_copy(turn, d).wait_recv())
            line = jnp.sum(sec_total[turn], axis=0)
        return [
            jnp.broadcast_to(jnp.sum(jnp.where(lane == number, line, 0.0), axis=1, keepdims=True), (1, 128))
            for number in range(8)
        ]

    def sum_sent(turn):
        if one_stage:
            sum_all(turn).wait_send()
        else:
            each(n_row - 1, lambda d: row_copy(turn, d).wait_send())
            each(n_sec - 1, lambda d: sec_copy(turn, d).wait_send())

    def mix(factors, vectors):
        result = []
        for c in range(3):
            value = factors[0] * vectors[0][c]
            for factor, vector in zip(factors[1:], vectors[1:]):
                value = value + factor * vector[c]
            result.append(value)
        return result

    send_halo(0, start)
    keep(0, (regular, cross, back))
    for number in range(4):
        where_wanted(got_from[number], gram_copies[number].wait_recv)
        keep(number + 1, received(number))
    wait_halo(0)
    w0 = start
    first_ring = normal_around(0, w0)
    w1 = first_ring[0]
    w2 = normal(0, *first_ring)
    send_halo(1, w2)
    sum_open(0, ((w0, w0), (w0, w1), (w1, w1), (w1, w2), (w2, w2)))
    wait_halo(1)
    third_ring = normal_around(1, w2)
    w3 = third_ring[0]
    w4 = normal(0, *third_ring)
    m0, m1, m2, m3, m4 = sum_close(0)[:5]

    alpha0 = m0 / m1
    gamma1 = m0 - 2.0 * alpha0 * m1 + alpha0 * alpha0 * m2
    s1w1 = m1 - alpha0 * m2
    beta0 = -s1w1 / m1
    curv1 = (m1 - 2.0 * alpha0 * m2 + alpha0 * alpha0 * m3) + 2.0 * beta0 * s1w1 + beta0 * beta0 * m1
    alpha1 = gamma1 / curv1
    lead = 1.0 + beta0
    s_one = -(alpha0 + alpha1 * lead)
    s_two = alpha0 * alpha1
    s2q1 = lead * (m1 + s_one * m2 + s_two * m3) - alpha0 * (m2 + s_one * m3 + s_two * m4)
    beta1 = -s2q1 / curv1
    p_zero = 1.0 + beta1 * lead
    p_one = s_one - beta1 * alpha0
    p_two = s_two

    one = jnp.ones((1, 128), f32)
    v = mix((one, s_one, s_two), (w0, w1, w2))
    t = mix((one, s_one, s_two), (w1, w2, w3))
    p = mix((p_zero, p_one, p_two), (w0, w1, w2))
    q = mix((p_zero, p_one, p_two), (w1, w2, w3))
    z = mix((p_zero, p_one, p_two), (w2, w3, w4))
    sum_open(1, ((v, p), (p, q), (v, q), (q, q), (v, v), (v, t), (q, t), (q, z)))
    for number in range(5):
        sends[number].wait_send()

    @pl.when(has_prev_row)
    def _():
        sends[5].wait_send()
        sends[6].wait_send()

    @pl.when(has_next_row)
    def _():
        sends[7].wait_send()
        sends[8].wait_send()
        sends[9].wait_send()

    for copy, wanted in zip(gram_copies, sent_to):
        where_wanted(wanted, copy.wait_send)
    wait_halo_sent(0)
    wait_halo_sent(1)
    sum_sent(0)
    for copy in stores:
        copy.wait()
    vp, pq, vq, qq, vv, vt, qt, qz = sum_close(1)
    alpha2 = vp / pq
    left = vq - alpha2 * qq
    beta2 = -left / pq
    gamma3 = vv - 2.0 * alpha2 * vq + alpha2 * alpha2 * qq
    curv3 = (
        (vt - alpha2 * qt + beta2 * vq) - alpha2 * (qt - alpha2 * qz + beta2 * qq) + beta2 * (left + beta2 * pq)
    )
    alpha3 = gamma3 / curv3
    both = alpha2 + alpha3 * beta2
    factors = (
        alpha0 + alpha1 * lead + both * p_zero + alpha3,
        both * p_one - alpha1 * alpha0 + alpha3 * (s_one - alpha2 * p_zero),
        both * p_two + alpha3 * (s_two - alpha2 * p_one),
        -alpha3 * alpha2 * p_two,
    )
    x = mix(factors, (w0, w1, w2, w3))
    beyond = []
    for place, slot in ((1, 1), (3, 5)):
        beyond.append(
            mix(
                factors,
                (
                    unpacked(0, slot), first_ring[place],
                    unpacked(1, slot), third_ring[place],
                ),
            )
        )
    x_sec, x_row = beyond
    far = [ahead(x[c], x_sec[c], x_row[c]) for c in range(3)]

    for c in range(3):
        solved[c] = x[c]
        solved[3 + c] = far[c]
    for kind in range(4):
        solved[6, pl.ds(kind, 1), :] = live[kind].astype(f32)
    solved[6, pl.ds(4, 4), :] = jnp.zeros((4, 128), f32)
    last = pltpu.make_async_copy(solved, solved_hbm, store_sem.at[4])
    last.start()

    sum_sent(1)
    last.wait()


def finish(pts_hbm, solved_hbm, aff, res, pts, solved, out, small, store_sem, load_sem):
    loads = [pltpu.make_async_copy(solved_hbm, solved, load_sem.at[4])]
    for kind in range(4):
        loads.append(pltpu.make_async_copy(pts_hbm.at[kind], pts.at[kind], load_sem.at[kind]))
    for copy in loads:
        copy.start()
    loads[0].wait()
    point = lax.broadcasted_iota(jnp.int32, (128, 128), 0).astype(f32)
    stores = []
    for kind in range(4):
        loads[1 + kind].wait()
        u1, v1, u2, v2 = [pts[kind, number] for number in range(4)]
        inside = point < solved[6, pl.ds(kind, 1), :]
        for part_no in range(2):
            a0, a1, a2 = [solved[c, pl.ds(part_no, 1), :] for c in range(3)]
            b0, b1, b2 = [solved[3 + c, pl.ds(2 * kind + part_no, 1), :] for c in range(3)]
            base = u2 - u1 if part_no == 0 else v2 - v1
            value = base - (a0 * u1 + a1 * v1) + (b0 * u2 + b1 * v2) + jnp.where(inside, b2 - a2, 0.0)
            out[kind, pl.ds(part_no, 128, stride=2), :] = value.T
        stores.append(pltpu.make_async_copy(out.at[kind], res.at[kind], store_sem.at[kind]))
        stores[-1].start()
    for part_no in range(2):
        for c in range(3):
            for number in range(4):
                small[3 * part_no + c, number // 2, pl.ds(number % 2, 1), :] = solved[
                    c, pl.ds(part_no, 1), pl.ds(32 * number, 32)
                ]
    stores.append(pltpu.make_async_copy(small, aff, store_sem.at[4]))
    stores[-1].start()
    for copy in stores:
        copy.wait()


def per_device(n_sec, n_row, first_pts, second_pts, counts):
    f = first_pts.reshape(4, 256, 128)
    g = second_pts.reshape(4, 256, 128)
    hbm = pl.BlockSpec(memory_space=pl.ANY)
    sems = pltpu.SemaphoreType.DMA
    sums = n_sec * n_row if n_sec * n_row <= 64 else n_sec + n_row
    pts, solved = pl.pallas_call(
        functools.partial(kernel, n_sec, n_row),
        out_shape=(
            jax.ShapeDtypeStruct((4, 4, 128, 128), f32),
            jax.ShapeDtypeStruct((7, 8, 128), f32),
        ),
        in_specs=[hbm, hbm, hbm],
        out_specs=(hbm, hbm),
        scratch_shapes=[
            pltpu.VMEM((6, 4, 128, 128), f32),
            pltpu.VMEM((7, 8, 128), f32),
            pltpu.VMEM((3,) + counts.shape, jnp.int32),
            pltpu.VMEM((6, 256, 128), f32),
            pltpu.VMEM((6, 264, 128), f32),
            pltpu.VMEM((2, 4, 16, 128), f32),
            pltpu.VMEM((9, 8, 128), f32),
            pltpu.VMEM((4, 9, 8, 128), f32),
            pltpu.VMEM((5, 27, 8, 128), f32),
            pltpu.VMEM((2, 11, 8, 128), f32),
            pltpu.VMEM((2, 2, 1, 128), f32),
            pltpu.VMEM((2, sums, 1, 128), f32),
            pltpu.VMEM((2, n_sec, 1, 128), f32),
            pltpu.VMEM((2, n_row, 1, 128), f32),
            sems((13,)), sems((5,)), sems((10,)), sems((10,)), sems((4,)), sems((4,)),
            sems((2, 3)), sems((2, 3)), sems((2, sums)), sems((2, sums)),
        ],
        compiler_params=pltpu.CompilerParams(
            collective_id=0, has_side_effects=True, vmem_limit_bytes=60 * 1024 * 1024
        ),
    )(f, g, counts)
    aff, res = pl.pallas_call(
        finish,
        out_shape=(
            jax.ShapeDtypeStruct((6,) + counts.shape[1:], f32),
            jax.ShapeDtypeStruct((4, 256, 128), f32),
        ),
        in_specs=[hbm, hbm],
        out_specs=(hbm, hbm),
        scratch_shapes=[
            pltpu.VMEM((4, 4, 128, 128), f32),
            pltpu.VMEM((7, 8, 128), f32),
            pltpu.VMEM((4, 256, 128), f32),
            pltpu.VMEM((6,) + counts.shape[1:], f32),
            sems((5,)),
            sems((5,)),
        ],
        compiler_params=pltpu.CompilerParams(vmem_limit_bytes=60 * 1024 * 1024),
    )(pts, solved)
    return aff, res.reshape(first_pts.shape)


def solution(mesh):
    in_specs = (
        P(None, "sec", "row", None, None, None),
        P(None, "sec", "row", None, None, None),
        P(None, "sec", "row", None),
    )
    out_specs = (P(None, "sec", "row", None), P(None, "sec", "row", None, None, None))
    return jax.shard_map(
        functools.partial(per_device, mesh.shape["sec"], mesh.shape["row"]),
        mesh=mesh, in_specs=in_specs, out_specs=out_specs, check_vma=False,
    )
```
